256 devices in a mesh: seq: 32 (over z, y), head: 8 (over x, core).
Axes of the slice: x: 4, y: 4, z: 8, core: 2. Of those that a mesh axis runs over, the one named last changes fastest.
Arguments:
- queries: bfloat16 [32768, 4096], P('seq', 'head'), may hold values from -16 to 16
- keys: bfloat16 [32768, 4096], P('seq', 'head'), may hold values from -16 to 16
- values: bfloat16 [32768, 4096], P('seq', 'head'), may hold values from -6 to 6
- out_weight: bfloat16 [4096, 4096], P('seq', 'head'), may hold values from -0.09375 to 0.09375
- out_grad: bfloat16 [32768, 4096], P('seq', 'head'), may hold values from -6 to 6
Outputs:
- query_grad: bfloat16 [32768, 4096], P('seq', 'head')
- key_grad: bfloat16 [32768, 4096], P('seq', 'head')
- values_gradient: bfloat16 [32768, 4096], P('seq', 'head')
- weight_grad: float32 [4096, 4096], P('seq', 'head')
The draws below stay inside these ranges and needn't reach their ends.
All inputs are finite; a program needn't handle non-finite values.
Results may differ from the reference program's by a relative error of at most 0.013.
The reference program's roundings to bfloat16 on the way count: a program that leaves them out, or rounds other values in their place, can miss the bound.
Values may be sent and summed in bfloat16 or wider, within the bound.
No kernel may reach another device: no remote copies, remote signals or barrier semaphores. Data moves between devices by JAX's collectives and lax.ppermute only.
A program may use at most 128 MiB of HBM per device.

```python
import jax
import jax.numpy as jnp
from jax import lax

HEAD_COUNT = 32
HEAD_SIZE = 128
M = 64
NEWTON = 6
D = 4096
DOCUMENT_TOKENS = 32768
SEG = 512


def segment_field(key):
    base = jax.random.normal(jax.random.fold_in(key, 1), (DOCUMENT_TOKENS, D), jnp.float32)
    centers = jax.random.normal(jax.random.fold_in(key, 2), (M, D), jnp.float32)
    field = 0.8 * base + jnp.repeat(centers, SEG, axis=0)
    return field


def draw_queries(key, part):
    key = jax.random.fold_in(key, 3)
    field = segment_field(key)
    return jnp.clip(field, -16.0, 16.0).astype(jnp.bfloat16)


def draw_keys(key, part):
    key = jax.random.fold_in(key, 7)
    field = segment_field(key)
    return jnp.clip(field, -16.0, 16.0).astype(jnp.bfloat16)


def levels(stream_key, shape, split, low, top_value):
    def one(position, shards_of):
        steps = jax.random.uniform(jax.random.fold_in(jax.random.fold_in(stream_key, 6), position), (shards_of,), jnp.float32, low / len(split), top_value / len(split))
        return jnp.repeat(jnp.exp(steps), shape[position] // shards_of).reshape((-1,) + (1,) * (len(shape) - position - 1))

    factor_of = one(*split[0])
    for cut in split[1:]:
        factor_of = factor_of * one(*cut)
    return factor_of


def centred(rng, extent, deviation, limit, pieces=(), held_as=jnp.bfloat16):
    array = jax.random.normal(rng, extent, jnp.float32) * deviation
    if len(pieces) > 0:
        array = levels(rng, extent, pieces, -0.22, 0.18) * array
    return jnp.clip(array, min=-limit, max=limit).astype(held_as)


def setup_inputs(seed: int = 0) -> dict:
    seeds = jax.random.split(jax.random.key(seed), 6)
    return {
        "queries": draw_queries(jax.random.fold_in(seeds[5], 71), 0),
        "keys": draw_keys(jax.random.fold_in(seeds[5], 71), 0),
        "values": centred(seeds[2], (DOCUMENT_TOKENS, D), 1.0, 6.0, ((0, 32), (1, 8))),
        "out_weight": centred(seeds[3], (D, D), D ** -0.5, 0.09375, ((0, 32), (1, 8))),
        "out_grad": centred(seeds[4], (DOCUMENT_TOKENS, D), 1.0, 6.0, ((0, 32), (1, 8))),
    }


HIGH_PRECISION = lax.Precision.HIGHEST

def matmul(a, b):
    return jnp.einsum('hij,hjk->hik', a, b, precision=HIGH_PRECISION)

def newton(a, denom):
    size = a.shape[-1]
    eye = jnp.eye(size, dtype=a.dtype)[None]
    z = jnp.swapaxes(a, -1, -2) / denom
    for step in range(NEWTON):
        az = matmul(a, z)
        z = 0.25 * matmul(z, 13.0 * eye - matmul(az, 15.0 * eye - matmul(az, 7.0 * eye - az)))
    return z

def reference(queries, keys, values, out_weight, out_grad):
    single_float_type = jnp.float32
    brain_float_type = jnp.bfloat16
    score_scale = HEAD_SIZE ** (-0.5)
    queries_three_dim = queries.reshape(DOCUMENT_TOKENS, HEAD_COUNT, HEAD_SIZE)
    keys_three_dim = keys.reshape(DOCUMENT_TOKENS, HEAD_COUNT, HEAD_SIZE)
    values_three_dim = values.reshape(DOCUMENT_TOKENS, HEAD_COUNT, HEAD_SIZE)
    query_tile = lax.optimization_barrier(jnp.sum(queries_three_dim.reshape(M, SEG, HEAD_COUNT, HEAD_SIZE), axis=1, dtype=single_float_type)) / SEG
    key_tile = lax.optimization_barrier(jnp.sum(keys_three_dim.reshape(M, SEG, HEAD_COUNT, HEAD_SIZE), axis=1, dtype=single_float_type)) / SEG
    query_tile_half = query_tile.astype(brain_float_type)
    key_tile_half = key_tile.astype(brain_float_type)
    panel_matrix = jax.nn.softmax(jnp.einsum('glb,elb->lge', key_tile_half, queries_three_dim, preferred_element_type=single_float_type) * score_scale, axis=1)
    panel_half = panel_matrix.astype(brain_float_type)
    kernel_matrix = jax.nn.softmax(jnp.einsum('gwt,cwt->wgc', query_tile, key_tile, precision=HIGH_PRECISION) * score_scale, axis=-1)
    score_matrix = jnp.einsum('glb,elb->lge', query_tile_half, keys_three_dim, preferred_element_type=single_float_type) * score_scale
    top = lax.optimization_barrier(jnp.max(score_matrix, axis=-1, keepdims=True))
    exponentials = jnp.exp(score_matrix - top)
    grand_total = lax.optimization_barrier(jnp.sum(exponentials, axis=-1, keepdims=True))
    weights_single = exponentials / grand_total
    landmark_values = jnp.einsum('cuz,zcg->cug', exponentials, values_three_dim.astype(single_float_type), precision=HIGH_PRECISION) / grand_total
    denom = jnp.max(lax.optimization_barrier(jnp.sum(kernel_matrix, axis=1))) * jnp.max(lax.optimization_barrier(jnp.sum(kernel_matrix, axis=2)))
    pseudo_inverse = newton(kernel_matrix, denom)
    mixing = matmul(pseudo_inverse, landmark_values)
    panel_single = panel_half.astype(single_float_type)
    attention_probs = jnp.einsum('xkc,xkf->cxf', panel_single, mixing, precision=HIGH_PRECISION).reshape(DOCUMENT_TOKENS, HEAD_COUNT * HEAD_SIZE)
    output_grad = jnp.dot(out_grad, out_weight, preferred_element_type=single_float_type).astype(brain_float_type).reshape(DOCUMENT_TOKENS, HEAD_COUNT, HEAD_SIZE)
    weight_grad = lax.dot_general(out_grad.astype(single_float_type), attention_probs, (((0,), (0,)), ((), ())), precision=HIGH_PRECISION)
    panel_grad = jnp.einsum('nce,cge->cgn', output_grad.astype(single_float_type), mixing, precision=HIGH_PRECISION)
    mixing_grad = jnp.einsum('cuz,zcg->cug', panel_half, output_grad, preferred_element_type=single_float_type)
    right_score_grad = (panel_matrix * (panel_grad - lax.optimization_barrier(jnp.sum(panel_grad * panel_matrix, axis=1, keepdims=True)))).astype(brain_float_type)
    query_panel_grad = jnp.einsum('fzb,zfq->bfq', right_score_grad, key_tile_half, preferred_element_type=single_float_type) * score_scale
    key_tile_panel_grad = jnp.einsum('nul,lnx->unx', right_score_grad, queries_three_dim, preferred_element_type=single_float_type) * score_scale
    inverse_grad = jnp.einsum('zxw,zpw->zxp', mixing_grad, landmark_values, precision=HIGH_PRECISION)
    landmark_values_grad_half = jnp.einsum('xrc,xrl->xcl', pseudo_inverse, mixing_grad, precision=HIGH_PRECISION).astype(brain_float_type)
    weights_grad = jnp.einsum('uec,fuc->uef', landmark_values_grad_half, values_three_dim, preferred_element_type=single_float_type)
    beta = lax.optimization_barrier(jnp.sum(weights_grad * weights_single, axis=-1, keepdims=True))
    middle_score_grad = (weights_single * (weights_grad - beta)).astype(brain_float_type)
    values_gradient = jnp.einsum('xkc,xkf->cxf', weights_single.astype(brain_float_type), landmark_values_grad_half, preferred_element_type=single_float_type)
    landmark_key_grad = jnp.einsum('fzb,zfq->bfq', middle_score_grad, query_tile_half, preferred_element_type=single_float_type) * score_scale
    landmark_query_grad = jnp.einsum('nul,lnx->unx', middle_score_grad, keys_three_dim, preferred_element_type=single_float_type) * score_scale
    pullback = jax.vjp(lambda a: newton(a, denom), kernel_matrix)[1]
    d_kernel = pullback(inverse_grad)[0]
    left_score_grad = kernel_matrix * (d_kernel - lax.optimization_barrier(jnp.sum(d_kernel * kernel_matrix, axis=-1, keepdims=True)))
    query_tile_grad = landmark_query_grad + jnp.einsum('xky,yxz->kxz', left_score_grad, key_tile, precision=HIGH_PRECISION) * score_scale
    key_tile_grad = key_tile_panel_grad + jnp.einsum('frt,rfa->tfa', left_score_grad, query_tile, precision=HIGH_PRECISION) * score_scale
    query_grad = (query_panel_grad.reshape(M, SEG, HEAD_COUNT, HEAD_SIZE) + query_tile_grad[:, None] / SEG).astype(brain_float_type).reshape(DOCUMENT_TOKENS, HEAD_COUNT * HEAD_SIZE)
    key_grad = (landmark_key_grad.reshape(M, SEG, HEAD_COUNT, HEAD_SIZE) + key_tile_grad[:, None] / SEG).astype(brain_float_type).reshape(DOCUMENT_TOKENS, HEAD_COUNT * HEAD_SIZE)
    values_gradient = values_gradient.astype(brain_float_type).reshape(DOCUMENT_TOKENS, HEAD_COUNT * HEAD_SIZE)
    return (query_grad, key_grad, values_gradient, weight_grad)
```

```python
import functools

import jax
import jax.numpy as jnp
from jax import lax
from jax.experimental import pallas as pl
from jax.experimental.pallas import tpu as pltpu
from jax.sharding import Mesh
from jax.sharding import PartitionSpec as P

HEAD_SIZE = 128
M = 64
NEWTON = 6
SCALE = HEAD_SIZE**-0.5
HIGHEST = lax.Precision.HIGHEST
F32 = jnp.float32
BF16 = jnp.bfloat16

Z, Y, X, C = 8, 4, 4, 2
SEQ = ("z", "y")
HEAD = ("x", "core")
S = Z * Y
H = 4
T = 1024
W = H * HEAD_SIZE


def dot(a, b, ca=1, cb=0, precision=None):
    return lax.dot_general(
        a, b, (((ca,), (cb,)), ((), ())), preferred_element_type=F32, precision=precision
    )


def parts_of(x):
    hi = x.astype(BF16)
    rest = x - hi.astype(F32)
    mid = rest.astype(BF16)
    lo = (rest - mid.astype(F32)).astype(BF16)
    return hi, mid, lo


def wide_dot(x, y, ca=1, cb=0):
    hi, mid, lo = parts_of(x)
    return dot(hi, y, ca, cb) + (dot(mid, y, ca, cb) + dot(lo, y, ca, cb))


def call(kernel, name, grid, in_specs, out_specs, out_shape, cost, scratch=(), vmem=60):
    return pl.pallas_call(
        kernel,
        grid=grid,
        in_specs=in_specs,
        out_specs=out_specs,
        out_shape=out_shape,
        scratch_shapes=scratch,
        name=name,
        compiler_params=pltpu.CompilerParams(vmem_limit_bytes=vmem << 20),
        cost_estimate=pl.CostEstimate(
            flops=int(cost * 1e9), bytes_accessed=1 << 20, transcendentals=0
        ),
    )


def spec(shape, index=None):
    if index is None:
        index = lambda h, n=len(shape): (0,) * n
    return pl.BlockSpec(shape, index)


def sds(shape, dtype=F32):
    return jax.ShapeDtypeStruct(shape, dtype)


COLS = spec((T, HEAD_SIZE), lambda h: (0, h))
ROWS = spec((M, T), lambda h: (h, 0))
LAND = spec((M, HEAD_SIZE), lambda h: (h, 0))
TILE = spec((1, 2 * M, HEAD_SIZE), lambda h: (h, 0, 0))
SQUARE = spec((1, M, M), lambda h: (h, 0, 0))


def means_kernel(q_ref, k_ref, o_ref):
    seg = T // 2
    rows = []
    for ref in (q_ref, k_ref):
        for s in range(2):
            x = ref[s * seg : (s + 1) * seg, :].astype(F32)
            rows.append(jnp.sum(x, axis=0, keepdims=True) / seg)
    o_ref[0] = jnp.concatenate(rows, axis=0)


def scores_kernel(q_ref, k_ref, v_ref, t_ref, f_ref, fb_ref, e_ref, sent_ref, st_ref, a_ref, mx_ref):
    qt, kt = t_ref[0, :M], t_ref[0, M:]
    s1 = dot(kt.astype(BF16), q_ref[...], 1, 1) * SCALE
    p = jnp.exp(s1 - jnp.max(s1, axis=0, keepdims=True))
    f = p / jnp.sum(p, axis=0, keepdims=True)
    f_ref[...] = f
    fb_ref[...] = f.astype(BF16)
    s2 = dot(qt.astype(BF16), k_ref[...], 1, 1) * SCALE
    top = jnp.max(s2, axis=1, keepdims=True)
    e = jnp.exp(s2 - top)
    e_ref[...] = e
    total = jnp.sum(e, axis=1, keepdims=True)
    sent_ref[:, :8] = wide_dot(e, v_ref[...]).reshape(8, 8, HEAD_SIZE)
    lane = lax.broadcasted_iota(jnp.int32, (M, HEAD_SIZE), 1)
    stats = jnp.where(lane < M, top, total)
    st_ref[...] = stats
    sent_ref[:, 8:] = stats.reshape(8, 8, HEAD_SIZE)
    sa = dot(qt, kt, 1, 1, HIGHEST) * SCALE
    pa = jnp.exp(sa - jnp.max(sa, axis=1, keepdims=True))
    a = pa / jnp.sum(pa, axis=1, keepdims=True)
    a_ref[0] = a
    col = jnp.max(jnp.sum(a, axis=0, keepdims=True), axis=1, keepdims=True)
    row = jnp.max(jnp.sum(a, axis=1, keepdims=True), axis=0, keepdims=True)
    sub = lax.broadcasted_iota(jnp.int32, (8, HEAD_SIZE), 0)
    both = jnp.where(sub < 4, col, row)

    @pl.when(pl.program_id(0) == 0)
    def _():
        mx_ref[...] = both

    @pl.when(pl.program_id(0) > 0)
    def _():
        mx_ref[...] = jnp.maximum(mx_ref[...], both)


def newton_kernel(a_ref, mx_ref, z_ref, x_ref, t2_ref, t3_ref):
    eye = (
        lax.broadcasted_iota(jnp.int32, (M, M), 0) == lax.broadcasted_iota(jnp.int32, (M, M), 1)
    ).astype(F32)
    mx = jnp.max(mx_ref[...], axis=0)
    denom = mx[0:1, 0:1] * mx[4:5, 0:1]
    zs = []
    for h in range(H):
        z = a_ref[h].T / denom
        z_ref[0, h] = z
        zs.append(z)
    for n in range(NEWTON):
        xs = [dot(a_ref[h], zs[h], precision=HIGHEST) for h in range(H)]
        t2 = [15.0 * eye - dot(x, 7.0 * eye - x, precision=HIGHEST) for x in xs]
        t3 = [13.0 * eye - dot(x, t, precision=HIGHEST) for x, t in zip(xs, t2)]
        zs = [0.25 * dot(z, t, precision=HIGHEST) for z, t in zip(zs, t3)]
        for h in range(H):
            x_ref[n, h] = xs[h]
            t2_ref[n, h] = t2[h]
            t3_ref[n, h] = t3[h]
            z_ref[n + 1, h] = zs[h]


def merge_kernel(r_ref, o_ref):
    v, st = r_ref[:, :8, :], r_ref[:, 8:, :]
    top, total = st[:, :, 0:1], st[:, :, M : M + 1]
    mx = jnp.max(top, axis=0, keepdims=True)
    scale = jnp.exp(top - mx)
    whole = jnp.sum(scale * total, axis=0)
    o_ref[:8] = jnp.sum(scale * v, axis=0) / whole
    lane = lax.broadcasted_iota(jnp.int32, (8, HEAD_SIZE), 1)
    o_ref[8:] = jnp.where(lane < M, mx[0], whole)


def outer_kernel(j_ref, fb_ref, *refs):
    ogs, g_ref = refs[:-1], refs[-1]
    for b, og in enumerate(ogs):
        res = dot(fb_ref[...], og[...])
        for y in range(2):
            g_ref[y, j_ref[b]] = res[:, y * 128 : (y + 1) * 128]


def cotangent_kernel(j_ref, w_ref, fb_ref, merged_ref, *refs):
    ogs, do_ref, sent_ref = refs[:-2], refs[-2], refs[-1]
    acc = None
    for b, og in enumerate(ogs):
        at = pl.multiple_of(j_ref[b] * W, W)
        part = dot(og[...], w_ref[pl.ds(at, W), :])
        acc = part if acc is None else acc + part
    do = acc.astype(BF16)
    do_ref[...] = do
    i = pl.program_id(0)

    @pl.when(i == 0)
    def _():
        sent_ref[:, :8] = jnp.zeros((S, 8, HEAD_SIZE), F32)
        sent_ref[:, 8:] = jnp.broadcast_to(merged_ref[...][None], (S, 16, HEAD_SIZE))

    for h in range(H):
        part = dot(fb_ref[h * M : (h + 1) * M, :], do[:, h * HEAD_SIZE : (h + 1) * HEAD_SIZE])
        sent_ref[8 * h : 8 * h + 8, :8] += part.reshape(8, 8, HEAD_SIZE)


def spread_kernel(r_ref, o_ref):
    o_ref[...] = jnp.broadcast_to(jnp.sum(r_ref[:, :8, :], axis=0)[None], (S, 8, HEAD_SIZE))


def panels_kernel(
    q_ref, k_ref, v_ref, do_ref, t_ref, f_ref, e_ref, st_ref, got_ref, dw_ref, z_ref,
    dq_ref, dk_ref, dv_ref, dt_ref, wf_ref,
):
    qtb, ktb = t_ref[0, :M].astype(BF16), t_ref[0, M:].astype(BF16)
    z, dw = z_ref[0, 0], dw_ref[...].reshape(M, HEAD_SIZE)
    bv = got_ref[:, 8:16].reshape(M, HEAD_SIZE)
    whole = got_ref[:, 16:].reshape(M, HEAD_SIZE)
    wf = dot(z, bv, precision=HIGHEST)
    wf_ref[...] = wf
    f = f_ref[...]
    df = wide_dot(wf, do_ref[...], 1, 1)
    dsf = (f * (df - jnp.sum(df * f, axis=0, keepdims=True))).astype(BF16)
    dq_ref[...] = dot(dsf, ktb, 0, 0) * SCALE
    dt_ref[0, M:] = dot(dsf, q_ref[...]) * SCALE
    dbv = dot(z, dw, 0, 0, HIGHEST).astype(BF16)
    db = dot(dbv, v_ref[...], 1, 1)
    beta = jnp.sum(dbv.astype(F32) * bv, axis=1, keepdims=True)
    rescale = jnp.exp(st_ref[:, 0:1] - whole[:, 0:1]) / whole[:, M : M + 1]
    bf = e_ref[...] * rescale
    dsb = (bf * (db - beta)).astype(BF16)
    dv_ref[...] = dot(bf.astype(BF16), dbv, 0, 0).astype(BF16)
    dk_ref[...] = dot(dsb, qtb, 0, 0) * SCALE
    dt_ref[0, :M] = dot(dsb, k_ref[...]) * SCALE


def adjoint_kernel(own_ref, dw_ref, got_ref, mx_ref, a_ref, z_ref, x_ref, t2_ref, t3_ref, t_ref, o_ref):
    eye = (
        lax.broadcasted_iota(jnp.int32, (M, M), 0) == lax.broadcasted_iota(jnp.int32, (M, M), 1)
    ).astype(F32)
    hi = functools.partial(dot, precision=HIGHEST)
    heads = range(H)
    dz = []
    for h in heads:
        dw = dw_ref[8 * h : 8 * h + 8].reshape(M, HEAD_SIZE)
        bv = got_ref[8 * h : 8 * h + 8, 8:16].reshape(M, HEAD_SIZE)
        dz.append(hi(dw, bv, 1, 1))
    da = [jnp.zeros((M, M), F32) for h in heads]
    for n in reversed(range(NEWTON)):
        x = [x_ref[n, h] for h in heads]
        g = [0.25 * d for d in dz]
        dp2 = [-hi(z_ref[n, h], g[h], 0, 0) for h in heads]
        dz = [hi(g[h], t3_ref[n, h], 1, 1) for h in heads]
        dp1 = [-hi(x[h], dp2[h], 0, 0) for h in heads]
        dx = [hi(dp2[h], t2_ref[n, h], 1, 1) for h in heads]
        dt1 = [hi(x[h], dp1[h], 0, 0) for h in heads]
        dx = [dx[h] + hi(dp1[h], 7.0 * eye - x[h], 1, 1) - dt1[h] for h in heads]
        dz = [dz[h] + hi(a_ref[h], dx[h], 0, 0) for h in heads]
        da = [da[h] + hi(dx[h], z_ref[n, h], 1, 1) for h in heads]
    mx = jnp.max(mx_ref[...], axis=0)
    denom = mx[0:1, 0:1] * mx[4:5, 0:1]
    row = lax.broadcasted_iota(jnp.int32, (M, HEAD_SIZE), 0)
    for h in heads:
        d = da[h] + dz[h].T / denom
        a = a_ref[h]
        dsa = a * (d - jnp.sum(d * a, axis=1, keepdims=True))
        dqt = hi(dsa, t_ref[h, M:]) * SCALE
        dkt = hi(dsa, t_ref[h, :M], 0, 0) * SCALE
        for i, x in enumerate((dqt, dkt)):
            for s in range(2):
                mine = jnp.where(row == own_ref[0] + s * S, x, 0.0)
                o_ref[h, 2 * i + s : 2 * i + s + 1, :] = jnp.sum(mine, axis=0, keepdims=True)


def final_kernel(dq_ref, dk_ref, got_ref, add_ref, q_out, k_out, tot_ref):
    h = pl.program_id(0)
    seg = T // 2

    @pl.when(h == 0)
    def _():
        tot_ref[...] = jnp.sum(got_ref[...], axis=0)

    for i, (ref, out) in enumerate(((dq_ref, q_out), (dk_ref, k_out))):
        for s in range(2):
            r = 2 * i + s
            rows = slice(s * seg, (s + 1) * seg)
            add = tot_ref[pl.ds(4 * h + r, 1), :] + add_ref[0, r : r + 1, :]
            out[rows, :] = (ref[rows, :] + add / seg).astype(BF16)


def weight_kernel(g_ref, wf_ref, o_ref):
    o_ref[...] = dot(g_ref[...], wf_ref[...], 0, 0, HIGHEST)


def to_all(x, axes, n):
    return lax.all_to_all(jnp.broadcast_to(x[None], (n,) + x.shape), axes, 0, 0, tiled=True)


def gather_cotangent(x, tiles):
    right = [(i, (i + 1) % X) for i in range(X)]
    left = [(i, (i - 1) % X) for i in range(X)]
    other = [(0, 1), (1, 0)]
    half = x.shape[0] // 2
    a = lax.ppermute(x, "x", right)
    b = lax.ppermute(x, "x", left)
    c = lax.ppermute(x, "core", other)
    a, b, tiles = lax.optimization_barrier((a, b, tiles))
    d = jnp.concatenate([lax.ppermute(a[:half], "x", right), lax.ppermute(b[half:], "x", left)])
    a2, b2, d2 = (lax.ppermute(y, "core", other) for y in (a, b, d))
    px, pc = lax.axis_index("x"), lax.axis_index("core")
    places = []
    for step in (0, -1, 1, 2):
        for core in (pc, 1 - pc):
            places.append(((px + step) % X) * C + core)
    return [x, c, a, a2, b, b2, d, d2], jnp.stack(places).astype(jnp.int32), tiles


def local(queries, keys, values, out_weight, out_grad):
    full = lambda *shape: spec(shape)
    smem = pl.BlockSpec(memory_space=pltpu.SMEM)
    quad = spec((1, 4, HEAD_SIZE), lambda h: (h, 0, 0))
    weight = lax.all_gather(out_weight, "y", axis=0, tiled=True)
    weight = lax.all_gather(weight, "z", axis=0, tiled=True)

    means = call(
        means_kernel, "means", (H,), [COLS, COLS], quad, sds((H, 4, HEAD_SIZE)), 1
    )(queries, keys)
    out_grad, means = lax.optimization_barrier((out_grad, means))
    tiles = to_all(means.reshape(16, HEAD_SIZE), SEQ, S)
    blocks, places, tiles = gather_cotangent(out_grad, tiles)
    tiles = tiles.transpose(1, 0, 2).reshape(H, 2 * M, HEAD_SIZE)

    f, fb, e, sent, stats, a, tops = call(
        scores_kernel, "scores", (H,), [COLS, COLS, COLS, TILE],
        [ROWS, ROWS, ROWS, spec((8, 16, HEAD_SIZE), lambda h: (h, 0, 0)), LAND, SQUARE, full(8, HEAD_SIZE)],
        [sds((H * M, T)), sds((H * M, T), BF16), sds((H * M, T)), sds((S, 16, HEAD_SIZE)),
         sds((H * M, HEAD_SIZE)), sds((H, M, M)), sds((8, HEAD_SIZE))], 5,
    )(queries, keys, values, tiles)

    got = lax.all_to_all(sent, SEQ, 0, 0, tiled=True)
    tops = to_all(tops, HEAD, X * C)
    merged = call(
        merge_kernel, "merge", (1,), [full(S, 16, HEAD_SIZE)], full(16, HEAD_SIZE), sds((16, HEAD_SIZE)), 1
    )(got)
    inverse, xs, t2, t3 = call(
        newton_kernel, "newton", (1,), [full(H, M, M), full(X * C, 8, HEAD_SIZE)],
        [full(NEWTON + 1, H, M, M)] + [full(NEWTON, H, M, M)] * 3,
        [sds((NEWTON + 1, H, M, M))] + [sds((NEWTON, H, M, M))] * 3, 6,
    )(a, tops)

    wide = spec((T, 256), lambda i: (0, i))
    g = call(
        outer_kernel, "outer", (2,), [smem, full(H * M, T)] + [wide] * 8,
        spec((2, Z, H * M, 128), lambda i: (i, 0, 0, 0)), sds((Y, Z, H * M, 128)), 6,
    )(places, fb, *blocks)
    g = lax.psum_scatter(g, "y", scatter_dimension=0, tiled=True)
    g = lax.psum_scatter(g.reshape(Z, H * M, 128), "z", scatter_dimension=0, tiled=True)
    g = g.reshape(H * M, 128)

    tokens = 512
    panel = spec((H * M, tokens), lambda i: (0, i))
    block = spec((tokens, W), lambda i: (i, 0))
    do, sent = call(
        cotangent_kernel, "cotangent", (T // tokens,),
        [smem, full(Z * Y * 128, W), panel, full(16, HEAD_SIZE)] + [block] * 8,
        [block, full(S, 24, HEAD_SIZE)], [sds((T, W), BF16), sds((S, 24, HEAD_SIZE))], 10,
    )(places, weight, fb, merged, *blocks)

    got = lax.all_to_all(sent, SEQ, 0, 0, tiled=True)
    sent = call(
        spread_kernel, "spread", (1,), [full(S, 24, HEAD_SIZE)], full(S, 8, HEAD_SIZE), sds((S, 8, HEAD_SIZE)), 1
    )(got)
    dw = lax.all_to_all(sent, SEQ, 0, 0, tiled=True)

    dq, dk, dv, dt, wf = call(
        panels_kernel, "panels", (H,),
        [COLS, COLS, COLS, COLS, TILE, ROWS, ROWS, LAND, spec((8, 24, HEAD_SIZE), lambda h: (h, 0, 0)),
         spec((8, 8, HEAD_SIZE), lambda h: (h, 0, 0)), spec((1, 1, M, M), lambda h: (NEWTON, h, 0, 0))],
        [COLS, COLS, COLS, TILE, LAND],
        [sds((T, W)), sds((T, W)), sds((T, W), BF16), sds((H, 2 * M, HEAD_SIZE)),
         sds((H * M, HEAD_SIZE))], 8,
    )(queries, keys, values, do, tiles, f, e, stats, got, dw, inverse)

    sent = dt.reshape(16, S, HEAD_SIZE).transpose(1, 0, 2)
    summed = lax.all_to_all(sent, SEQ, 0, 0, tiled=True)
    own = lax.axis_index(SEQ).astype(jnp.int32).reshape(1)
    da = call(
        adjoint_kernel, "adjoint", (1,),
        [smem, full(S, 8, HEAD_SIZE), full(S, 24, HEAD_SIZE), full(X * C, 8, HEAD_SIZE), full(H, M, M),
         full(NEWTON + 1, H, M, M)] + [full(NEWTON, H, M, M)] * 3 + [full(H, 2 * M, HEAD_SIZE)],
        full(H, 4, HEAD_SIZE), sds((H, 4, HEAD_SIZE)), 11,
    )(own, dw, got, tops, a, inverse, xs, t2, t3, tiles)
    query_grad, key_grad = call(
        final_kernel, "final", (H,), [COLS, COLS, full(S, 16, HEAD_SIZE), quad],
        [COLS, COLS], [sds((T, W), BF16)] * 2, 2, [pltpu.VMEM((16, HEAD_SIZE), F32)],
    )(dq, dk, summed, da)
    weight_grad = call(
        weight_kernel, "weight", (H,), [spec((M, 128), lambda h: (h, 0)), LAND],
        spec((128, HEAD_SIZE), lambda h: (0, h)), sds((128, W)), 2,
    )(g, wf)
    return query_grad, key_grad, dv, weight_grad


def solution(mesh):
    grid = Mesh(mesh.devices.reshape(Z, Y, X, C), SEQ + HEAD)
    place = P(SEQ, HEAD)
    return jax.shard_map(
        local, mesh=grid, in_specs=(place,) * 5, out_specs=(place,) * 4, check_vma=False
    )
```

```python
import jax
import jax.numpy as jnp
from jax import lax
from jax.experimental import pallas as pl
from jax.experimental.pallas import tpu as pltpu
from jax.sharding import Mesh
from jax.sharding import PartitionSpec as P

HEAD_SIZE = 128
M = 64
NEWTON = 6
SCALE = HEAD_SIZE**-0.5
HIGHEST = lax.Precision.HIGHEST
F32 = jnp.float32
BF16 = jnp.bfloat16

Z, Y, X, C = 8, 4, 4, 2
SEQ = ("z", "y")
HEAD = ("x", "core")
S = Z * Y
H = 4
T = 1024
W = H * HEAD_SIZE


def dot(a, b, ca=1, cb=0, precision=None):
    return lax.dot_general(
        a, b, (((ca,), (cb,)), ((), ())), preferred_element_type=F32, precision=precision
    )


def parts_of(x):
    hi = x.astype(BF16)
    rest = x - hi.astype(F32)
    mid = rest.astype(BF16)
    lo = (rest - mid.astype(F32)).astype(BF16)
    return hi, mid, lo


def wide_dot(x, y, ca=1, cb=0):
    hi, mid, lo = parts_of(x)
    return dot(hi, y, ca, cb) + (dot(mid, y, ca, cb) + dot(lo, y, ca, cb))


def close_dot(x, y, ca=1, cb=0):
    xh, yh = x.astype(BF16), y.astype(BF16)
    xl = (x - xh.astype(F32)).astype(BF16)
    yl = (y - yh.astype(F32)).astype(BF16)
    return dot(xh, yh, ca, cb) + (dot(xh, yl, ca, cb) + dot(xl, yh, ca, cb))


def call(kernel, name, grid, in_specs, out_specs, out_shape, cost, scratch=(), vmem=62):
    return pl.pallas_call(
        kernel,
        grid=grid,
        in_specs=in_specs,
        out_specs=out_specs,
        out_shape=out_shape,
        scratch_shapes=scratch,
        name=name,
        compiler_params=pltpu.CompilerParams(vmem_limit_bytes=vmem << 20),
        cost_estimate=pl.CostEstimate(
            flops=int(cost * 1e9), bytes_accessed=1 << 20, transcendentals=0
        ),
    )


def spec(shape, index=None):
    if index is None:
        index = lambda h, n=len(shape): (0,) * n
    return pl.BlockSpec(shape, index)


def sds(shape, dtype=F32):
    return jax.ShapeDtypeStruct(shape, dtype)


COLS = spec((T, HEAD_SIZE), lambda h: (0, h))
ROWS = spec((M, T), lambda h: (h, 0))
LAND = spec((M, HEAD_SIZE), lambda h: (h, 0))
TILE = spec((1, 2 * M, HEAD_SIZE), lambda h: (h, 0, 0))
SQUARE = spec((1, M, M), lambda h: (h, 0, 0))


def means_kernel(q_ref, k_ref, o_ref):
    for i, ref in enumerate((q_ref, k_ref)):
        mean = jnp.sum(ref[...].astype(F32), axis=0, keepdims=True) / ref.shape[0]
        for h in range(H):
            o_ref[0, H * i + h : H * i + h + 1, :] = mean[:, h * HEAD_SIZE : (h + 1) * HEAD_SIZE]


def scores_kernel(q_ref, k_ref, v_ref, t_ref, f_ref, fb_ref, e_ref, sent_ref, st_ref, a_ref, mx_ref):
    qt, kt = t_ref[0, :M], t_ref[0, M:]
    s1 = dot(kt.astype(BF16), q_ref[...], 1, 1) * SCALE
    p = jnp.exp(s1 - jnp.max(s1, axis=0, keepdims=True))
    f = p / jnp.sum(p, axis=0, keepdims=True)
    f_ref[...] = f
    fb_ref[...] = f.astype(BF16)
    s2 = dot(qt.astype(BF16), k_ref[...], 1, 1) * SCALE
    top = jnp.max(s2, axis=1, keepdims=True)
    e = jnp.exp(s2 - top)
    e_ref[...] = e
    total = jnp.sum(e, axis=1, keepdims=True)
    sent_ref[:, :8] = wide_dot(e, v_ref[...]).reshape(8, 8, HEAD_SIZE)
    lane = lax.broadcasted_iota(jnp.int32, (M, HEAD_SIZE), 1)
    stats = jnp.where(lane < M, top, total)
    st_ref[...] = stats
    sent_ref[:, 8:] = stats.reshape(8, 8, HEAD_SIZE)
    sa = dot(qt, kt, 1, 1, HIGHEST) * SCALE
    pa = jnp.exp(sa - jnp.max(sa, axis=1, keepdims=True))
    a = pa / jnp.sum(pa, axis=1, keepdims=True)
    a_ref[0] = a
    col = jnp.max(jnp.sum(a, axis=0, keepdims=True), axis=1, keepdims=True)
    row = jnp.max(jnp.sum(a, axis=1, keepdims=True), axis=0, keepdims=True)
    sub = lax.broadcasted_iota(jnp.int32, (8, HEAD_SIZE), 0)
    both = jnp.where(sub < 4, col, row)

    @pl.when(pl.program_id(0) == 0)
    def _():
        mx_ref[...] = both

    @pl.when(pl.program_id(0) > 0)
    def _():
        mx_ref[...] = jnp.maximum(mx_ref[...], both)


def newton_kernel(a_ref, mx_ref, z_ref, x_ref, t2_ref, t3_ref):
    eye = (
        lax.broadcasted_iota(jnp.int32, (M, M), 0) == lax.broadcasted_iota(jnp.int32, (M, M), 1)
    ).astype(F32)
    mx = mx_ref[...]
    denom = mx[0:1, 0:1] * mx[4:5, 0:1]
    zs = []
    for h in range(H):
        z = a_ref[h].T / denom
        z_ref[0, h] = z
        zs.append(z)
    for n in range(NEWTON):
        xs = [dot(a_ref[h], zs[h], precision=HIGHEST) for h in range(H)]
        t2 = [15.0 * eye - dot(x, 7.0 * eye - x, precision=HIGHEST) for x in xs]
        t3 = [13.0 * eye - dot(x, t, precision=HIGHEST) for x, t in zip(xs, t2)]
        zs = [0.25 * dot(z, t, precision=HIGHEST) for z, t in zip(zs, t3)]
        for h in range(H):
            x_ref[n, h] = xs[h]
            t2_ref[n, h] = t2[h]
            t3_ref[n, h] = t3[h]
            z_ref[n + 1, h] = zs[h]


def merge_kernel(r_ref, o_ref):
    v, st = r_ref[:, :8, :], r_ref[:, 8:, :]
    top, total = st[:, :, 0:1], st[:, :, M : M + 1]
    mx = jnp.max(top, axis=0, keepdims=True)
    scale = jnp.exp(top - mx)
    whole = jnp.sum(scale * total, axis=0)
    o_ref[:8] = jnp.sum(scale * v, axis=0) / whole
    lane = lax.broadcasted_iota(jnp.int32, (8, HEAD_SIZE), 1)
    o_ref[8:] = jnp.where(lane < M, mx[0], whole)


def outer_kernel(j_ref, fb_ref, *refs):
    ogs, out = refs[:10], refs[10]
    fb = fb_ref[...]
    for b in range(8):
        if b < 6:
            res = dot(fb, ogs[b][...])
        else:
            top, low = ogs[2 * b - 6], ogs[2 * b - 5]
            res = dot(fb[:, : T // 2], top[...]) + dot(fb[:, T // 2 :], low[...])
        for y in range(2):
            out[y, j_ref[b]] = res[:, y * 128 : (y + 1) * 128].astype(BF16)


def add_kernel(*refs):
    a, b, c, d = (ref[...].astype(F32) for ref in refs[:-1])
    refs[-1][...] = (a + b) + (c + d)


def cotangent_kernel(j_ref, w_ref, fb_ref, merged_ref, *refs):
    ogs, do_ref, sent_ref = refs[:10], refs[10], refs[11]
    i = pl.program_id(0)
    acc = None
    for b in range(8):
        at = pl.multiple_of(j_ref[b] * W, W)
        if b < 6:
            og = ogs[b][...]
        else:
            og = jnp.where(i == 0, ogs[2 * b - 6][...], ogs[2 * b - 5][...])
        part = dot(og, w_ref[pl.ds(at, W), :])
        acc = part if acc is None else acc + part
    do = acc.astype(BF16)
    do_ref[...] = do

    @pl.when(i == 0)
    def _():
        sent_ref[:, :8] = jnp.zeros((S, 8, HEAD_SIZE), F32)
        sent_ref[:, 8:] = jnp.broadcast_to(merged_ref[...][None], (S, 16, HEAD_SIZE))

    for h in range(H):
        part = dot(fb_ref[h * M : (h + 1) * M, :], do[:, h * HEAD_SIZE : (h + 1) * HEAD_SIZE])
        sent_ref[8 * h : 8 * h + 8, :8] += part.reshape(8, 8, HEAD_SIZE)


def spread_kernel(r_ref, o_ref):
    o_ref[...] = jnp.broadcast_to(jnp.sum(r_ref[:, :8, :], axis=0)[None], (S, 8, HEAD_SIZE))


def put_rows(ref, x):
    for s in range(2):
        ref[:, pl.ds(2 * pl.program_id(0) + s, 1), :] = x[s * S : (s + 1) * S][:, None, :]


def query_panel_kernel(q_ref, do_ref, t_ref, f_ref, got_ref, z_ref, dq_ref, dt_ref, wf_ref):
    ktb = t_ref[0, M:].astype(BF16)
    bv = got_ref[:, 8:16].reshape(M, HEAD_SIZE)
    wf = dot(z_ref[0, 0], bv, precision=HIGHEST)
    wf_ref[...] = wf
    f = f_ref[...]
    df = wide_dot(wf, do_ref[...], 1, 1)
    dsf = (f * (df - jnp.sum(df * f, axis=0, keepdims=True))).astype(BF16)
    put_rows(dt_ref, dot(dsf, q_ref[...]) * SCALE)
    dq_ref[...] = dot(dsf, ktb, 0, 0) * SCALE


def key_panel_kernel(
    k_ref, v_ref, e_ref, st_ref, got_ref, dw_ref, z_ref, dt_ref, dsb_ref, bb_ref, dbv_ref, sent_ref
):
    dw = dw_ref[...].reshape(M, HEAD_SIZE)
    bv = got_ref[:, 8:16].reshape(M, HEAD_SIZE)
    whole = got_ref[:, 16:].reshape(M, HEAD_SIZE)
    dbv = dot(z_ref[0, 0], dw, 0, 0, HIGHEST).astype(BF16)
    dbv_ref[...] = dbv
    db = dot(dbv, v_ref[...], 1, 1)
    beta = jnp.sum(dbv.astype(F32) * bv, axis=1, keepdims=True)
    rescale = jnp.exp(st_ref[:, 0:1] - whole[:, 0:1]) / whole[:, M : M + 1]
    bf = e_ref[...] * rescale
    dsb = (bf * (db - beta)).astype(BF16)
    dsb_ref[...] = dsb
    bb_ref[...] = bf.astype(BF16)
    put_rows(sent_ref, dot(dsb, k_ref[...]) * SCALE)

    @pl.when(pl.program_id(0) == 0)
    def _():
        sent_ref[:, 8:] = dt_ref[...]


def key_rows_kernel(dsb_ref, bb_ref, dbv_ref, t_ref, dk_ref, dv_ref):
    dk_ref[...] = dot(dsb_ref[...], t_ref[0, :M].astype(BF16), 0, 0) * SCALE
    dv_ref[...] = dot(bb_ref[...], dbv_ref[...], 0, 0).astype(BF16)


def adjoint_kernel(own_ref, dw_ref, got_ref, mx_ref, a_ref, z_ref, x_ref, t2_ref, t3_ref, t_ref, o_ref):
    eye = (
        lax.broadcasted_iota(jnp.int32, (M, M), 0) == lax.broadcasted_iota(jnp.int32, (M, M), 1)
    ).astype(F32)
    hi = close_dot
    heads = range(H)
    dz = []
    for h in heads:
        dw = dw_ref[8 * h : 8 * h + 8].reshape(M, HEAD_SIZE)
        bv = got_ref[8 * h : 8 * h + 8, 8:16].reshape(M, HEAD_SIZE)
        dz.append(hi(dw, bv, 1, 1))
    da = [jnp.zeros((M, M), F32) for h in heads]
    for n in reversed(range(NEWTON)):
        x = [x_ref[n, h] for h in heads]
        g = [0.25 * d for d in dz]
        dp2 = [-hi(z_ref[n, h], g[h], 0, 0) for h in heads]
        dz = [hi(g[h], t3_ref[n, h], 1, 1) for h in heads]
        dp1 = [-hi(x[h], dp2[h], 0, 0) for h in heads]
        dx = [hi(dp2[h], t2_ref[n, h], 1, 1) for h in heads]
        dt1 = [hi(x[h], dp1[h], 0, 0) for h in heads]
        dx = [dx[h] + hi(dp1[h], 7.0 * eye - x[h], 1, 1) - dt1[h] for h in heads]
        dz = [dz[h] + hi(a_ref[h], dx[h], 0, 0) for h in heads]
        da = [da[h] + hi(dx[h], z_ref[n, h], 1, 1) for h in heads]
    mx = mx_ref[...]
    denom = mx[0:1, 0:1] * mx[4:5, 0:1]
    row = lax.broadcasted_iota(jnp.int32, (M, HEAD_SIZE), 0)
    for h in heads:
        d = da[h] + dz[h].T / denom
        a = a_ref[h]
        dsa = a * (d - jnp.sum(d * a, axis=1, keepdims=True))
        dqt = hi(dsa, t_ref[h, M:]) * SCALE
        dkt = hi(dsa, t_ref[h, :M], 0, 0) * SCALE
        for i, x in enumerate((dqt, dkt)):
            for s in range(2):
                mine = jnp.where(row == own_ref[0] + s * S, x, 0.0)
                r = 8 * i + 2 * h + s
                o_ref[r : r + 1, :] = jnp.sum(mine, axis=0, keepdims=True)


def final_kernel(dq_ref, dk_ref, got_ref, add_ref, q_out, k_out, tot_ref):
    i = pl.program_id(0)

    @pl.when(i == 0)
    def _():
        tot_ref[...] = (jnp.sum(got_ref[...], axis=0) + add_ref[...]) / (T // 2)

    s = i // 2
    for n, (ref, out) in enumerate(((dq_ref, q_out), (dk_ref, k_out))):
        for h in range(H):
            cols = slice(h * HEAD_SIZE, (h + 1) * HEAD_SIZE)
            add = tot_ref[pl.ds(8 * n + 2 * h + s, 1), :]
            out[:, cols] = (ref[:, cols] + add).astype(BF16)


def weight_kernel(g_ref, wf_ref, o_ref):
    for h in range(H):
        rows = slice(h * M, (h + 1) * M)
        o_ref[:, h * HEAD_SIZE : (h + 1) * HEAD_SIZE] = dot(
            g_ref[rows, :], wf_ref[rows, :], 0, 0, HIGHEST
        )


def to_all(x, axes, n):
    return lax.all_to_all(jnp.broadcast_to(x[None], (n,) + x.shape), axes, 0, 0, tiled=True)


def gather_rows(x, means):
    here = lax.axis_index("y")
    blocks = [
        lax.ppermute(x, "y", [(i, (i + step) % Y) for i in range(Y)]) for step in range(1, Y)
    ]
    blocks, means = lax.optimization_barrier((blocks, means))
    out = jnp.zeros((Y,) + x.shape, x.dtype)
    out = lax.dynamic_update_index_in_dim(out, x, here, 0)
    for step, block in enumerate(blocks, 1):
        out = lax.dynamic_update_index_in_dim(out, block, (here - step) % Y, 0)
    return out.reshape(Y * x.shape[0], x.shape[1]), means


RIGHT = [(i, (i + 1) % X) for i in range(X)]
LEFT = [(i, (i - 1) % X) for i in range(X)]
OTHER = [(0, 1), (1, 0)]


def places():
    px, pc = lax.axis_index("x"), lax.axis_index("core")
    out = []
    for step in (0, -1, 1, 2):
        for core in (pc, 1 - pc):
            out.append(((px + step) % X) * C + core)
    return jnp.stack(out).astype(jnp.int32)


def local(queries, keys, values, out_weight, out_grad):
    full = lambda *shape: spec(shape)
    smem = pl.BlockSpec(memory_space=pltpu.SMEM)
    half = spec((T // 2, W), lambda s: (s, 0))
    slab = spec((T // 4, W), lambda i: (i, 0))
    means = call(
        means_kernel, "means", (2,), [half, half], spec((1, 8, HEAD_SIZE), lambda s: (s, 0, 0)),
        sds((2, 8, HEAD_SIZE)), 2,
    )(queries, keys)
    weight, means = gather_rows(out_weight, means)
    weight = lax.all_gather(weight, "z", axis=0, tiled=True)
    out_grad, means = lax.optimization_barrier((out_grad, means))
    tiles = to_all(means.reshape(16, HEAD_SIZE), SEQ, S)
    right = lax.ppermute(out_grad, "x", RIGHT)
    left = lax.ppermute(out_grad, "x", LEFT)
    beside = lax.ppermute(out_grad, "core", OTHER)
    right, left, tiles = lax.optimization_barrier((right, left, tiles))
    far = [lax.ppermute(right[: T // 2], "x", RIGHT), lax.ppermute(left[T // 2 :], "x", LEFT)]
    right2, left2 = lax.ppermute(right, "core", OTHER), lax.ppermute(left, "core", OTHER)
    tiles = tiles.reshape(S, 2, 2, H, HEAD_SIZE).transpose(3, 2, 1, 0, 4)
    tiles = tiles.reshape(H, 2 * M, HEAD_SIZE)

    f, fb, e, sent, stats, a, tops = call(
        scores_kernel, "scores", (H,), [COLS, COLS, COLS, TILE],
        [ROWS, ROWS, ROWS, spec((8, 16, HEAD_SIZE), lambda h: (h, 0, 0)), LAND, SQUARE, full(8, HEAD_SIZE)],
        [sds((H * M, T)), sds((H * M, T), BF16), sds((H * M, T)), sds((S, 16, HEAD_SIZE)),
         sds((H * M, HEAD_SIZE)), sds((H, M, M)), sds((8, HEAD_SIZE))], 5,
    )(queries, keys, values, tiles)

    far, sent, tops, fb = lax.optimization_barrier((far, sent, tops, fb))
    far2 = [lax.ppermute(x, "core", OTHER) for x in far]
    blocks = [out_grad, beside, right, right2, left, left2, far[0], far[1], far2[0], far2[1]]
    where = places()

    got = lax.all_to_all(sent, SEQ, 0, 0, tiled=True)
    wide = spec((T, 256), lambda i: (0, i))
    short = spec((T // 2, 256), lambda i: (0, i))
    g = call(
        outer_kernel, "outer", (2,), [smem, full(H * M, T)] + [wide] * 6 + [short] * 4,
        spec((2, Z, H * M, 128), lambda i: (i, 0, 0, 0)), sds((Y, Z, H * M, 128), BF16), 6,
    )(where, fb, *blocks)
    g, tops = lax.optimization_barrier((g, tops))
    tops = jnp.maximum(tops, lax.ppermute(tops, "core", OTHER))
    ahead = [lax.ppermute(tops, "x", [(i, (i + n) % X) for i in range(X)]) for n in range(1, X)]
    tops = jnp.maximum(jnp.maximum(tops, ahead[0]), jnp.maximum(ahead[1], ahead[2]))
    g, got, tops = lax.optimization_barrier((g, got, tops))
    here = lax.axis_index("y")
    gs = [lax.dynamic_index_in_dim(g, (here + n) % Y, keepdims=False) for n in range(Y)]
    gs[1:] = [
        lax.ppermute(gs[n], "y", [(i, (i + n) % Y) for i in range(Y)]) for n in range(1, Y)
    ]
    merged = call(
        merge_kernel, "merge", (1,), [full(S, 16, HEAD_SIZE)], full(16, HEAD_SIZE), sds((16, HEAD_SIZE)), 1
    )(got)

    tokens = 512
    panel = spec((H * M, tokens), lambda i: (0, i))
    block = spec((tokens, W), lambda i: (i, 0))
    do, sent = call(
        cotangent_kernel, "cotangent", (T // tokens,),
        [smem, full(Z * Y * 128, W), panel, full(16, HEAD_SIZE)]
        + [block] * 6 + [full(T // 2, W)] * 4,
        [block, full(S, 24, HEAD_SIZE)], [sds((T, W), BF16), sds((S, 24, HEAD_SIZE))], 10,
    )(where, weight, fb, merged, *blocks)

    gs, do = lax.optimization_barrier((gs, do))
    inverse, xs, t2, t3 = call(
        newton_kernel, "newton", (1,), [full(H, M, M), full(8, HEAD_SIZE)],
        [full(NEWTON + 1, H, M, M)] + [full(NEWTON, H, M, M)] * 3,
        [sds((NEWTON + 1, H, M, M))] + [sds((NEWTON, H, M, M))] * 3, 6,
    )(a, tops)

    g = call(
        add_kernel, "add", (Z // 2,), [spec((2, H * M, 128), lambda i: (i, 0, 0))] * Y,
        spec((2, H * M, 128), lambda i: (i, 0, 0)), sds((Z, H * M, 128)), 2,
    )(*gs)
    g = lax.psum_scatter(g, "z", scatter_dimension=0, tiled=True).reshape(H * M, 128)
    got = lax.all_to_all(sent, SEQ, 0, 0, tiled=True)
    sent = call(
        spread_kernel, "spread", (1,), [full(S, 24, HEAD_SIZE)], full(S, 8, HEAD_SIZE), sds((S, 8, HEAD_SIZE)), 1
    )(got)
    sent, got = lax.optimization_barrier((sent, got))
    dw = lax.all_to_all(sent, SEQ, 0, 0, tiled=True)

    parts = spec((8, 24, HEAD_SIZE), lambda h: (h, 0, 0))
    last = spec((1, 1, M, M), lambda h: (NEWTON, h, 0, 0))
    dq, dktf, wf = call(
        query_panel_kernel, "query_panel", (H,), [COLS, COLS, TILE, ROWS, parts, last],
        [COLS, full(S, 8, HEAD_SIZE), LAND], [sds((T, W)), sds((S, 8, HEAD_SIZE)), sds((H * M, HEAD_SIZE))], 5,
    )(queries, do, tiles, f, got, inverse)
    dsb, bb, dbv, sent = call(
        key_panel_kernel, "key_panel", (H,),
        [COLS, COLS, ROWS, LAND, parts, spec((8, 8, HEAD_SIZE), lambda h: (h, 0, 0)), last,
         full(S, 8, HEAD_SIZE)],
        [ROWS, ROWS, LAND, full(S, 16, HEAD_SIZE)],
        [sds((H * M, T), BF16), sds((H * M, T), BF16), sds((H * M, HEAD_SIZE), BF16),
         sds((S, 16, HEAD_SIZE))], 4,
    )(keys, values, e, stats, got, dw, inverse, dktf)
    dk, dv = call(
        key_rows_kernel, "key_rows", (H,), [ROWS, ROWS, LAND, TILE], [COLS, COLS],
        [sds((T, W)), sds((T, W), BF16)], 4,
    )(dsb, bb, dbv, tiles)

    summed = lax.all_to_all(sent, SEQ, 0, 0, tiled=True)
    g, summed = lax.optimization_barrier((g, summed))
    own = lax.axis_index(SEQ).astype(jnp.int32).reshape(1)
    da = call(
        adjoint_kernel, "adjoint", (1,),
        [smem, full(S, 8, HEAD_SIZE), full(S, 24, HEAD_SIZE), full(8, HEAD_SIZE), full(H, M, M),
         full(NEWTON + 1, H, M, M)] + [full(NEWTON, H, M, M)] * 3 + [full(H, 2 * M, HEAD_SIZE)],
        full(16, HEAD_SIZE), sds((16, HEAD_SIZE)), 9,
    )(own, dw, got, tops, a, inverse, xs, t2, t3, tiles)
    query_grad, key_grad = call(
        final_kernel, "final", (4,), [slab, slab, full(S, 16, HEAD_SIZE), full(16, HEAD_SIZE)],
        [slab, slab], [sds((T, W), BF16)] * 2, 2, [pltpu.VMEM((16, HEAD_SIZE), F32)],
    )(dq, dk, summed, da)
    weight_grad = call(
        weight_kernel, "weight", (1,), [full(H * M, 128), full(H * M, HEAD_SIZE)], full(128, W), sds((128, W)), 2,
    )(g, wf)
    return query_grad, key_grad, dv, weight_grad


def solution(mesh):
    grid = Mesh(mesh.devices.reshape(Z, Y, X, C), SEQ + HEAD)
    place = P(SEQ, HEAD)
    return jax.shard_map(
        local, mesh=grid, in_specs=(place,) * 5, out_specs=(place,) * 4, check_vma=False
    )
```

```python
import jax
import jax.numpy as jnp
from jax import lax
from jax.experimental import pallas as pl
from jax.experimental.pallas import tpu as pltpu
from jax.sharding import Mesh
from jax.sharding import PartitionSpec as P

HEAD_SIZE = 128
M = 64
NEWTON = 6
SCALE = HEAD_SIZE**-0.5
HIGHEST = lax.Precision.HIGHEST
F32 = jnp.float32
BF16 = jnp.bfloat16

Z, Y, X, C = 8, 4, 4, 2
SEQ = ("z", "y")
HEAD = ("x", "core")
S = Z * Y
H = 4
T = 1024
W = H * HEAD_SIZE


def dot(a, b, ca=1, cb=0, precision=None):
    return lax.dot_general(
        a, b, (((ca,), (cb,)), ((), ())), preferred_element_type=F32, precision=precision
    )


def parts_of(x):
    hi = x.astype(BF16)
    rest = x - hi.astype(F32)
    mid = rest.astype(BF16)
    lo = (rest - mid.astype(F32)).astype(BF16)
    return hi, mid, lo


def wide_dot(x, y, ca=1, cb=0):
    hi, mid, lo = parts_of(x)
    return dot(hi, y, ca, cb) + (dot(mid, y, ca, cb) + dot(lo, y, ca, cb))


def close_dot(x, y, ca=1, cb=0):
    xh, yh = x.astype(BF16), y.astype(BF16)
    xl = (x - xh.astype(F32)).astype(BF16)
    yl = (y - yh.astype(F32)).astype(BF16)
    return dot(xh, yh, ca, cb) + (dot(xh, yl, ca, cb) + dot(xl, yh, ca, cb))


def call(kernel, name, grid, in_specs, out_specs, out_shape, cost, scratch=(), vmem=62):
    return pl.pallas_call(
        kernel,
        grid=grid,
        in_specs=in_specs,
        out_specs=out_specs,
        out_shape=out_shape,
        scratch_shapes=scratch,
        name=name,
        compiler_params=pltpu.CompilerParams(vmem_limit_bytes=vmem << 20),
        cost_estimate=pl.CostEstimate(
            flops=int(cost * 1e9), bytes_accessed=1 << 20, transcendentals=0
        ),
    )


def spec(shape, index=None):
    if index is None:
        index = lambda h, n=len(shape): (0,) * n
    return pl.BlockSpec(shape, index)


def sds(shape, dtype=F32):
    return jax.ShapeDtypeStruct(shape, dtype)


COLS = spec((T, HEAD_SIZE), lambda h: (0, h))
ROWS = spec((M, T), lambda h: (h, 0))
LAND = spec((M, HEAD_SIZE), lambda h: (h, 0))
TILE = spec((1, 2 * M, HEAD_SIZE), lambda h: (h, 0, 0))
SQUARE = spec((1, M, M), lambda h: (h, 0, 0))


def means_kernel(q_ref, k_ref, o_ref):
    for i, ref in enumerate((q_ref, k_ref)):
        mean = jnp.sum(ref[...].astype(F32), axis=0, keepdims=True) / ref.shape[0]
        for h in range(H):
            o_ref[0, H * i + h : H * i + h + 1, :] = mean[:, h * HEAD_SIZE : (h + 1) * HEAD_SIZE]


def scores_kernel(q_ref, k_ref, v_ref, t_ref, f_ref, fb_ref, e_ref, sent_ref, st_ref, a_ref, mx_ref):
    qt, kt = t_ref[0, :M], t_ref[0, M:]
    s1 = dot(kt.astype(BF16), q_ref[...], 1, 1) * SCALE
    p = jnp.exp(s1 - jnp.max(s1, axis=0, keepdims=True))
    f = p / jnp.sum(p, axis=0, keepdims=True)
    f_ref[...] = f
    fb_ref[...] = f.astype(BF16)
    s2 = dot(qt.astype(BF16), k_ref[...], 1, 1) * SCALE
    top = jnp.max(s2, axis=1, keepdims=True)
    e = jnp.exp(s2 - top)
    e_ref[...] = e
    total = jnp.sum(e, axis=1, keepdims=True)
    sent_ref[:, :8] = wide_dot(e, v_ref[...]).reshape(8, 8, HEAD_SIZE)
    lane = lax.broadcasted_iota(jnp.int32, (M, HEAD_SIZE), 1)
    stats = jnp.where(lane < M, top, total)
    st_ref[...] = stats
    sent_ref[:, 8:] = stats.reshape(8, 8, HEAD_SIZE)
    sa = dot(qt, kt, 1, 1, HIGHEST) * SCALE
    pa = jnp.exp(sa - jnp.max(sa, axis=1, keepdims=True))
    a = pa / jnp.sum(pa, axis=1, keepdims=True)
    a_ref[0] = a
    col = jnp.max(jnp.sum(a, axis=0, keepdims=True), axis=1, keepdims=True)
    row = jnp.max(jnp.sum(a, axis=1, keepdims=True), axis=0, keepdims=True)
    sub = lax.broadcasted_iota(jnp.int32, (8, HEAD_SIZE), 0)
    both = jnp.where(sub < 4, col, row)

    @pl.when(pl.program_id(0) == 0)
    def _():
        mx_ref[...] = both

    @pl.when(pl.program_id(0) > 0)
    def _():
        mx_ref[...] = jnp.maximum(mx_ref[...], both)


def newton_kernel(a_ref, mx_ref, z_ref, x_ref, t2_ref, t3_ref):
    eye = (
        lax.broadcasted_iota(jnp.int32, (M, M), 0) == lax.broadcasted_iota(jnp.int32, (M, M), 1)
    ).astype(F32)
    mx = mx_ref[...]
    denom = mx[0:1, 0:1] * mx[4:5, 0:1]
    zs = []
    for h in range(H):
        z = a_ref[h].T / denom
        z_ref[0, h] = z
        zs.append(z)
    for n in range(NEWTON):
        xs = [dot(a_ref[h], zs[h], precision=HIGHEST) for h in range(H)]
        t2 = [15.0 * eye - dot(x, 7.0 * eye - x, precision=HIGHEST) for x in xs]
        t3 = [13.0 * eye - dot(x, t, precision=HIGHEST) for x, t in zip(xs, t2)]
        zs = [0.25 * dot(z, t, precision=HIGHEST) for z, t in zip(zs, t3)]
        for h in range(H):
            x_ref[n, h] = xs[h]
            t2_ref[n, h] = t2[h]
            t3_ref[n, h] = t3[h]
            z_ref[n + 1, h] = zs[h]


def merge_kernel(r_ref, o_ref):
    v, st = r_ref[:, :8, :], r_ref[:, 8:, :]
    top, total = st[:, :, 0:1], st[:, :, M : M + 1]
    mx = jnp.max(top, axis=0, keepdims=True)
    scale = jnp.exp(top - mx)
    whole = jnp.sum(scale * total, axis=0)
    o_ref[:8] = jnp.sum(scale * v, axis=0) / whole
    lane = lax.broadcasted_iota(jnp.int32, (8, HEAD_SIZE), 1)
    o_ref[8:] = jnp.where(lane < M, mx[0], whole)


def outer_kernel(j_ref, fb_ref, *refs):
    ogs, out = refs[:10], refs[10]
    fb = fb_ref[...]
    for b in range(8):
        if b < 6:
            res = dot(fb, ogs[b][...])
        else:
            top, low = ogs[2 * b - 6], ogs[2 * b - 5]
            res = dot(fb[:, : T // 2], top[...]) + dot(fb[:, T // 2 :], low[...])
        for y in range(2):
            out[y, j_ref[b]] = res[:, y * 128 : (y + 1) * 128].astype(BF16)


def cotangent_kernel(j_ref, w_ref, fb_ref, merged_ref, *refs):
    ogs, do_ref, sent_ref = refs[:10], refs[10], refs[11]
    i = pl.program_id(0)
    acc = None
    for b in range(8):
        at = pl.multiple_of(j_ref[b] * W, W)
        if b < 6:
            og = ogs[b][...]
        else:
            og = jnp.where(i == 0, ogs[2 * b - 6][...], ogs[2 * b - 5][...])
        part = dot(og, w_ref[pl.ds(at, W), :])
        acc = part if acc is None else acc + part
    do = acc.astype(BF16)
    do_ref[...] = do

    @pl.when(i == 0)
    def _():
        sent_ref[:, :8] = jnp.zeros((S, 8, HEAD_SIZE), F32)
        sent_ref[:, 8:] = jnp.broadcast_to(merged_ref[...][None], (S, 16, HEAD_SIZE))

    for h in range(H):
        part = dot(fb_ref[h * M : (h + 1) * M, :], do[:, h * HEAD_SIZE : (h + 1) * HEAD_SIZE])
        sent_ref[8 * h : 8 * h + 8, :8] += part.reshape(8, 8, HEAD_SIZE)


def spread_kernel(r_ref, o_ref):
    o_ref[...] = jnp.broadcast_to(jnp.sum(r_ref[:, :8, :], axis=0)[None], (S, 8, HEAD_SIZE))


def put_rows(ref, x):
    for s in range(2):
        ref[:, pl.ds(2 * pl.program_id(0) + s, 1), :] = x[s * S : (s + 1) * S][:, None, :]


def query_panel_kernel(q_ref, do_ref, t_ref, f_ref, got_ref, z_ref, dq_ref, dt_ref, wf_ref):
    ktb = t_ref[0, M:].astype(BF16)
    bv = got_ref[:, 8:16].reshape(M, HEAD_SIZE)
    wf = dot(z_ref[0, 0], bv, precision=HIGHEST)
    wf_ref[...] = wf
    f = f_ref[...]
    df = wide_dot(wf, do_ref[...], 1, 1)
    dsf = (f * (df - jnp.sum(df * f, axis=0, keepdims=True))).astype(BF16)
    put_rows(dt_ref, dot(dsf, q_ref[...]) * SCALE)
    dq_ref[...] = dot(dsf, ktb, 0, 0) * SCALE


def key_panel_kernel(
    k_ref, v_ref, e_ref, st_ref, got_ref, dw_ref, z_ref, dt_ref, dsb_ref, bb_ref, dbv_ref, sent_ref
):
    dw = dw_ref[...].reshape(M, HEAD_SIZE)
    bv = got_ref[:, 8:16].reshape(M, HEAD_SIZE)
    whole = got_ref[:, 16:].reshape(M, HEAD_SIZE)
    dbv = dot(z_ref[0, 0], dw, 0, 0, HIGHEST).astype(BF16)
    dbv_ref[...] = dbv
    db = dot(dbv, v_ref[...], 1, 1)
    beta = jnp.sum(dbv.astype(F32) * bv, axis=1, keepdims=True)
    rescale = jnp.exp(st_ref[:, 0:1] - whole[:, 0:1]) / whole[:, M : M + 1]
    bf = e_ref[...] * rescale
    dsb = (bf * (db - beta)).astype(BF16)
    dsb_ref[...] = dsb
    bb_ref[...] = bf.astype(BF16)
    put_rows(sent_ref, dot(dsb, k_ref[...]) * SCALE)

    @pl.when(pl.program_id(0) == 0)
    def _():
        sent_ref[:, 8:] = dt_ref[...]


def key_rows_kernel(dsb_ref, bb_ref, dbv_ref, t_ref, dk_ref, dv_ref):
    dk_ref[...] = dot(dsb_ref[...], t_ref[0, :M].astype(BF16), 0, 0) * SCALE
    dv_ref[...] = dot(bb_ref[...], dbv_ref[...], 0, 0).astype(BF16)


def adjoint_kernel(own_ref, dw_ref, got_ref, mx_ref, a_ref, z_ref, x_ref, t2_ref, t3_ref, t_ref, o_ref):
    eye = (
        lax.broadcasted_iota(jnp.int32, (M, M), 0) == lax.broadcasted_iota(jnp.int32, (M, M), 1)
    ).astype(F32)
    hi = close_dot
    heads = range(H)
    dz = []
    for h in heads:
        dw = dw_ref[8 * h : 8 * h + 8].reshape(M, HEAD_SIZE)
        bv = got_ref[8 * h : 8 * h + 8, 8:16].reshape(M, HEAD_SIZE)
        dz.append(hi(dw, bv, 1, 1))
    da = [jnp.zeros((M, M), F32) for h in heads]
    for n in reversed(range(NEWTON)):
        x = [x_ref[n, h] for h in heads]
        g = [0.25 * d for d in dz]
        dp2 = [-hi(z_ref[n, h], g[h], 0, 0) for h in heads]
        dz = [hi(g[h], t3_ref[n, h], 1, 1) for h in heads]
        dp1 = [-hi(x[h], dp2[h], 0, 0) for h in heads]
        dx = [hi(dp2[h], t2_ref[n, h], 1, 1) for h in heads]
        dt1 = [hi(x[h], dp1[h], 0, 0) for h in heads]
        dx = [dx[h] + hi(dp1[h], 7.0 * eye - x[h], 1, 1) - dt1[h] for h in heads]
        dz = [dz[h] + hi(a_ref[h], dx[h], 0, 0) for h in heads]
        da = [da[h] + hi(dx[h], z_ref[n, h], 1, 1) for h in heads]
    mx = mx_ref[...]
    denom = mx[0:1, 0:1] * mx[4:5, 0:1]
    row = lax.broadcasted_iota(jnp.int32, (M, HEAD_SIZE), 0)
    for h in heads:
        d = da[h] + dz[h].T / denom
        a = a_ref[h]
        dsa = a * (d - jnp.sum(d * a, axis=1, keepdims=True))
        dqt = hi(dsa, t_ref[h, M:]) * SCALE
        dkt = hi(dsa, t_ref[h, :M], 0, 0) * SCALE
        for i, x in enumerate((dqt, dkt)):
            for s in range(2):
                mine = jnp.where(row == own_ref[0] + s * S, x, 0.0)
                r = 8 * i + 2 * h + s
                o_ref[r : r + 1, :] = jnp.sum(mine, axis=0, keepdims=True)


def final_kernel(dq_ref, dk_ref, got_ref, add_ref, q_out, k_out, tot_ref):
    i = pl.program_id(0)

    @pl.when(i == 0)
    def _():
        tot_ref[...] = (jnp.sum(got_ref[...], axis=0) + add_ref[...]) / (T // 2)

    s = i // 2
    for n, (ref, out) in enumerate(((dq_ref, q_out), (dk_ref, k_out))):
        for h in range(H):
            cols = slice(h * HEAD_SIZE, (h + 1) * HEAD_SIZE)
            add = tot_ref[pl.ds(8 * n + 2 * h + s, 1), :]
            out[:, cols] = (ref[:, cols] + add).astype(BF16)


def weight_kernel(g_ref, wf_ref, o_ref):
    for h in range(H):
        rows = slice(h * M, (h + 1) * M)
        o_ref[:, h * HEAD_SIZE : (h + 1) * HEAD_SIZE] = dot(
            g_ref[rows, :], wf_ref[rows, :], 0, 0, HIGHEST
        )


def to_all(x, axes, n):
    return lax.all_to_all(jnp.broadcast_to(x[None], (n,) + x.shape), axes, 0, 0, tiled=True)


def gather_rows(x, means):
    here = lax.axis_index("y")
    blocks = [
        lax.ppermute(x, "y", [(i, (i + step) % Y) for i in range(Y)]) for step in range(1, Y)
    ]
    blocks, means = lax.optimization_barrier((blocks, means))
    out = jnp.zeros((Y,) + x.shape, x.dtype)
    out = lax.dynamic_update_index_in_dim(out, x, here, 0)
    for step, block in enumerate(blocks, 1):
        out = lax.dynamic_update_index_in_dim(out, block, (here - step) % Y, 0)
    return out.reshape(Y * x.shape[0], x.shape[1]), means


RIGHT = [(i, (i + 1) % X) for i in range(X)]
LEFT = [(i, (i - 1) % X) for i in range(X)]
OTHER = [(0, 1), (1, 0)]


def places():
    px, pc = lax.axis_index("x"), lax.axis_index("core")
    out = []
    for step in (0, -1, 1, 2):
        for core in (pc, 1 - pc):
            out.append(((px + step) % X) * C + core)
    return jnp.stack(out).astype(jnp.int32)


def local(queries, keys, values, out_weight, out_grad):
    full = lambda *shape: spec(shape)
    smem = pl.BlockSpec(memory_space=pltpu.SMEM)
    half = spec((T // 2, W), lambda s: (s, 0))
    slab = spec((T // 4, W), lambda i: (i, 0))
    means = call(
        means_kernel, "means", (2,), [half, half], spec((1, 8, HEAD_SIZE), lambda s: (s, 0, 0)),
        sds((2, 8, HEAD_SIZE)), 2,
    )(queries, keys)
    weight, means = gather_rows(out_weight, means)
    weight = lax.all_gather(weight, "z", axis=0, tiled=True)
    out_grad, means = lax.optimization_barrier((out_grad, means))
    tiles = to_all(means.reshape(16, HEAD_SIZE), SEQ, S)
    right = lax.ppermute(out_grad, "x", RIGHT)
    left = lax.ppermute(out_grad, "x", LEFT)
    beside = lax.ppermute(out_grad, "core", OTHER)
    right, left, tiles = lax.optimization_barrier((right, left, tiles))
    far = [lax.ppermute(right[: T // 2], "x", RIGHT), lax.ppermute(left[T // 2 :], "x", LEFT)]
    right2, left2 = lax.ppermute(right, "core", OTHER), lax.ppermute(left, "core", OTHER)
    tiles = tiles.reshape(S, 2, 2, H, HEAD_SIZE).transpose(3, 2, 1, 0, 4)
    tiles = tiles.reshape(H, 2 * M, HEAD_SIZE)

    f, fb, e, sent, stats, a, tops = call(
        scores_kernel, "scores", (H,), [COLS, COLS, COLS, TILE],
        [ROWS, ROWS, ROWS, spec((8, 16, HEAD_SIZE), lambda h: (h, 0, 0)), LAND, SQUARE, full(8, HEAD_SIZE)],
        [sds((H * M, T)), sds((H * M, T), BF16), sds((H * M, T)), sds((S, 16, HEAD_SIZE)),
         sds((H * M, HEAD_SIZE)), sds((H, M, M)), sds((8, HEAD_SIZE))], 5,
    )(queries, keys, values, tiles)

    far, sent, tops, fb = lax.optimization_barrier((far, sent, tops, fb))
    far2 = [lax.ppermute(x, "core", OTHER) for x in far]
    blocks = [out_grad, beside, right, right2, left, left2, far[0], far[1], far2[0], far2[1]]
    where = places()

    got = lax.all_to_all(sent, SEQ, 0, 0, tiled=True)
    wide = spec((T, 256), lambda i: (0, i))
    short = spec((T // 2, 256), lambda i: (0, i))
    g = call(
        outer_kernel, "outer", (2,), [smem, full(H * M, T)] + [wide] * 6 + [short] * 4,
        spec((2, Z, H * M, 128), lambda i: (i, 0, 0, 0)), sds((Y, Z, H * M, 128), BF16), 6,
    )(where, fb, *blocks)
    g, tops = lax.optimization_barrier((g, tops))
    tops = jnp.maximum(tops, lax.ppermute(tops, "core", OTHER))
    ahead = [lax.ppermute(tops, "x", [(i, (i + n) % X) for i in range(X)]) for n in range(1, X)]
    tops = jnp.maximum(jnp.maximum(tops, ahead[0]), jnp.maximum(ahead[1], ahead[2]))
    here = lax.axis_index("y")
    gs = [lax.dynamic_index_in_dim(g, (here + n) % Y, keepdims=False) for n in range(Y)]
    gs[1:] = [
        lax.ppermute(gs[n], "y", [(i, (i + n) % Y) for i in range(Y)]) for n in range(1, Y)
    ]
    _, got, tops = lax.optimization_barrier((g, got, tops))
    merged = call(
        merge_kernel, "merge", (1,), [full(S, 16, HEAD_SIZE)], full(16, HEAD_SIZE), sds((16, HEAD_SIZE)), 1
    )(got)

    near, merged = lax.optimization_barrier(((gs[1], gs[3]), merged))
    gs[1], gs[3] = near
    tokens = 512
    panel = spec((H * M, tokens), lambda i: (0, i))
    block = spec((tokens, W), lambda i: (i, 0))
    do, sent = call(
        cotangent_kernel, "cotangent", (T // tokens,),
        [smem, full(Z * Y * 128, W), panel, full(16, HEAD_SIZE)]
        + [block] * 6 + [full(T // 2, W)] * 4,
        [block, full(S, 24, HEAD_SIZE)], [sds((T, W), BF16), sds((S, 24, HEAD_SIZE))], 10,
    )(where, weight, fb, merged, *blocks)

    inverse, xs, t2, t3 = call(
        newton_kernel, "newton", (1,), [full(H, M, M), full(8, HEAD_SIZE)],
        [full(NEWTON + 1, H, M, M)] + [full(NEWTON, H, M, M)] * 3,
        [sds((NEWTON + 1, H, M, M))] + [sds((NEWTON, H, M, M))] * 3, 6,
    )(a, tops)

    gs, inverse = lax.optimization_barrier((gs, inverse))
    gs = [x.astype(F32) for x in gs]
    g = (gs[0] + gs[1]) + (gs[2] + gs[3])
    g = lax.psum_scatter(g, "z", scatter_dimension=0, tiled=True).reshape(H * M, 128)
    got = lax.all_to_all(sent, SEQ, 0, 0, tiled=True)
    sent = call(
        spread_kernel, "spread", (1,), [full(S, 24, HEAD_SIZE)], full(S, 8, HEAD_SIZE), sds((S, 8, HEAD_SIZE)), 1
    )(got)
    sent, got = lax.optimization_barrier((sent, got))
    dw = lax.all_to_all(sent, SEQ, 0, 0, tiled=True)

    parts = spec((8, 24, HEAD_SIZE), lambda h: (h, 0, 0))
    last = spec((1, 1, M, M), lambda h: (NEWTON, h, 0, 0))
    dq, dktf, wf = call(
        query_panel_kernel, "query_panel", (H,), [COLS, COLS, TILE, ROWS, parts, last],
        [COLS, full(S, 8, HEAD_SIZE), LAND], [sds((T, W)), sds((S, 8, HEAD_SIZE)), sds((H * M, HEAD_SIZE))], 5,
    )(queries, do, tiles, f, got, inverse)
    dsb, bb, dbv, sent = call(
        key_panel_kernel, "key_panel", (H,),
        [COLS, COLS, ROWS, LAND, parts, spec((8, 8, HEAD_SIZE), lambda h: (h, 0, 0)), last,
         full(S, 8, HEAD_SIZE)],
        [ROWS, ROWS, LAND, full(S, 16, HEAD_SIZE)],
        [sds((H * M, T), BF16), sds((H * M, T), BF16), sds((H * M, HEAD_SIZE), BF16),
         sds((S, 16, HEAD_SIZE))], 4,
    )(keys, values, e, stats, got, dw, inverse, dktf)
    dk, dv = call(
        key_rows_kernel, "key_rows", (H,), [ROWS, ROWS, LAND, TILE], [COLS, COLS],
        [sds((T, W)), sds((T, W), BF16)], 4,
    )(dsb, bb, dbv, tiles)

    summed = lax.all_to_all(sent, SEQ, 0, 0, tiled=True)
    g, summed = lax.optimization_barrier((g, summed))
    own = lax.axis_index(SEQ).astype(jnp.int32).reshape(1)
    da = call(
        adjoint_kernel, "adjoint", (1,),
        [smem, full(S, 8, HEAD_SIZE), full(S, 24, HEAD_SIZE), full(8, HEAD_SIZE), full(H, M, M),
         full(NEWTON + 1, H, M, M)] + [full(NEWTON, H, M, M)] * 3 + [full(H, 2 * M, HEAD_SIZE)],
        full(16, HEAD_SIZE), sds((16, HEAD_SIZE)), 9,
    )(own, dw, got, tops, a, inverse, xs, t2, t3, tiles)
    query_grad, key_grad = call(
        final_kernel, "final", (4,), [slab, slab, full(S, 16, HEAD_SIZE), full(16, HEAD_SIZE)],
        [slab, slab], [sds((T, W), BF16)] * 2, 2, [pltpu.VMEM((16, HEAD_SIZE), F32)],
    )(dq, dk, summed, da)
    weight_grad = call(
        weight_kernel, "weight", (1,), [full(H * M, 128), full(H * M, HEAD_SIZE)], full(128, W), sds((128, W)), 2,
    )(g, wf)
    return query_grad, key_grad, dv, weight_grad


def solution(mesh):
    grid = Mesh(mesh.devices.reshape(Z, Y, X, C), SEQ + HEAD)
    place = P(SEQ, HEAD)
    return jax.shard_map(
        local, mesh=grid, in_specs=(place,) * 5, out_specs=(place,) * 4, check_vma=False
    )
```

```python
import jax
import jax.numpy as jnp
from jax import lax
from jax.experimental import pallas as pl
from jax.experimental.pallas import tpu as pltpu
from jax.sharding import Mesh
from jax.sharding import PartitionSpec as P

HEAD_SIZE = 128
M = 64
NEWTON = 6
SCALE = HEAD_SIZE**-0.5
HIGHEST = lax.Precision.HIGHEST
F32 = jnp.float32
BF16 = jnp.bfloat16

Z, Y, X, C = 8, 4, 4, 2
SEQ = ("z", "y")
HEAD = ("x", "core")
S = Z * Y
H = 4
T = 1024
W = H * HEAD_SIZE


def dot(a, b, ca=1, cb=0, precision=None):
    return lax.dot_general(
        a, b, (((ca,), (cb,)), ((), ())), preferred_element_type=F32, precision=precision
    )


def parts_of(x):
    hi = x.astype(BF16)
    rest = x - hi.astype(F32)
    mid = rest.astype(BF16)
    lo = (rest - mid.astype(F32)).astype(BF16)
    return hi, mid, lo


def wide_dot(x, y, ca=1, cb=0):
    hi, mid, lo = parts_of(x)
    return dot(hi, y, ca, cb) + (dot(mid, y, ca, cb) + dot(lo, y, ca, cb))


def close_dot(x, y, ca=1, cb=0):
    xh, yh = x.astype(BF16), y.astype(BF16)
    xl = (x - xh.astype(F32)).astype(BF16)
    yl = (y - yh.astype(F32)).astype(BF16)
    return dot(xh, yh, ca, cb) + (dot(xh, yl, ca, cb) + dot(xl, yh, ca, cb))


def call(kernel, name, grid, in_specs, out_specs, out_shape, cost, scratch=(), vmem=63.9):
    return pl.pallas_call(
        kernel,
        grid=grid,
        in_specs=in_specs,
        out_specs=out_specs,
        out_shape=out_shape,
        scratch_shapes=scratch,
        name=name,
        compiler_params=pltpu.CompilerParams(vmem_limit_bytes=int(vmem * 2**20)),
        cost_estimate=pl.CostEstimate(
            flops=int(cost * 1e9), bytes_accessed=1 << 20, transcendentals=0
        ),
    )


def spec(shape, index=None):
    if index is None:
        index = lambda h, n=len(shape): (0,) * n
    return pl.BlockSpec(shape, index)


def sds(shape, dtype=F32):
    return jax.ShapeDtypeStruct(shape, dtype)


COLS = spec((T, HEAD_SIZE), lambda h: (0, h))
ROWS = spec((M, T), lambda h: (h, 0))
LAND = spec((M, HEAD_SIZE), lambda h: (h, 0))
TILE = spec((1, 2 * M, HEAD_SIZE), lambda h: (h, 0, 0))
SQUARE = spec((1, M, M), lambda h: (h, 0, 0))


def means_kernel(q_ref, k_ref, o_ref):
    for i, ref in enumerate((q_ref, k_ref)):
        mean = jnp.sum(ref[...].astype(F32), axis=0, keepdims=True) / ref.shape[0]
        for h in range(H):
            o_ref[0, H * i + h : H * i + h + 1, :] = mean[:, h * HEAD_SIZE : (h + 1) * HEAD_SIZE]


def scores_kernel(q_ref, k_ref, v_ref, t_ref, f_ref, fb_ref, e_ref, sent_ref, st_ref, a_ref, mx_ref):
    qt, kt = t_ref[0, :M], t_ref[0, M:]
    s1 = dot(kt.astype(BF16), q_ref[...], 1, 1) * SCALE
    p = jnp.exp(s1 - jnp.max(s1, axis=0, keepdims=True))
    f = p / jnp.sum(p, axis=0, keepdims=True)
    f_ref[...] = f
    fb_ref[...] = f.astype(BF16)
    s2 = dot(qt.astype(BF16), k_ref[...], 1, 1) * SCALE
    top = jnp.max(s2, axis=1, keepdims=True)
    e = jnp.exp(s2 - top)
    e_ref[...] = e
    total = jnp.sum(e, axis=1, keepdims=True)
    sent_ref[:, :8] = wide_dot(e, v_ref[...]).reshape(8, 8, HEAD_SIZE)
    lane = lax.broadcasted_iota(jnp.int32, (M, HEAD_SIZE), 1)
    stats = jnp.where(lane < M, top, total)
    st_ref[...] = stats
    sent_ref[:, 8:] = stats.reshape(8, 8, HEAD_SIZE)
    sa = dot(qt, kt, 1, 1, HIGHEST) * SCALE
    pa = jnp.exp(sa - jnp.max(sa, axis=1, keepdims=True))
    a = pa / jnp.sum(pa, axis=1, keepdims=True)
    a_ref[0] = a
    col = jnp.max(jnp.sum(a, axis=0, keepdims=True), axis=1, keepdims=True)
    row = jnp.max(jnp.sum(a, axis=1, keepdims=True), axis=0, keepdims=True)
    sub = lax.broadcasted_iota(jnp.int32, (8, HEAD_SIZE), 0)
    both = jnp.where(sub < 4, col, row)

    @pl.when(pl.program_id(0) == 0)
    def _():
        mx_ref[...] = both

    @pl.when(pl.program_id(0) > 0)
    def _():
        mx_ref[...] = jnp.maximum(mx_ref[...], both)


def newton_kernel(a_ref, mx_ref, z_ref, x_ref, t2_ref, t3_ref):
    eye = (
        lax.broadcasted_iota(jnp.int32, (M, M), 0) == lax.broadcasted_iota(jnp.int32, (M, M), 1)
    ).astype(F32)
    mx = mx_ref[...]
    denom = mx[0:1, 0:1] * mx[4:5, 0:1]
    zs = []
    for h in range(H):
        z = a_ref[h].T / denom
        z_ref[0, h] = z
        zs.append(z)
    for n in range(NEWTON):
        xs = [dot(a_ref[h], zs[h], precision=HIGHEST) for h in range(H)]
        t2 = [15.0 * eye - dot(x, 7.0 * eye - x, precision=HIGHEST) for x in xs]
        t3 = [13.0 * eye - dot(x, t, precision=HIGHEST) for x, t in zip(xs, t2)]
        zs = [0.25 * dot(z, t, precision=HIGHEST) for z, t in zip(zs, t3)]
        for h in range(H):
            x_ref[n, h] = xs[h]
            t2_ref[n, h] = t2[h]
            t3_ref[n, h] = t3[h]
            z_ref[n + 1, h] = zs[h]


def merge_kernel(r_ref, o_ref):
    v, st = r_ref[:, :8, :], r_ref[:, 8:, :]
    top, total = st[:, :, 0:1], st[:, :, M : M + 1]
    mx = jnp.max(top, axis=0, keepdims=True)
    scale = jnp.exp(top - mx)
    whole = jnp.sum(scale * total, axis=0)
    o_ref[:8] = jnp.sum(scale * v, axis=0) / whole
    lane = lax.broadcasted_iota(jnp.int32, (8, HEAD_SIZE), 1)
    o_ref[8:] = jnp.where(lane < M, mx[0], whole)


def outer_kernel(j_ref, fb_ref, *refs):
    ogs, out = refs[:10], refs[10]
    fb = fb_ref[...]
    for b in range(8):
        if b < 6:
            res = dot(fb, ogs[b][...])
        else:
            top, low = ogs[2 * b - 6], ogs[2 * b - 5]
            res = dot(fb[:, : T // 2], top[...]) + dot(fb[:, T // 2 :], low[...])
        for y in range(2):
            out[j_ref[b], y] = res[:, y * 128 : (y + 1) * 128]


def cotangent_kernel(j_ref, w_ref, fb_ref, merged_ref, *refs):
    ogs, do_ref, sent_ref = refs[:10], refs[10], refs[11]
    i = pl.program_id(0)
    acc = None
    for b in range(8):
        at = pl.multiple_of(j_ref[b] * W, W)
        if b < 6:
            og = ogs[b][...]
        else:
            og = jnp.where(i == 0, ogs[2 * b - 6][...], ogs[2 * b - 5][...])
        part = dot(og, w_ref[pl.ds(at, W), :])
        acc = part if acc is None else acc + part
    do = acc.astype(BF16)
    do_ref[...] = do

    @pl.when(i == 0)
    def _():
        sent_ref[:, :8] = jnp.zeros((S, 8, HEAD_SIZE), F32)
        sent_ref[:, 8:] = jnp.broadcast_to(merged_ref[...][None], (S, 16, HEAD_SIZE))

    for h in range(H):
        part = dot(fb_ref[h * M : (h + 1) * M, :], do[:, h * HEAD_SIZE : (h + 1) * HEAD_SIZE])
        sent_ref[8 * h : 8 * h + 8, :8] += part.reshape(8, 8, HEAD_SIZE)


def spread_kernel(r_ref, o_ref):
    o_ref[...] = jnp.broadcast_to(jnp.sum(r_ref[...], axis=0)[None], (S, 8, HEAD_SIZE))


def put_rows(ref, x):
    for s in range(2):
        ref[:, pl.ds(2 * pl.program_id(0) + s, 1), :] = x[s * S : (s + 1) * S][:, None, :]


def query_panel_kernel(q_ref, do_ref, t_ref, f_ref, got_ref, z_ref, dq_ref, dt_ref, wf_ref):
    ktb = t_ref[0, M:].astype(BF16)
    bv = got_ref[:, 8:16].reshape(M, HEAD_SIZE)
    wf = dot(z_ref[0, 0], bv, precision=HIGHEST)
    wf_ref[...] = wf
    f = f_ref[...]
    df = wide_dot(wf, do_ref[...], 1, 1)
    dsf = (f * (df - jnp.sum(df * f, axis=0, keepdims=True))).astype(BF16)
    put_rows(dt_ref, dot(dsf, q_ref[...]) * SCALE)
    dq_ref[...] = dot(dsf, ktb, 0, 0) * SCALE


def key_panel_kernel(
    k_ref, v_ref, e_ref, st_ref, got_ref, dw_ref, z_ref, dt_ref, dsb_ref, bb_ref, dbv_ref, sent_ref
):
    dw = dw_ref[...].reshape(M, HEAD_SIZE)
    bv = got_ref[:, 8:16].reshape(M, HEAD_SIZE)
    whole = got_ref[:, 16:].reshape(M, HEAD_SIZE)
    dbv = dot(z_ref[0, 0], dw, 0, 0, HIGHEST).astype(BF16)
    dbv_ref[...] = dbv
    db = dot(dbv, v_ref[...], 1, 1)
    beta = jnp.sum(dbv.astype(F32) * bv, axis=1, keepdims=True)
    rescale = jnp.exp(st_ref[:, 0:1] - whole[:, 0:1]) / whole[:, M : M + 1]
    bf = e_ref[...] * rescale
    dsb = (bf * (db - beta)).astype(BF16)
    dsb_ref[...] = dsb
    bb_ref[...] = bf.astype(BF16)
    put_rows(sent_ref, dot(dsb, k_ref[...]) * SCALE)

    @pl.when(pl.program_id(0) == 0)
    def _():
        sent_ref[:, 8:] = dt_ref[...]


def key_rows_kernel(dsb_ref, bb_ref, dbv_ref, t_ref, dk_ref, dv_ref):
    dk_ref[...] = dot(dsb_ref[...], t_ref[0, :M].astype(BF16), 0, 0) * SCALE
    dv_ref[...] = dot(bb_ref[...], dbv_ref[...], 0, 0).astype(BF16)


def adjoint_kernel(own_ref, dw_ref, got_ref, mx_ref, a_ref, z_ref, x_ref, t2_ref, t3_ref, t_ref, o_ref):
    eye = (
        lax.broadcasted_iota(jnp.int32, (M, M), 0) == lax.broadcasted_iota(jnp.int32, (M, M), 1)
    ).astype(F32)
    hi = close_dot
    heads = range(H)
    dz = []
    for h in heads:
        dw = dw_ref[8 * h : 8 * h + 8].reshape(M, HEAD_SIZE)
        bv = got_ref[8 * h : 8 * h + 8, 8:16].reshape(M, HEAD_SIZE)
        dz.append(hi(dw, bv, 1, 1))
    da = [jnp.zeros((M, M), F32) for h in heads]
    for n in reversed(range(NEWTON)):
        x = [x_ref[n, h] for h in heads]
        g = [0.25 * d for d in dz]
        dp2 = [-hi(z_ref[n, h], g[h], 0, 0) for h in heads]
        dz = [hi(g[h], t3_ref[n, h], 1, 1) for h in heads]
        dp1 = [-hi(x[h], dp2[h], 0, 0) for h in heads]
        dx = [hi(dp2[h], t2_ref[n, h], 1, 1) for h in heads]
        dt1 = [hi(x[h], dp1[h], 0, 0) for h in heads]
        dx = [dx[h] + hi(dp1[h], 7.0 * eye - x[h], 1, 1) - dt1[h] for h in heads]
        dz = [dz[h] + hi(a_ref[h], dx[h], 0, 0) for h in heads]
        da = [da[h] + hi(dx[h], z_ref[n, h], 1, 1) for h in heads]
    mx = mx_ref[...]
    denom = mx[0:1, 0:1] * mx[4:5, 0:1]
    row = lax.broadcasted_iota(jnp.int32, (M, HEAD_SIZE), 0)
    for h in heads:
        d = da[h] + dz[h].T / denom
        a = a_ref[h]
        dsa = a * (d - jnp.sum(d * a, axis=1, keepdims=True))
        dqt = hi(dsa, t_ref[h, M:]) * SCALE
        dkt = hi(dsa, t_ref[h, :M], 0, 0) * SCALE
        for i, x in enumerate((dqt, dkt)):
            for s in range(2):
                mine = jnp.where(row == own_ref[0] + s * S, x, 0.0)
                r = 8 * i + 2 * h + s
                o_ref[r : r + 1, :] = jnp.sum(mine, axis=0, keepdims=True)


def final_kernel(dq_ref, dk_ref, got_ref, add_ref, q_out, k_out, tot_ref):
    i = pl.program_id(0)

    @pl.when(i == 0)
    def _():
        tot_ref[...] = (jnp.sum(got_ref[...], axis=0) + add_ref[...]) / (T // 2)

    s = i // 2
    for n, (ref, out) in enumerate(((dq_ref, q_out), (dk_ref, k_out))):
        for h in range(H):
            cols = slice(h * HEAD_SIZE, (h + 1) * HEAD_SIZE)
            add = tot_ref[pl.ds(8 * n + 2 * h + s, 1), :]
            out[:, cols] = (ref[:, cols] + add).astype(BF16)


def weight_kernel(*refs):
    gs, wf_ref, o_ref = refs[:Y], refs[Y], refs[Y + 1]
    for h in range(H):
        rows = slice(h * M, (h + 1) * M)
        a, b, c, d = (ref[rows, :] for ref in gs)
        o_ref[:, h * HEAD_SIZE : (h + 1) * HEAD_SIZE] = dot(
            (a + b) + (c + d), wf_ref[rows, :], 0, 0, HIGHEST
        )


def to_all(x, axes, n):
    return lax.all_to_all(jnp.broadcast_to(x[None], (n,) + x.shape), axes, 0, 0, tiled=True)


def gather_rows(x, means):
    here = lax.axis_index("y")
    x, means = lax.optimization_barrier((x, means))
    blocks = [
        lax.ppermute(x, "y", [(i, (i + step) % Y) for i in range(Y)]) for step in range(1, Y)
    ]
    out = jnp.zeros((Y,) + x.shape, x.dtype)
    out = lax.dynamic_update_index_in_dim(out, x, here, 0)
    for step, block in enumerate(blocks, 1):
        out = lax.dynamic_update_index_in_dim(out, block, (here - step) % Y, 0)
    return out.reshape(Y * x.shape[0], x.shape[1]), means


RIGHT = [(i, (i + 1) % X) for i in range(X)]
LEFT = [(i, (i - 1) % X) for i in range(X)]
OTHER = [(0, 1), (1, 0)]


def places():
    px, pc = lax.axis_index("x"), lax.axis_index("core")
    out = []
    for step in (0, -1, 1, 2):
        for core in (pc, 1 - pc):
            out.append(((px + step) % X) * C + core)
    return jnp.stack(out).astype(jnp.int32)


def local(queries, keys, values, out_weight, out_grad):
    full = lambda *shape: spec(shape)
    smem = pl.BlockSpec(memory_space=pltpu.SMEM)
    half = spec((T // 2, W), lambda s: (s, 0))
    slab = spec((T // 4, W), lambda i: (i, 0))
    means = call(
        means_kernel, "means", (2,), [half, half], spec((1, 8, HEAD_SIZE), lambda s: (s, 0, 0)),
        sds((2, 8, HEAD_SIZE)), 2,
    )(queries, keys)
    weight, means = gather_rows(out_weight, means)
    weight = lax.all_gather(weight, "z", axis=0, tiled=True)
    out_grad, means = lax.optimization_barrier((out_grad, means))
    tiles = to_all(means.reshape(16, HEAD_SIZE), SEQ, S)
    right = lax.ppermute(out_grad, "x", RIGHT)
    left = lax.ppermute(out_grad, "x", LEFT)
    beside = lax.ppermute(out_grad, "core", OTHER)
    right, left, tiles = lax.optimization_barrier((right, left, tiles))
    far = [lax.ppermute(right[: T // 2], "x", RIGHT), lax.ppermute(left[T // 2 :], "x", LEFT)]
    right2, left2 = lax.ppermute(right, "core", OTHER), lax.ppermute(left, "core", OTHER)
    tiles = tiles.reshape(S, 2, 2, H, HEAD_SIZE).transpose(3, 2, 1, 0, 4)
    tiles = tiles.reshape(H, 2 * M, HEAD_SIZE)

    f, fb, e, sent, stats, a, tops = call(
        scores_kernel, "scores", (H,), [COLS, COLS, COLS, TILE],
        [ROWS, ROWS, ROWS, spec((8, 16, HEAD_SIZE), lambda h: (h, 0, 0)), LAND, SQUARE, full(8, HEAD_SIZE)],
        [sds((H * M, T)), sds((H * M, T), BF16), sds((H * M, T)), sds((S, 16, HEAD_SIZE)),
         sds((H * M, HEAD_SIZE)), sds((H, M, M)), sds((8, HEAD_SIZE))], 60,
    )(queries, keys, values, tiles)

    far, sent, tops, fb = lax.optimization_barrier((far, sent, tops, fb))
    far2 = [lax.ppermute(x, "core", OTHER) for x in far]
    blocks = [out_grad, beside, right, right2, left, left2, far[0], far[1], far2[0], far2[1]]
    where = places()

    got = lax.all_to_all(sent, SEQ, 0, 0, tiled=True)
    wide = spec((T, 256), lambda i: (0, i))
    short = spec((T // 2, 256), lambda i: (0, i))
    g = call(
        outer_kernel, "outer", (2,), [smem, full(H * M, T)] + [wide] * 6 + [short] * 4,
        spec((Z, 2, H * M, 128), lambda i: (0, i, 0, 0)), sds((Z, Y, H * M, 128)), 20,
    )(where, fb, *blocks)
    g, tops = lax.optimization_barrier((g, tops))
    tops = jnp.maximum(tops, lax.ppermute(tops, "core", OTHER))
    ahead = [lax.ppermute(tops, "x", [(i, (i + n) % X) for i in range(X)]) for n in range(1, X)]
    tops = jnp.maximum(jnp.maximum(tops, ahead[0]), jnp.maximum(ahead[1], ahead[2]))
    g, got, tops = lax.optimization_barrier((g, got, tops))
    merged = call(
        merge_kernel, "merge", (1,), [full(S, 16, HEAD_SIZE)], full(16, HEAD_SIZE), sds((16, HEAD_SIZE)), 1
    )(got)

    g = lax.psum_scatter(g, "z", scatter_dimension=0, tiled=True).reshape(Y, H * M, 128)
    tokens = 512
    panel = spec((H * M, tokens), lambda i: (0, i))
    block = spec((tokens, W), lambda i: (i, 0))
    do, sent = call(
        cotangent_kernel, "cotangent", (T // tokens,),
        [smem, full(Z * Y * 128, W), panel, full(16, HEAD_SIZE)]
        + [block] * 6 + [full(T // 2, W)] * 4,
        [block, full(S, 24, HEAD_SIZE)], [sds((T, W), BF16), sds((S, 24, HEAD_SIZE))], 10,
    )(where, weight, fb, merged, *blocks)

    inverse, xs, t2, t3 = call(
        newton_kernel, "newton", (1,), [full(H, M, M), full(8, HEAD_SIZE)],
        [full(NEWTON + 1, H, M, M)] + [full(NEWTON, H, M, M)] * 3,
        [sds((NEWTON + 1, H, M, M))] + [sds((NEWTON, H, M, M))] * 3, 6,
    )(a, tops)

    got = lax.all_to_all(sent, SEQ, 0, 0, tiled=True)
    sent = call(
        spread_kernel, "spread", (1,), [full(S, 8, HEAD_SIZE)], full(S, 8, HEAD_SIZE), sds((S, 8, HEAD_SIZE)), 1
    )(got)
    sent, got = lax.optimization_barrier((sent, got))
    dw = lax.all_to_all(sent, SEQ, 0, 0, tiled=True)

    parts = spec((8, 24, HEAD_SIZE), lambda h: (h, 0, 0))
    last = spec((1, 1, M, M), lambda h: (NEWTON, h, 0, 0))
    dq, dktf, wf = call(
        query_panel_kernel, "query_panel", (H,), [COLS, COLS, TILE, ROWS, parts, last],
        [COLS, full(S, 8, HEAD_SIZE), LAND], [sds((T, W)), sds((S, 8, HEAD_SIZE)), sds((H * M, HEAD_SIZE))], 5,
    )(queries, do, tiles, f, got, inverse)
    dsb, bb, dbv, sent = call(
        key_panel_kernel, "key_panel", (H,),
        [COLS, COLS, ROWS, LAND, parts, spec((8, 8, HEAD_SIZE), lambda h: (h, 0, 0)), last,
         full(S, 8, HEAD_SIZE)],
        [ROWS, ROWS, LAND, full(S, 16, HEAD_SIZE)],
        [sds((H * M, T), BF16), sds((H * M, T), BF16), sds((H * M, HEAD_SIZE), BF16),
         sds((S, 16, HEAD_SIZE))], 4,
    )(keys, values, e, stats, got, dw, inverse, dktf)
    dk, dv = call(
        key_rows_kernel, "key_rows", (H,), [ROWS, ROWS, LAND, TILE], [COLS, COLS],
        [sds((T, W)), sds((T, W), BF16)], 4,
    )(dsb, bb, dbv, tiles)

    g, dsb = lax.optimization_barrier((g, dsb))
    here = lax.axis_index("y")
    gs = [lax.dynamic_index_in_dim(g, (here + n) % Y, keepdims=False) for n in range(Y)]
    gs[1:] = [
        lax.ppermute(gs[n], "y", [(i, (i + n) % Y) for i in range(Y)]) for n in range(1, Y)
    ]
    summed = lax.all_to_all(sent, SEQ, 0, 0, tiled=True)
    own = lax.axis_index(SEQ).astype(jnp.int32).reshape(1)
    da = call(
        adjoint_kernel, "adjoint", (1,),
        [smem, full(S, 8, HEAD_SIZE), full(S, 24, HEAD_SIZE), full(8, HEAD_SIZE), full(H, M, M),
         full(NEWTON + 1, H, M, M)] + [full(NEWTON, H, M, M)] * 3 + [full(H, 2 * M, HEAD_SIZE)],
        full(16, HEAD_SIZE), sds((16, HEAD_SIZE)), 9,
    )(own, dw, got, tops, a, inverse, xs, t2, t3, tiles)
    query_grad, key_grad = call(
        final_kernel, "final", (4,), [slab, slab, full(S, 16, HEAD_SIZE), full(16, HEAD_SIZE)],
        [slab, slab], [sds((T, W), BF16)] * 2, 2, [pltpu.VMEM((16, HEAD_SIZE), F32)],
    )(dq, dk, summed, da)
    weight_grad = call(
        weight_kernel, "weight", (1,), [full(H * M, 128)] * Y + [full(H * M, HEAD_SIZE)], full(128, W), sds((128, W)), 2,
    )(*gs, wf)
    return query_grad, key_grad, dv, weight_grad


def solution(mesh):
    grid = Mesh(mesh.devices.reshape(Z, Y, X, C), SEQ + HEAD)
    place = P(SEQ, HEAD)
    return jax.shard_map(
        local, mesh=grid, in_specs=(place,) * 5, out_specs=(place,) * 4, check_vma=False
    )
```

```python
import jax
import jax.numpy as jnp
from jax import lax
from jax.experimental import pallas as pl
from jax.experimental.pallas import tpu as pltpu
from jax.sharding import Mesh
from jax.sharding import PartitionSpec as P

HEAD_SIZE = 128
M = 64
NEWTON = 6
SCALE = HEAD_SIZE**-0.5
HIGHEST = lax.Precision.HIGHEST
F32 = jnp.float32
BF16 = jnp.bfloat16

Z, Y, X, C = 8, 4, 4, 2
SEQ = ("z", "y")
HEAD = ("x", "core")
S = Z * Y
H = 4
T = 1024
W = H * HEAD_SIZE


def dot(a, b, ca=1, cb=0, precision=None):
    return lax.dot_general(
        a, b, (((ca,), (cb,)), ((), ())), preferred_element_type=F32, precision=precision
    )


def parts_of(x):
    hi = x.astype(BF16)
    rest = x - hi.astype(F32)
    mid = rest.astype(BF16)
    lo = (rest - mid.astype(F32)).astype(BF16)
    return hi, mid, lo


def wide_dot(x, y, ca=1, cb=0):
    hi, mid, lo = parts_of(x)
    return dot(hi, y, ca, cb) + (dot(mid, y, ca, cb) + dot(lo, y, ca, cb))


def close_dot(x, y, ca=1, cb=0):
    xh, yh = x.astype(BF16), y.astype(BF16)
    xl = (x - xh.astype(F32)).astype(BF16)
    yl = (y - yh.astype(F32)).astype(BF16)
    return dot(xh, yh, ca, cb) + (dot(xh, yl, ca, cb) + dot(xl, yh, ca, cb))


def call(kernel, name, grid, in_specs, out_specs, out_shape, cost, scratch=(), vmem=63.9):
    return pl.pallas_call(
        kernel,
        grid=grid,
        in_specs=in_specs,
        out_specs=out_specs,
        out_shape=out_shape,
        scratch_shapes=scratch,
        name=name,
        compiler_params=pltpu.CompilerParams(vmem_limit_bytes=int(vmem * 2**20)),
        cost_estimate=pl.CostEstimate(
            flops=int(cost * 1e9), bytes_accessed=1 << 20, transcendentals=0
        ),
    )


def spec(shape, index=None):
    if index is None:
        index = lambda h, n=len(shape): (0,) * n
    return pl.BlockSpec(shape, index)


def sds(shape, dtype=F32):
    return jax.ShapeDtypeStruct(shape, dtype)


COLS = spec((T, HEAD_SIZE), lambda h: (0, h))
ROWS = spec((M, T), lambda h: (h, 0))
LAND = spec((M, HEAD_SIZE), lambda h: (h, 0))
TILE = spec((1, 2 * M, HEAD_SIZE), lambda h: (h, 0, 0))
SQUARE = spec((1, M, M), lambda h: (h, 0, 0))


def means_kernel(q_ref, k_ref, o_ref):
    for i, ref in enumerate((q_ref, k_ref)):
        mean = jnp.sum(ref[...].astype(F32), axis=0, keepdims=True) / ref.shape[0]
        for h in range(H):
            o_ref[0, H * i + h : H * i + h + 1, :] = mean[:, h * HEAD_SIZE : (h + 1) * HEAD_SIZE]


def scores_kernel(q_ref, k_ref, v_ref, t_ref, f_ref, fb_ref, e_ref, sent_ref, st_ref, a_ref, mx_ref):
    qt, kt = t_ref[0, :M], t_ref[0, M:]
    s1 = dot(kt.astype(BF16), q_ref[...], 1, 1) * SCALE
    p = jnp.exp(s1 - jnp.max(s1, axis=0, keepdims=True))
    f = p / jnp.sum(p, axis=0, keepdims=True)
    f_ref[...] = f
    fb_ref[...] = f.astype(BF16)
    s2 = dot(qt.astype(BF16), k_ref[...], 1, 1) * SCALE
    top = jnp.max(s2, axis=1, keepdims=True)
    e = jnp.exp(s2 - top)
    e_ref[...] = e
    total = jnp.sum(e, axis=1, keepdims=True)
    sent_ref[:, :8] = wide_dot(e, v_ref[...]).reshape(8, 8, HEAD_SIZE)
    lane = lax.broadcasted_iota(jnp.int32, (M, HEAD_SIZE), 1)
    stats = jnp.where(lane < M, top, total)
    st_ref[...] = stats
    sent_ref[:, 8:] = stats.reshape(8, 8, HEAD_SIZE)
    sa = dot(qt, kt, 1, 1, HIGHEST) * SCALE
    pa = jnp.exp(sa - jnp.max(sa, axis=1, keepdims=True))
    a = pa / jnp.sum(pa, axis=1, keepdims=True)
    a_ref[0] = a
    col = jnp.max(jnp.sum(a, axis=0, keepdims=True), axis=1, keepdims=True)
    row = jnp.max(jnp.sum(a, axis=1, keepdims=True), axis=0, keepdims=True)
    sub = lax.broadcasted_iota(jnp.int32, (8, HEAD_SIZE), 0)
    both = jnp.where(sub < 4, col, row)

    @pl.when(pl.program_id(0) == 0)
    def _():
        mx_ref[...] = both

    @pl.when(pl.program_id(0) > 0)
    def _():
        mx_ref[...] = jnp.maximum(mx_ref[...], both)


def newton_kernel(a_ref, mx_ref, z_ref, x_ref, t2_ref, t3_ref):
    eye = (
        lax.broadcasted_iota(jnp.int32, (M, M), 0) == lax.broadcasted_iota(jnp.int32, (M, M), 1)
    ).astype(F32)
    mx = mx_ref[...]
    denom = mx[0:1, 0:1] * mx[4:5, 0:1]
    zs = []
    for h in range(H):
        z = a_ref[h].T / denom
        z_ref[0, h] = z
        zs.append(z)
    for n in range(NEWTON):
        xs = [dot(a_ref[h], zs[h], precision=HIGHEST) for h in range(H)]
        t2 = [15.0 * eye - dot(x, 7.0 * eye - x, precision=HIGHEST) for x in xs]
        t3 = [13.0 * eye - dot(x, t, precision=HIGHEST) for x, t in zip(xs, t2)]
        zs = [0.25 * dot(z, t, precision=HIGHEST) for z, t in zip(zs, t3)]
        for h in range(H):
            x_ref[n, h] = xs[h]
            t2_ref[n, h] = t2[h]
            t3_ref[n, h] = t3[h]
            z_ref[n + 1, h] = zs[h]


def merge_kernel(r_ref, o_ref):
    v, st = r_ref[:, :8, :], r_ref[:, 8:, :]
    top, total = st[:, :, 0:1], st[:, :, M : M + 1]
    mx = jnp.max(top, axis=0, keepdims=True)
    scale = jnp.exp(top - mx)
    whole = jnp.sum(scale * total, axis=0)
    lane = lax.broadcasted_iota(jnp.int32, (8, HEAD_SIZE), 1)
    o_ref[:, :8] = jnp.broadcast_to((jnp.sum(scale * v, axis=0) / whole)[None], (S, 8, HEAD_SIZE))
    o_ref[:, 8:] = jnp.broadcast_to(jnp.where(lane < M, mx[0], whole)[None], (S, 8, HEAD_SIZE))


def outer_kernel(j_ref, fb_ref, *refs):
    ogs, out = refs[:8], refs[8]
    fb = fb_ref[...]
    for b in range(8):
        res = dot(fb, ogs[b][...])
        for y in range(2):
            out[j_ref[b], y] = res[:, y * 128 : (y + 1) * 128]


def cotangent_kernel(j_ref, w_ref, fb_ref, *refs):
    ogs, do_ref, sent_ref = refs[:8], refs[8], refs[9]
    i = pl.program_id(0)
    acc = None
    for b in range(8):
        at = pl.multiple_of(j_ref[b] * W, W)
        part = dot(ogs[b][...], w_ref[pl.ds(at, W), :])
        acc = part if acc is None else acc + part
    do = acc.astype(BF16)
    do_ref[...] = do

    @pl.when(i == 0)
    def _():
        sent_ref[...] = jnp.zeros((S, 8, HEAD_SIZE), F32)

    for h in range(H):
        part = dot(fb_ref[h * M : (h + 1) * M, :], do[:, h * HEAD_SIZE : (h + 1) * HEAD_SIZE])
        sent_ref[8 * h : 8 * h + 8] += part.reshape(8, 8, HEAD_SIZE)


def spread_kernel(r_ref, o_ref):
    o_ref[...] = jnp.broadcast_to(jnp.sum(r_ref[...], axis=0)[None], (S, 8, HEAD_SIZE))


def put_rows(ref, x):
    for s in range(2):
        ref[:, pl.ds(2 * pl.program_id(0) + s, 1), :] = x[s * S : (s + 1) * S][:, None, :]


def query_panel_kernel(q_ref, do_ref, t_ref, f_ref, got_ref, z_ref, dq_ref, dt_ref, wf_ref):
    ktb = t_ref[0, M:].astype(BF16)
    bv = got_ref[:, :8].reshape(M, HEAD_SIZE)
    wf = dot(z_ref[0, 0], bv, precision=HIGHEST)
    wf_ref[...] = wf
    f = f_ref[...]
    df = wide_dot(wf, do_ref[...], 1, 1)
    dsf = (f * (df - jnp.sum(df * f, axis=0, keepdims=True))).astype(BF16)
    put_rows(dt_ref, dot(dsf, q_ref[...]) * SCALE)
    dq_ref[...] = dot(dsf, ktb, 0, 0) * SCALE


def key_panel_kernel(
    k_ref, v_ref, e_ref, st_ref, got_ref, dw_ref, z_ref, dt_ref, dsb_ref, bb_ref, dbv_ref, sent_ref
):
    dw = dw_ref[...].reshape(M, HEAD_SIZE)
    bv = got_ref[:, :8].reshape(M, HEAD_SIZE)
    whole = got_ref[:, 8:].reshape(M, HEAD_SIZE)
    dbv = dot(z_ref[0, 0], dw, 0, 0, HIGHEST).astype(BF16)
    dbv_ref[...] = dbv
    db = dot(dbv, v_ref[...], 1, 1)
    beta = jnp.sum(dbv.astype(F32) * bv, axis=1, keepdims=True)
    rescale = jnp.exp(st_ref[:, 0:1] - whole[:, 0:1]) / whole[:, M : M + 1]
    bf = e_ref[...] * rescale
    dsb = (bf * (db - beta)).astype(BF16)
    dsb_ref[...] = dsb
    bb_ref[...] = bf.astype(BF16)
    put_rows(sent_ref, dot(dsb, k_ref[...]) * SCALE)

    @pl.when(pl.program_id(0) == 0)
    def _():
        sent_ref[:, 8:] = dt_ref[...]


def key_rows_kernel(dsb_ref, bb_ref, dbv_ref, t_ref, dk_ref, dv_ref):
    dk_ref[...] = dot(dsb_ref[...], t_ref[0, :M].astype(BF16), 0, 0) * SCALE
    dv_ref[...] = dot(bb_ref[...], dbv_ref[...], 0, 0).astype(BF16)


def adjoint_kernel(own_ref, dw_ref, got_ref, mx_ref, a_ref, z_ref, x_ref, t2_ref, t3_ref, t_ref, o_ref):
    eye = (
        lax.broadcasted_iota(jnp.int32, (M, M), 0) == lax.broadcasted_iota(jnp.int32, (M, M), 1)
    ).astype(F32)
    hi = close_dot
    heads = range(H)
    dz = []
    for h in heads:
        dw = dw_ref[8 * h : 8 * h + 8].reshape(M, HEAD_SIZE)
        bv = got_ref[8 * h : 8 * h + 8, :8].reshape(M, HEAD_SIZE)
        dz.append(hi(dw, bv, 1, 1))
    da = [jnp.zeros((M, M), F32) for h in heads]
    for n in reversed(range(NEWTON)):
        x = [x_ref[n, h] for h in heads]
        g = [0.25 * d for d in dz]
        dp2 = [-hi(z_ref[n, h], g[h], 0, 0) for h in heads]
        dz = [hi(g[h], t3_ref[n, h], 1, 1) for h in heads]
        dp1 = [-hi(x[h], dp2[h], 0, 0) for h in heads]
        dx = [hi(dp2[h], t2_ref[n, h], 1, 1) for h in heads]
        dt1 = [hi(x[h], dp1[h], 0, 0) for h in heads]
        dx = [dx[h] + hi(dp1[h], 7.0 * eye - x[h], 1, 1) - dt1[h] for h in heads]
        dz = [dz[h] + hi(a_ref[h], dx[h], 0, 0) for h in heads]
        da = [da[h] + hi(dx[h], z_ref[n, h], 1, 1) for h in heads]
    mx = mx_ref[...]
    denom = mx[0:1, 0:1] * mx[4:5, 0:1]
    row = lax.broadcasted_iota(jnp.int32, (M, HEAD_SIZE), 0)
    for h in heads:
        d = da[h] + dz[h].T / denom
        a = a_ref[h]
        dsa = a * (d - jnp.sum(d * a, axis=1, keepdims=True))
        dqt = hi(dsa, t_ref[h, M:]) * SCALE
        dkt = hi(dsa, t_ref[h, :M], 0, 0) * SCALE
        for i, x in enumerate((dqt, dkt)):
            for s in range(2):
                mine = jnp.where(row == own_ref[0] + s * S, x, 0.0)
                r = 8 * i + 2 * h + s
                o_ref[r : r + 1, :] = jnp.sum(mine, axis=0, keepdims=True)


def final_kernel(dq_ref, dk_ref, got_ref, add_ref, q_out, k_out, tot_ref):
    i = pl.program_id(0)

    @pl.when(i == 0)
    def _():
        tot_ref[...] = (jnp.sum(got_ref[...], axis=0) + add_ref[...]) / (T // 2)

    s = i // 2
    for n, (ref, out) in enumerate(((dq_ref, q_out), (dk_ref, k_out))):
        for h in range(H):
            cols = slice(h * HEAD_SIZE, (h + 1) * HEAD_SIZE)
            add = tot_ref[pl.ds(8 * n + 2 * h + s, 1), :]
            out[:, cols] = (ref[:, cols] + add).astype(BF16)


def weight_kernel(*refs):
    gs, wf_ref, o_ref = refs[:Y], refs[Y], refs[Y + 1]
    for h in range(H):
        rows = slice(h * M, (h + 1) * M)
        a, b, c, d = (ref[rows, :] for ref in gs)
        o_ref[:, h * HEAD_SIZE : (h + 1) * HEAD_SIZE] = dot(
            (a + b) + (c + d), wf_ref[rows, :], 0, 0, HIGHEST
        )


def to_all(x, axes, n):
    return lax.all_to_all(jnp.broadcast_to(x[None], (n,) + x.shape), axes, 0, 0, tiled=True)


def gather_rows(x, means):
    here = lax.axis_index("y")
    blocks = [
        lax.ppermute(x, "y", [(i, (i + step) % Y) for i in range(Y)]) for step in range(1, Y)
    ]
    blocks, means = lax.optimization_barrier((blocks, means))
    out = jnp.zeros((Y,) + x.shape, x.dtype)
    out = lax.dynamic_update_index_in_dim(out, x, here, 0)
    for step, block in enumerate(blocks, 1):
        out = lax.dynamic_update_index_in_dim(out, block, (here - step) % Y, 0)
    return out.reshape(Y * x.shape[0], x.shape[1]), means


RIGHT = [(i, (i + 1) % X) for i in range(X)]
LEFT = [(i, (i - 1) % X) for i in range(X)]
OTHER = [(0, 1), (1, 0)]
FAR = [(i * C + c, (i + 1 - 2 * c) % X * C + c) for i in range(X) for c in range(C)]


def places():
    px, pc = lax.axis_index("x"), lax.axis_index("core")
    out = []
    for step in (0, -1, 1, 2):
        for core in (pc, 1 - pc):
            out.append(((px + step) % X) * C + core)
    return jnp.stack(out).astype(jnp.int32)


def local(queries, keys, values, out_weight, out_grad):
    full = lambda *shape: spec(shape)
    smem = pl.BlockSpec(memory_space=pltpu.SMEM)
    half = spec((T // 2, W), lambda s: (s, 0))
    slab = spec((T // 4, W), lambda i: (i, 0))
    means = call(
        means_kernel, "means", (2,), [half, half], spec((1, 8, HEAD_SIZE), lambda s: (s, 0, 0)),
        sds((2, 8, HEAD_SIZE)), 2,
    )(queries, keys)
    weight, means = gather_rows(out_weight, means)
    weight = lax.all_gather(weight, "z", axis=0, tiled=True)
    out_grad, means = lax.optimization_barrier((out_grad, means))
    tiles = to_all(means.reshape(16, HEAD_SIZE), SEQ, S)
    right = lax.ppermute(out_grad, "x", RIGHT)
    left = lax.ppermute(out_grad, "x", LEFT)
    beside = lax.ppermute(out_grad, "core", OTHER)
    right, left, tiles = lax.optimization_barrier((right, left, tiles))
    far = jnp.where(lax.axis_index("core") == 0, right, left)
    right, left, far = lax.optimization_barrier((right, left, far))
    far = lax.ppermute(far, HEAD, FAR)
    right2, left2 = lax.ppermute(right, "core", OTHER), lax.ppermute(left, "core", OTHER)
    tiles = tiles.reshape(S, 2, 2, H, HEAD_SIZE).transpose(3, 2, 1, 0, 4)
    tiles = tiles.reshape(H, 2 * M, HEAD_SIZE)

    f, fb, e, sent, stats, a, tops = call(
        scores_kernel, "scores", (H,), [COLS, COLS, COLS, TILE],
        [ROWS, ROWS, ROWS, spec((8, 16, HEAD_SIZE), lambda h: (h, 0, 0)), LAND, SQUARE, full(8, HEAD_SIZE)],
        [sds((H * M, T)), sds((H * M, T), BF16), sds((H * M, T)), sds((S, 16, HEAD_SIZE)),
         sds((H * M, HEAD_SIZE)), sds((H, M, M)), sds((8, HEAD_SIZE))], 15,
    )(queries, keys, values, tiles)

    far, fb = lax.optimization_barrier((far, fb))
    far2 = lax.ppermute(far, "core", OTHER)
    blocks = [out_grad, beside, right, right2, left, left2, far, far2]
    where = places()

    got = lax.all_to_all(sent, SEQ, 0, 0, tiled=True)
    wide = spec((T, 256), lambda i: (0, i))
    g = call(
        outer_kernel, "outer", (2,), [smem, full(H * M, T)] + [wide] * 8,
        spec((Z, 2, H * M, 128), lambda i: (0, i, 0, 0)), sds((Z, Y, H * M, 128)), 6,
    )(where, fb, *blocks)
    g, tops = lax.optimization_barrier((g, tops))
    tops = jnp.maximum(tops, lax.ppermute(tops, "core", OTHER))
    ahead = [lax.ppermute(tops, "x", [(i, (i + n) % X) for i in range(X)]) for n in range(1, X)]
    tops = jnp.maximum(jnp.maximum(tops, ahead[0]), jnp.maximum(ahead[1], ahead[2]))
    g, got, tops = lax.optimization_barrier((g, got, tops))
    merged = call(
        merge_kernel, "merge", (1,), [full(S, 16, HEAD_SIZE)], full(S, 16, HEAD_SIZE),
        sds((S, 16, HEAD_SIZE)), 1,
    )(got)
    land = lax.all_to_all(merged, SEQ, 0, 0, tiled=True)
    g = lax.psum_scatter(g, "z", scatter_dimension=0, tiled=True).reshape(Y, H * M, 128)

    tokens = 512
    panel = spec((H * M, tokens), lambda i: (0, i))
    block = spec((tokens, W), lambda i: (i, 0))
    do, sent = call(
        cotangent_kernel, "cotangent", (T // tokens,),
        [smem, full(Z * Y * 128, W), panel] + [block] * 8,
        [block, full(S, 8, HEAD_SIZE)], [sds((T, W), BF16), sds((S, 8, HEAD_SIZE))], 10,
    )(where, weight, fb, *blocks)

    land, sent, tops = lax.optimization_barrier((land, sent, tops))
    inverse, xs, t2, t3 = call(
        newton_kernel, "newton", (1,), [full(H, M, M), full(8, HEAD_SIZE)],
        [full(NEWTON + 1, H, M, M)] + [full(NEWTON, H, M, M)] * 3,
        [sds((NEWTON + 1, H, M, M))] + [sds((NEWTON, H, M, M))] * 3, 6,
    )(a, tops)

    got = lax.all_to_all(sent, SEQ, 0, 0, tiled=True)
    sent = call(
        spread_kernel, "spread", (1,), [full(S, 8, HEAD_SIZE)], full(S, 8, HEAD_SIZE), sds((S, 8, HEAD_SIZE)), 1
    )(got)
    dw = lax.all_to_all(sent, SEQ, 0, 0, tiled=True)

    parts = spec((8, 16, HEAD_SIZE), lambda h: (h, 0, 0))
    last = spec((1, 1, M, M), lambda h: (NEWTON, h, 0, 0))
    dq, dktf, wf = call(
        query_panel_kernel, "query_panel", (H,), [COLS, COLS, TILE, ROWS, parts, last],
        [COLS, full(S, 8, HEAD_SIZE), LAND], [sds((T, W)), sds((S, 8, HEAD_SIZE)), sds((H * M, HEAD_SIZE))], 5,
    )(queries, do, tiles, f, land, inverse)
    dsb, bb, dbv, sent = call(
        key_panel_kernel, "key_panel", (H,),
        [COLS, COLS, ROWS, LAND, parts, spec((8, 8, HEAD_SIZE), lambda h: (h, 0, 0)), last,
         full(S, 8, HEAD_SIZE)],
        [ROWS, ROWS, LAND, full(S, 16, HEAD_SIZE)],
        [sds((H * M, T), BF16), sds((H * M, T), BF16), sds((H * M, HEAD_SIZE), BF16),
         sds((S, 16, HEAD_SIZE))], 4,
    )(keys, values, e, stats, land, dw, inverse, dktf)
    dk, dv = call(
        key_rows_kernel, "key_rows", (H,), [ROWS, ROWS, LAND, TILE], [COLS, COLS],
        [sds((T, W)), sds((T, W), BF16)], 4,
    )(dsb, bb, dbv, tiles)

    g, dsb = lax.optimization_barrier((g, dsb))
    here = lax.axis_index("y")
    gs = [lax.dynamic_index_in_dim(g, (here + n) % Y, keepdims=False) for n in range(Y)]
    gs[1:] = [
        lax.ppermute(gs[n], "y", [(i, (i + n) % Y) for i in range(Y)]) for n in range(1, Y)
    ]
    summed = lax.all_to_all(sent, SEQ, 0, 0, tiled=True)
    own = lax.axis_index(SEQ).astype(jnp.int32).reshape(1)
    da = call(
        adjoint_kernel, "adjoint", (1,),
        [smem, full(S, 8, HEAD_SIZE), full(S, 16, HEAD_SIZE), full(8, HEAD_SIZE), full(H, M, M),
         full(NEWTON + 1, H, M, M)] + [full(NEWTON, H, M, M)] * 3 + [full(H, 2 * M, HEAD_SIZE)],
        full(16, HEAD_SIZE), sds((16, HEAD_SIZE)), 9,
    )(own, dw, land, tops, a, inverse, xs, t2, t3, tiles)
    query_grad, key_grad = call(
        final_kernel, "final", (4,), [slab, slab, full(S, 16, HEAD_SIZE), full(16, HEAD_SIZE)],
        [slab, slab], [sds((T, W), BF16)] * 2, 2, [pltpu.VMEM((16, HEAD_SIZE), F32)],
    )(dq, dk, summed, da)
    weight_grad = call(
        weight_kernel, "weight", (1,), [full(H * M, 128)] * Y + [full(H * M, HEAD_SIZE)], full(128, W), sds((128, W)), 2,
    )(*gs, wf)
    return query_grad, key_grad, dv, weight_grad


def solution(mesh):
    grid = Mesh(mesh.devices.reshape(Z, Y, X, C), SEQ + HEAD)
    place = P(SEQ, HEAD)
    return jax.shard_map(
        local, mesh=grid, in_specs=(place,) * 5, out_specs=(place,) * 4, check_vma=False
    )
```

```python
import jax
import jax.numpy as jnp
from jax import lax
from jax.experimental import pallas as pl
from jax.experimental.pallas import tpu as pltpu
from jax.sharding import Mesh
from jax.sharding import PartitionSpec as P

HEAD_SIZE = 128
M = 64
NEWTON = 6
SCALE = HEAD_SIZE**-0.5
HIGHEST = lax.Precision.HIGHEST
F32 = jnp.float32
BF16 = jnp.bfloat16

Z, Y, X, C = 8, 4, 4, 2
SEQ = ("z", "y")
HEAD = ("x", "core")
S = Z * Y
H = 4
T = 1024
W = H * HEAD_SIZE


def dot(a, b, ca=1, cb=0, precision=None):
    return lax.dot_general(
        a, b, (((ca,), (cb,)), ((), ())), preferred_element_type=F32, precision=precision
    )


def parts_of(x):
    hi = x.astype(BF16)
    rest = x - hi.astype(F32)
    mid = rest.astype(BF16)
    lo = (rest - mid.astype(F32)).astype(BF16)
    return hi, mid, lo


def wide_dot(x, y, ca=1, cb=0):
    hi, mid, lo = parts_of(x)
    return dot(hi, y, ca, cb) + (dot(mid, y, ca, cb) + dot(lo, y, ca, cb))


def close_dot(x, y, ca=1, cb=0):
    xh, yh = x.astype(BF16), y.astype(BF16)
    xl = (x - xh.astype(F32)).astype(BF16)
    yl = (y - yh.astype(F32)).astype(BF16)
    return dot(xh, yh, ca, cb) + (dot(xh, yl, ca, cb) + dot(xl, yh, ca, cb))


def call(kernel, name, grid, in_specs, out_specs, out_shape, cost, scratch=(), vmem=63.9):
    return pl.pallas_call(
        kernel,
        grid=grid,
        in_specs=in_specs,
        out_specs=out_specs,
        out_shape=out_shape,
        scratch_shapes=scratch,
        name=name,
        compiler_params=pltpu.CompilerParams(vmem_limit_bytes=int(vmem * 2**20)),
        cost_estimate=pl.CostEstimate(
            flops=int(cost * 1e9), bytes_accessed=1 << 20, transcendentals=0
        ),
    )


def spec(shape, index=None):
    if index is None:
        index = lambda h, n=len(shape): (0,) * n
    return pl.BlockSpec(shape, index)


def sds(shape, dtype=F32):
    return jax.ShapeDtypeStruct(shape, dtype)


COLS = spec((T, HEAD_SIZE), lambda h: (0, h))
ROWS = spec((M, T), lambda h: (h, 0))
LAND = spec((M, HEAD_SIZE), lambda h: (h, 0))
TILE = spec((1, 2 * M, HEAD_SIZE), lambda h: (h, 0, 0))
SQUARE = spec((1, M, M), lambda h: (h, 0, 0))


def means_kernel(q_ref, k_ref, o_ref):
    for i, ref in enumerate((q_ref, k_ref)):
        mean = jnp.sum(ref[...].astype(F32), axis=0, keepdims=True) / ref.shape[0]
        for h in range(H):
            o_ref[0, H * i + h : H * i + h + 1, :] = mean[:, h * HEAD_SIZE : (h + 1) * HEAD_SIZE]


def scores_kernel(q_ref, k_ref, v_ref, t_ref, f_ref, fb_ref, e_ref, sent_ref, st_ref, a_ref, mx_ref):
    qt, kt = t_ref[0, :M], t_ref[0, M:]
    s1 = dot(kt.astype(BF16), q_ref[...], 1, 1) * SCALE
    p = jnp.exp(s1 - jnp.max(s1, axis=0, keepdims=True))
    f = p / jnp.sum(p, axis=0, keepdims=True)
    f_ref[...] = f
    fb_ref[...] = f.astype(BF16)
    s2 = dot(qt.astype(BF16), k_ref[...], 1, 1) * SCALE
    top = jnp.max(s2, axis=1, keepdims=True)
    e = jnp.exp(s2 - top)
    e_ref[...] = e
    total = jnp.sum(e, axis=1, keepdims=True)
    sent_ref[:, :8] = wide_dot(e, v_ref[...]).reshape(8, 8, HEAD_SIZE)
    lane = lax.broadcasted_iota(jnp.int32, (M, HEAD_SIZE), 1)
    stats = jnp.where(lane < M, top, total)
    st_ref[...] = stats
    sent_ref[:, 8:] = stats.reshape(8, 8, HEAD_SIZE)
    sa = dot(qt, kt, 1, 1, HIGHEST) * SCALE
    pa = jnp.exp(sa - jnp.max(sa, axis=1, keepdims=True))
    a = pa / jnp.sum(pa, axis=1, keepdims=True)
    a_ref[0] = a
    col = jnp.max(jnp.sum(a, axis=0, keepdims=True), axis=1, keepdims=True)
    row = jnp.max(jnp.sum(a, axis=1, keepdims=True), axis=0, keepdims=True)
    sub = lax.broadcasted_iota(jnp.int32, (8, HEAD_SIZE), 0)
    both = jnp.where(sub < 4, col, row)

    @pl.when(pl.program_id(0) == 0)
    def _():
        mx_ref[...] = both

    @pl.when(pl.program_id(0) > 0)
    def _():
        mx_ref[...] = jnp.maximum(mx_ref[...], both)


def newton_kernel(a_ref, mx_ref, z_ref, x_ref, t2_ref, t3_ref):
    eye = (
        lax.broadcasted_iota(jnp.int32, (M, M), 0) == lax.broadcasted_iota(jnp.int32, (M, M), 1)
    ).astype(F32)
    mx = mx_ref[...]
    denom = mx[0:1, 0:1] * mx[4:5, 0:1]
    zs = []
    for h in range(H):
        z = a_ref[h].T / denom
        z_ref[0, h] = z
        zs.append(z)
    for n in range(NEWTON):
        xs = [dot(a_ref[h], zs[h], precision=HIGHEST) for h in range(H)]
        t2 = [15.0 * eye - dot(x, 7.0 * eye - x, precision=HIGHEST) for x in xs]
        t3 = [13.0 * eye - dot(x, t, precision=HIGHEST) for x, t in zip(xs, t2)]
        zs = [0.25 * dot(z, t, precision=HIGHEST) for z, t in zip(zs, t3)]
        for h in range(H):
            x_ref[n, h] = xs[h]
            t2_ref[n, h] = t2[h]
            t3_ref[n, h] = t3[h]
            z_ref[n + 1, h] = zs[h]


def merge_kernel(r_ref, o_ref):
    v, st = r_ref[:, :8, :], r_ref[:, 8:, :]
    top, total = st[:, :, 0:1], st[:, :, M : M + 1]
    mx = jnp.max(top, axis=0, keepdims=True)
    scale = jnp.exp(top - mx)
    whole = jnp.sum(scale * total, axis=0)
    lane = lax.broadcasted_iota(jnp.int32, (8, HEAD_SIZE), 1)
    o_ref[:, :8] = jnp.broadcast_to((jnp.sum(scale * v, axis=0) / whole)[None], (S, 8, HEAD_SIZE))
    o_ref[:, 8:] = jnp.broadcast_to(jnp.where(lane < M, mx[0], whole)[None], (S, 8, HEAD_SIZE))


def outer_kernel(j_ref, fb_ref, *refs):
    ogs, out = refs[:8], refs[8]
    fb = fb_ref[...]
    for b in range(8):
        res = dot(fb, ogs[b][...])
        for y in range(2):
            out[j_ref[b], y] = res[:, y * 128 : (y + 1) * 128]


def cotangent_kernel(j_ref, w_ref, fb_ref, *refs):
    ogs, do_ref, sent_ref = refs[:8], refs[8], refs[9]
    i = pl.program_id(0)
    acc = None
    for b in range(8):
        at = pl.multiple_of(j_ref[b] * W, W)
        part = dot(ogs[b][...], w_ref[pl.ds(at, W), :])
        acc = part if acc is None else acc + part
    do = acc.astype(BF16)
    do_ref[...] = do

    @pl.when(i == 0)
    def _():
        sent_ref[...] = jnp.zeros((S, 8, HEAD_SIZE), F32)

    for h in range(H):
        part = dot(fb_ref[h * M : (h + 1) * M, :], do[:, h * HEAD_SIZE : (h + 1) * HEAD_SIZE])
        sent_ref[8 * h : 8 * h + 8] += part.reshape(8, 8, HEAD_SIZE)


def spread_kernel(r_ref, o_ref):
    o_ref[...] = jnp.broadcast_to(jnp.sum(r_ref[...], axis=0)[None], (S, 8, HEAD_SIZE))


def put_rows(ref, x):
    for s in range(2):
        ref[:, pl.ds(2 * pl.program_id(0) + s, 1), :] = x[s * S : (s + 1) * S][:, None, :]


def query_panel_kernel(q_ref, do_ref, t_ref, f_ref, got_ref, z_ref, dq_ref, dt_ref, wf_ref):
    ktb = t_ref[0, M:].astype(BF16)
    bv = got_ref[:, :8].reshape(M, HEAD_SIZE)
    wf = dot(z_ref[0, 0], bv, precision=HIGHEST)
    wf_ref[...] = wf
    f = f_ref[...]
    df = wide_dot(wf, do_ref[...], 1, 1)
    dsf = (f * (df - jnp.sum(df * f, axis=0, keepdims=True))).astype(BF16)
    put_rows(dt_ref, dot(dsf, q_ref[...]) * SCALE)
    dq_ref[...] = dot(dsf, ktb, 0, 0) * SCALE


def key_panel_kernel(
    k_ref, v_ref, e_ref, st_ref, got_ref, dw_ref, z_ref, dt_ref, dsb_ref, bb_ref, dbv_ref, sent_ref
):
    dw = dw_ref[...].reshape(M, HEAD_SIZE)
    bv = got_ref[:, :8].reshape(M, HEAD_SIZE)
    whole = got_ref[:, 8:].reshape(M, HEAD_SIZE)
    dbv = dot(z_ref[0, 0], dw, 0, 0, HIGHEST).astype(BF16)
    dbv_ref[...] = dbv
    db = dot(dbv, v_ref[...], 1, 1)
    beta = jnp.sum(dbv.astype(F32) * bv, axis=1, keepdims=True)
    rescale = jnp.exp(st_ref[:, 0:1] - whole[:, 0:1]) / whole[:, M : M + 1]
    bf = e_ref[...] * rescale
    dsb = (bf * (db - beta)).astype(BF16)
    dsb_ref[...] = dsb
    bb_ref[...] = bf.astype(BF16)
    put_rows(sent_ref, dot(dsb, k_ref[...]) * SCALE)

    @pl.when(pl.program_id(0) == 0)
    def _():
        sent_ref[:, 8:] = dt_ref[...]


def key_rows_kernel(dsb_ref, bb_ref, dbv_ref, t_ref, dk_ref, dv_ref):
    dk_ref[...] = dot(dsb_ref[...], t_ref[0, :M].astype(BF16), 0, 0) * SCALE
    dv_ref[...] = dot(bb_ref[...], dbv_ref[...], 0, 0).astype(BF16)


def adjoint_kernel(own_ref, dw_ref, got_ref, mx_ref, a_ref, z_ref, x_ref, t2_ref, t3_ref, t_ref, o_ref):
    eye = (
        lax.broadcasted_iota(jnp.int32, (M, M), 0) == lax.broadcasted_iota(jnp.int32, (M, M), 1)
    ).astype(F32)
    hi = close_dot
    heads = range(H)
    dz = []
    for h in heads:
        dw = dw_ref[8 * h : 8 * h + 8].reshape(M, HEAD_SIZE)
        bv = got_ref[8 * h : 8 * h + 8, :8].reshape(M, HEAD_SIZE)
        dz.append(hi(dw, bv, 1, 1))
    da = [jnp.zeros((M, M), F32) for h in heads]
    for n in reversed(range(NEWTON)):
        x = [x_ref[n, h] for h in heads]
        g = [0.25 * d for d in dz]
        dp2 = [-hi(z_ref[n, h], g[h], 0, 0) for h in heads]
        dz = [hi(g[h], t3_ref[n, h], 1, 1) for h in heads]
        dp1 = [-hi(x[h], dp2[h], 0, 0) for h in heads]
        dx = [hi(dp2[h], t2_ref[n, h], 1, 1) for h in heads]
        dt1 = [hi(x[h], dp1[h], 0, 0) for h in heads]
        dx = [dx[h] + hi(dp1[h], 7.0 * eye - x[h], 1, 1) - dt1[h] for h in heads]
        dz = [dz[h] + hi(a_ref[h], dx[h], 0, 0) for h in heads]
        da = [da[h] + hi(dx[h], z_ref[n, h], 1, 1) for h in heads]
    mx = mx_ref[...]
    denom = mx[0:1, 0:1] * mx[4:5, 0:1]
    row = lax.broadcasted_iota(jnp.int32, (M, HEAD_SIZE), 0)
    for h in heads:
        d = da[h] + dz[h].T / denom
        a = a_ref[h]
        dsa = a * (d - jnp.sum(d * a, axis=1, keepdims=True))
        dqt = hi(dsa, t_ref[h, M:]) * SCALE
        dkt = hi(dsa, t_ref[h, :M], 0, 0) * SCALE
        for i, x in enumerate((dqt, dkt)):
            for s in range(2):
                mine = jnp.where(row == own_ref[0] + s * S, x, 0.0)
                r = 8 * i + 2 * h + s
                o_ref[r : r + 1, :] = jnp.sum(mine, axis=0, keepdims=True)


def final_kernel(dq_ref, dk_ref, got_ref, add_ref, q_out, k_out, tot_ref):
    i = pl.program_id(0)

    @pl.when(i == 0)
    def _():
        tot_ref[...] = (jnp.sum(got_ref[...], axis=0) + add_ref[...]) / (T // 2)

    s = i // 2
    for n, (ref, out) in enumerate(((dq_ref, q_out), (dk_ref, k_out))):
        for h in range(H):
            cols = slice(h * HEAD_SIZE, (h + 1) * HEAD_SIZE)
            add = tot_ref[pl.ds(8 * n + 2 * h + s, 1), :]
            out[:, cols] = (ref[:, cols] + add).astype(BF16)


def weight_kernel(*refs):
    gs, wf_ref, o_ref = refs[:Y], refs[Y], refs[Y + 1]
    for h in range(H):
        rows = slice(h * M, (h + 1) * M)
        a, b, c, d = (ref[rows, :] for ref in gs)
        o_ref[:, h * HEAD_SIZE : (h + 1) * HEAD_SIZE] = dot(
            (a + b) + (c + d), wf_ref[rows, :], 0, 0, HIGHEST
        )


def to_all(x, axes, n):
    return lax.all_to_all(jnp.broadcast_to(x[None], (n,) + x.shape), axes, 0, 0, tiled=True)


def gather_rows(x, means):
    here = lax.axis_index("y")
    x, means = lax.optimization_barrier((x, means))
    blocks = [
        lax.ppermute(x, "y", [(i, (i + step) % Y) for i in range(Y)]) for step in range(1, Y)
    ]
    out = jnp.zeros((Y,) + x.shape, x.dtype)
    out = lax.dynamic_update_index_in_dim(out, x, here, 0)
    for step, block in enumerate(blocks, 1):
        out = lax.dynamic_update_index_in_dim(out, block, (here - step) % Y, 0)
    return out.reshape(Y * x.shape[0], x.shape[1]), means


RIGHT = [(i, (i + 1) % X) for i in range(X)]
LEFT = [(i, (i - 1) % X) for i in range(X)]
OTHER = [(0, 1), (1, 0)]
FAR = [(i * C + c, (i + 1 - 2 * c) % X * C + c) for i in range(X) for c in range(C)]


def places():
    px, pc = lax.axis_index("x"), lax.axis_index("core")
    out = []
    for step in (0, -1, 1, 2):
        for core in (pc, 1 - pc):
            out.append(((px + step) % X) * C + core)
    return jnp.stack(out).astype(jnp.int32)


def local(queries, keys, values, out_weight, out_grad):
    full = lambda *shape: spec(shape)
    smem = pl.BlockSpec(memory_space=pltpu.SMEM)
    half = spec((T // 2, W), lambda s: (s, 0))
    slab = spec((T // 4, W), lambda i: (i, 0))
    means = call(
        means_kernel, "means", (2,), [half, half], spec((1, 8, HEAD_SIZE), lambda s: (s, 0, 0)),
        sds((2, 8, HEAD_SIZE)), 2,
    )(queries, keys)
    weight, means = gather_rows(out_weight, means)
    weight = lax.all_gather(weight, "z", axis=0, tiled=True)
    out_grad, means = lax.optimization_barrier((out_grad, means))
    tiles = to_all(means.reshape(16, HEAD_SIZE), SEQ, S)
    right = lax.ppermute(out_grad, "x", RIGHT)
    left = lax.ppermute(out_grad, "x", LEFT)
    beside = lax.ppermute(out_grad, "core", OTHER)
    right, left, tiles = lax.optimization_barrier((right, left, tiles))
    far = jnp.where(lax.axis_index("core") == 0, right, left)
    right, left, far = lax.optimization_barrier((right, left, far))
    far = lax.ppermute(far, HEAD, FAR)
    right2, left2 = lax.ppermute(right, "core", OTHER), lax.ppermute(left, "core", OTHER)
    tiles = tiles.reshape(S, 2, 2, H, HEAD_SIZE).transpose(3, 2, 1, 0, 4)
    tiles = tiles.reshape(H, 2 * M, HEAD_SIZE)

    f, fb, e, sent, stats, a, tops = call(
        scores_kernel, "scores", (H,), [COLS, COLS, COLS, TILE],
        [ROWS, ROWS, ROWS, spec((8, 16, HEAD_SIZE), lambda h: (h, 0, 0)), LAND, SQUARE, full(8, HEAD_SIZE)],
        [sds((H * M, T)), sds((H * M, T), BF16), sds((H * M, T)), sds((S, 16, HEAD_SIZE)),
         sds((H * M, HEAD_SIZE)), sds((H, M, M)), sds((8, HEAD_SIZE))], 60,
    )(queries, keys, values, tiles)

    far, fb = lax.optimization_barrier((far, fb))
    far2 = lax.ppermute(far, "core", OTHER)
    blocks = [out_grad, beside, right, right2, left, left2, far, far2]
    where = places()

    got = lax.all_to_all(sent, SEQ, 0, 0, tiled=True)
    wide = spec((T, 256), lambda i: (0, i))
    g = call(
        outer_kernel, "outer", (2,), [smem, full(H * M, T)] + [wide] * 8,
        spec((Z, 2, H * M, 128), lambda i: (0, i, 0, 0)), sds((Z, Y, H * M, 128)), 20,
    )(where, fb, *blocks)
    g, tops = lax.optimization_barrier((g, tops))
    tops = jnp.maximum(tops, lax.ppermute(tops, "core", OTHER))
    ahead = [lax.ppermute(tops, "x", [(i, (i + n) % X) for i in range(X)]) for n in range(1, X)]
    tops = jnp.maximum(jnp.maximum(tops, ahead[0]), jnp.maximum(ahead[1], ahead[2]))
    g, got, tops = lax.optimization_barrier((g, got, tops))
    merged = call(
        merge_kernel, "merge", (1,), [full(S, 16, HEAD_SIZE)], full(S, 16, HEAD_SIZE),
        sds((S, 16, HEAD_SIZE)), 1,
    )(got)
    land = lax.all_to_all(merged, SEQ, 0, 0, tiled=True)
    g = lax.psum_scatter(g, "z", scatter_dimension=0, tiled=True).reshape(Y, H * M, 128)

    tokens = 512
    panel = spec((H * M, tokens), lambda i: (0, i))
    block = spec((tokens, W), lambda i: (i, 0))
    do, sent = call(
        cotangent_kernel, "cotangent", (T // tokens,),
        [smem, full(Z * Y * 128, W), panel] + [block] * 8,
        [block, full(S, 8, HEAD_SIZE)], [sds((T, W), BF16), sds((S, 8, HEAD_SIZE))], 10,
    )(where, weight, fb, *blocks)

    land, sent, tops = lax.optimization_barrier((land, sent, tops))
    inverse, xs, t2, t3 = call(
        newton_kernel, "newton", (1,), [full(H, M, M), full(8, HEAD_SIZE)],
        [full(NEWTON + 1, H, M, M)] + [full(NEWTON, H, M, M)] * 3,
        [sds((NEWTON + 1, H, M, M))] + [sds((NEWTON, H, M, M))] * 3, 6,
    )(a, tops)

    got = lax.all_to_all(sent, SEQ, 0, 0, tiled=True)
    sent = call(
        spread_kernel, "spread", (1,), [full(S, 8, HEAD_SIZE)], full(S, 8, HEAD_SIZE), sds((S, 8, HEAD_SIZE)), 1
    )(got)
    dw = lax.all_to_all(sent, SEQ, 0, 0, tiled=True)

    parts = spec((8, 16, HEAD_SIZE), lambda h: (h, 0, 0))
    last = spec((1, 1, M, M), lambda h: (NEWTON, h, 0, 0))
    dq, dktf, wf = call(
        query_panel_kernel, "query_panel", (H,), [COLS, COLS, TILE, ROWS, parts, last],
        [COLS, full(S, 8, HEAD_SIZE), LAND], [sds((T, W)), sds((S, 8, HEAD_SIZE)), sds((H * M, HEAD_SIZE))], 5,
    )(queries, do, tiles, f, land, inverse)
    dsb, bb, dbv, sent = call(
        key_panel_kernel, "key_panel", (H,),
        [COLS, COLS, ROWS, LAND, parts, spec((8, 8, HEAD_SIZE), lambda h: (h, 0, 0)), last,
         full(S, 8, HEAD_SIZE)],
        [ROWS, ROWS, LAND, full(S, 16, HEAD_SIZE)],
        [sds((H * M, T), BF16), sds((H * M, T), BF16), sds((H * M, HEAD_SIZE), BF16),
         sds((S, 16, HEAD_SIZE))], 4,
    )(keys, values, e, stats, land, dw, inverse, dktf)
    dk, dv = call(
        key_rows_kernel, "key_rows", (H,), [ROWS, ROWS, LAND, TILE], [COLS, COLS],
        [sds((T, W)), sds((T, W), BF16)], 4,
    )(dsb, bb, dbv, tiles)

    g, dsb = lax.optimization_barrier((g, dsb))
    here = lax.axis_index("y")
    gs = [lax.dynamic_index_in_dim(g, (here + n) % Y, keepdims=False) for n in range(Y)]
    gs[1:] = [
        lax.ppermute(gs[n], "y", [(i, (i + n) % Y) for i in range(Y)]) for n in range(1, Y)
    ]
    summed = lax.all_to_all(sent, SEQ, 0, 0, tiled=True)
    own = lax.axis_index(SEQ).astype(jnp.int32).reshape(1)
    da = call(
        adjoint_kernel, "adjoint", (1,),
        [smem, full(S, 8, HEAD_SIZE), full(S, 16, HEAD_SIZE), full(8, HEAD_SIZE), full(H, M, M),
         full(NEWTON + 1, H, M, M)] + [full(NEWTON, H, M, M)] * 3 + [full(H, 2 * M, HEAD_SIZE)],
        full(16, HEAD_SIZE), sds((16, HEAD_SIZE)), 9,
    )(own, dw, land, tops, a, inverse, xs, t2, t3, tiles)
    query_grad, key_grad = call(
        final_kernel, "final", (4,), [slab, slab, full(S, 16, HEAD_SIZE), full(16, HEAD_SIZE)],
        [slab, slab], [sds((T, W), BF16)] * 2, 2, [pltpu.VMEM((16, HEAD_SIZE), F32)],
    )(dq, dk, summed, da)
    weight_grad = call(
        weight_kernel, "weight", (1,), [full(H * M, 128)] * Y + [full(H * M, HEAD_SIZE)], full(128, W), sds((128, W)), 2,
    )(*gs, wf)
    return query_grad, key_grad, dv, weight_grad


def solution(mesh):
    grid = Mesh(mesh.devices.reshape(Z, Y, X, C), SEQ + HEAD)
    place = P(SEQ, HEAD)
    return jax.shard_map(
        local, mesh=grid, in_specs=(place,) * 5, out_specs=(place,) * 4, check_vma=False
    )
```

```python
import jax
import jax.numpy as jnp
from jax import lax
from jax.experimental import pallas as pl
from jax.experimental.pallas import tpu as pltpu
from jax.sharding import Mesh
from jax.sharding import PartitionSpec as P

HEAD_SIZE = 128
M = 64
NEWTON = 6
SCALE = HEAD_SIZE**-0.5
HIGHEST = lax.Precision.HIGHEST
F32 = jnp.float32
BF16 = jnp.bfloat16

Z, Y, X, C = 8, 4, 4, 2
SEQ = ("z", "y")
HEAD = ("x", "core")
S = Z * Y
H = 4
T = 1024
W = H * HEAD_SIZE


def dot(a, b, ca=1, cb=0, precision=None):
    return lax.dot_general(
        a, b, (((ca,), (cb,)), ((), ())), preferred_element_type=F32, precision=precision
    )


def parts_of(x):
    hi = x.astype(BF16)
    rest = x - hi.astype(F32)
    mid = rest.astype(BF16)
    lo = (rest - mid.astype(F32)).astype(BF16)
    return hi, mid, lo


def wide_dot(x, y, ca=1, cb=0):
    hi, mid, lo = parts_of(x)
    return dot(hi, y, ca, cb) + (dot(mid, y, ca, cb) + dot(lo, y, ca, cb))


def close_dot(x, y, ca=1, cb=0):
    xh, yh = x.astype(BF16), y.astype(BF16)
    xl = (x - xh.astype(F32)).astype(BF16)
    yl = (y - yh.astype(F32)).astype(BF16)
    return dot(xh, yh, ca, cb) + (dot(xh, yl, ca, cb) + dot(xl, yh, ca, cb))


def call(kernel, name, grid, in_specs, out_specs, out_shape, cost, scratch=(), vmem=63.9):
    return pl.pallas_call(
        kernel,
        grid=grid,
        in_specs=in_specs,
        out_specs=out_specs,
        out_shape=out_shape,
        scratch_shapes=scratch,
        name=name,
        compiler_params=pltpu.CompilerParams(vmem_limit_bytes=int(vmem * 2**20)),
        cost_estimate=pl.CostEstimate(
            flops=int(cost * 1e9), bytes_accessed=1 << 20, transcendentals=0
        ),
    )


def spec(shape, index=None):
    if index is None:
        index = lambda h, n=len(shape): (0,) * n
    return pl.BlockSpec(shape, index)


def sds(shape, dtype=F32):
    return jax.ShapeDtypeStruct(shape, dtype)


COLS = spec((T, HEAD_SIZE), lambda h: (0, h))
ROWS = spec((M, T), lambda h: (h, 0))
LAND = spec((M, HEAD_SIZE), lambda h: (h, 0))
TILE = spec((1, 2 * M, HEAD_SIZE), lambda h: (h, 0, 0))
SQUARE = spec((1, M, M), lambda h: (h, 0, 0))


def means_kernel(q_ref, k_ref, o_ref):
    for i, ref in enumerate((q_ref, k_ref)):
        mean = jnp.sum(ref[...].astype(F32), axis=0, keepdims=True) / ref.shape[0]
        for h in range(H):
            o_ref[0, H * i + h : H * i + h + 1, :] = mean[:, h * HEAD_SIZE : (h + 1) * HEAD_SIZE]


def scores_kernel(q_ref, k_ref, v_ref, t_ref, f_ref, fb_ref, e_ref, sent_ref, st_ref, a_ref, mx_ref):
    qt, kt = t_ref[0, :M], t_ref[0, M:]
    s1 = dot(kt.astype(BF16), q_ref[...], 1, 1) * SCALE
    p = jnp.exp(s1 - jnp.max(s1, axis=0, keepdims=True))
    f = p / jnp.sum(p, axis=0, keepdims=True)
    f_ref[...] = f
    fb_ref[...] = f.astype(BF16)
    s2 = dot(qt.astype(BF16), k_ref[...], 1, 1) * SCALE
    top = jnp.max(s2, axis=1, keepdims=True)
    e = jnp.exp(s2 - top)
    e_ref[...] = e
    total = jnp.sum(e, axis=1, keepdims=True)
    sent_ref[:, :8] = wide_dot(e, v_ref[...]).reshape(8, 8, HEAD_SIZE)
    lane = lax.broadcasted_iota(jnp.int32, (M, HEAD_SIZE), 1)
    stats = jnp.where(lane < M, top, total)
    st_ref[...] = stats
    sent_ref[:, 8:] = stats.reshape(8, 8, HEAD_SIZE)
    sa = dot(qt, kt, 1, 1, HIGHEST) * SCALE
    pa = jnp.exp(sa - jnp.max(sa, axis=1, keepdims=True))
    a = pa / jnp.sum(pa, axis=1, keepdims=True)
    a_ref[0] = a
    col = jnp.max(jnp.sum(a, axis=0, keepdims=True), axis=1, keepdims=True)
    row = jnp.max(jnp.sum(a, axis=1, keepdims=True), axis=0, keepdims=True)
    sub = lax.broadcasted_iota(jnp.int32, (8, HEAD_SIZE), 0)
    both = jnp.where(sub < 4, col, row)

    @pl.when(pl.program_id(0) == 0)
    def _():
        mx_ref[...] = both

    @pl.when(pl.program_id(0) > 0)
    def _():
        mx_ref[...] = jnp.maximum(mx_ref[...], both)


def newton_kernel(a_ref, mx_ref, z_ref, x_ref, t2_ref, t3_ref):
    eye = (
        lax.broadcasted_iota(jnp.int32, (M, M), 0) == lax.broadcasted_iota(jnp.int32, (M, M), 1)
    ).astype(F32)
    mx = mx_ref[...]
    denom = mx[0:1, 0:1] * mx[4:5, 0:1]
    zs = []
    for h in range(H):
        z = a_ref[h].T / denom
        z_ref[0, h] = z
        zs.append(z)
    for n in range(NEWTON):
        xs = [dot(a_ref[h], zs[h], precision=HIGHEST) for h in range(H)]
        t2 = [15.0 * eye - dot(x, 7.0 * eye - x, precision=HIGHEST) for x in xs]
        t3 = [13.0 * eye - dot(x, t, precision=HIGHEST) for x, t in zip(xs, t2)]
        zs = [0.25 * dot(z, t, precision=HIGHEST) for z, t in zip(zs, t3)]
        for h in range(H):
            x_ref[n, h] = xs[h]
            t2_ref[n, h] = t2[h]
            t3_ref[n, h] = t3[h]
            z_ref[n + 1, h] = zs[h]


def merge_kernel(r_ref, o_ref):
    v, st = r_ref[:, :8, :], r_ref[:, 8:, :]
    top, total = st[:, :, 0:1], st[:, :, M : M + 1]
    mx = jnp.max(top, axis=0, keepdims=True)
    scale = jnp.exp(top - mx)
    whole = jnp.sum(scale * total, axis=0)
    lane = lax.broadcasted_iota(jnp.int32, (8, HEAD_SIZE), 1)
    o_ref[:, :8] = jnp.broadcast_to((jnp.sum(scale * v, axis=0) / whole)[None], (S, 8, HEAD_SIZE))
    o_ref[:, 8:] = jnp.broadcast_to(jnp.where(lane < M, mx[0], whole)[None], (S, 8, HEAD_SIZE))


def outer_kernel(j_ref, fb_ref, *refs):
    ogs, out = refs[:-1], refs[-1]
    for b, og in enumerate(ogs):
        res = dot(fb_ref[...], og[...])
        for y in range(2):
            out[j_ref[b], y] = res[:, y * 128 : (y + 1) * 128]


def outer_far_kernel(j_ref, fb_ref, far_ref, far2_ref, g_ref, out_ref):
    for i, og in enumerate((far_ref, far2_ref)):

        @pl.when(pl.program_id(0) == i)
        def _(og=og):
            res = dot(fb_ref[...], og[...])
            for y in range(Y):
                out_ref[0, y] = res[:, y * 128 : (y + 1) * 128]


def cotangent_kernel(j_ref, w_ref, fb_ref, *refs):
    ogs, do_ref, sent_ref = refs[:8], refs[8], refs[9]
    i = pl.program_id(0)
    acc = None
    for b in range(8):
        at = pl.multiple_of(j_ref[b] * W, W)
        part = dot(ogs[b][...], w_ref[pl.ds(at, W), :])
        acc = part if acc is None else acc + part
    do = acc.astype(BF16)
    do_ref[...] = do

    @pl.when(i == 0)
    def _():
        sent_ref[...] = jnp.zeros((S, 8, HEAD_SIZE), F32)

    for h in range(H):
        part = dot(fb_ref[h * M : (h + 1) * M, :], do[:, h * HEAD_SIZE : (h + 1) * HEAD_SIZE])
        sent_ref[8 * h : 8 * h + 8] += part.reshape(8, 8, HEAD_SIZE)


def spread_kernel(r_ref, o_ref):
    o_ref[...] = jnp.broadcast_to(jnp.sum(r_ref[...], axis=0)[None], (S, 8, HEAD_SIZE))


def put_rows(ref, x):
    for s in range(2):
        ref[:, pl.ds(2 * pl.program_id(0) + s, 1), :] = x[s * S : (s + 1) * S][:, None, :]


def query_panel_kernel(q_ref, do_ref, t_ref, f_ref, got_ref, z_ref, dq_ref, dt_ref, wf_ref):
    ktb = t_ref[0, M:].astype(BF16)
    bv = got_ref[:, :8].reshape(M, HEAD_SIZE)
    wf = dot(z_ref[0, 0], bv, precision=HIGHEST)
    wf_ref[...] = wf
    f = f_ref[...]
    df = wide_dot(wf, do_ref[...], 1, 1)
    dsf = (f * (df - jnp.sum(df * f, axis=0, keepdims=True))).astype(BF16)
    put_rows(dt_ref, dot(dsf, q_ref[...]) * SCALE)
    dq_ref[...] = dot(dsf, ktb, 0, 0) * SCALE


def key_panel_kernel(
    k_ref, v_ref, e_ref, st_ref, got_ref, dw_ref, z_ref, dt_ref, dsb_ref, bb_ref, dbv_ref, sent_ref
):
    dw = dw_ref[...].reshape(M, HEAD_SIZE)
    bv = got_ref[:, :8].reshape(M, HEAD_SIZE)
    whole = got_ref[:, 8:].reshape(M, HEAD_SIZE)
    dbv = dot(z_ref[0, 0], dw, 0, 0, HIGHEST).astype(BF16)
    dbv_ref[...] = dbv
    db = dot(dbv, v_ref[...], 1, 1)
    beta = jnp.sum(dbv.astype(F32) * bv, axis=1, keepdims=True)
    rescale = jnp.exp(st_ref[:, 0:1] - whole[:, 0:1]) / whole[:, M : M + 1]
    bf = e_ref[...] * rescale
    dsb = (bf * (db - beta)).astype(BF16)
    dsb_ref[...] = dsb
    bb_ref[...] = bf.astype(BF16)
    put_rows(sent_ref, dot(dsb, k_ref[...]) * SCALE)

    @pl.when(pl.program_id(0) == 0)
    def _():
        sent_ref[:, 8:] = dt_ref[...]


def value_rows_kernel(bb_ref, dbv_ref, dv_ref):
    dv_ref[...] = dot(bb_ref[...], dbv_ref[...], 0, 0).astype(BF16)


def adjoint_kernel(own_ref, dw_ref, got_ref, mx_ref, a_ref, z_ref, x_ref, t2_ref, t3_ref, t_ref, o_ref):
    eye = (
        lax.broadcasted_iota(jnp.int32, (M, M), 0) == lax.broadcasted_iota(jnp.int32, (M, M), 1)
    ).astype(F32)
    hi = close_dot
    heads = range(H)
    dz = []
    for h in heads:
        dw = dw_ref[8 * h : 8 * h + 8].reshape(M, HEAD_SIZE)
        bv = got_ref[8 * h : 8 * h + 8, :8].reshape(M, HEAD_SIZE)
        dz.append(hi(dw, bv, 1, 1))
    da = [jnp.zeros((M, M), F32) for h in heads]
    for n in reversed(range(NEWTON)):
        x = [x_ref[n, h] for h in heads]
        g = [0.25 * d for d in dz]
        dp2 = [-hi(z_ref[n, h], g[h], 0, 0) for h in heads]
        dz = [hi(g[h], t3_ref[n, h], 1, 1) for h in heads]
        dp1 = [-hi(x[h], dp2[h], 0, 0) for h in heads]
        dx = [hi(dp2[h], t2_ref[n, h], 1, 1) for h in heads]
        dt1 = [hi(x[h], dp1[h], 0, 0) for h in heads]
        dx = [dx[h] + hi(dp1[h], 7.0 * eye - x[h], 1, 1) - dt1[h] for h in heads]
        dz = [dz[h] + hi(a_ref[h], dx[h], 0, 0) for h in heads]
        da = [da[h] + hi(dx[h], z_ref[n, h], 1, 1) for h in heads]
    mx = mx_ref[...]
    denom = mx[0:1, 0:1] * mx[4:5, 0:1]
    row = lax.broadcasted_iota(jnp.int32, (M, HEAD_SIZE), 0)
    for h in heads:
        d = da[h] + dz[h].T / denom
        a = a_ref[h]
        dsa = a * (d - jnp.sum(d * a, axis=1, keepdims=True))
        dqt = hi(dsa, t_ref[h, M:]) * SCALE
        dkt = hi(dsa, t_ref[h, :M], 0, 0) * SCALE
        for i, x in enumerate((dqt, dkt)):
            for s in range(2):
                mine = jnp.where(row == own_ref[0] + s * S, x, 0.0)
                r = 8 * i + 2 * h + s
                o_ref[r : r + 1, :] = jnp.sum(mine, axis=0, keepdims=True)


def final_kernel(dq_ref, dsb_ref, t_ref, got_ref, add_ref, q_out, k_out, tot_ref):
    i = pl.program_id(0)

    @pl.when(i == 0)
    def _():
        tot_ref[...] = (jnp.sum(got_ref[...], axis=0) + add_ref[...]) / (T // 2)

    s = i // 2
    for h in range(H):
        cols = slice(h * HEAD_SIZE, (h + 1) * HEAD_SIZE)
        add = tot_ref[pl.ds(2 * h + s, 1), :]
        q_out[:, cols] = (dq_ref[:, cols] + add).astype(BF16)
        dk = dot(dsb_ref[h * M : (h + 1) * M, :], t_ref[h, :M].astype(BF16), 0, 0) * SCALE
        add = tot_ref[pl.ds(8 + 2 * h + s, 1), :]
        k_out[:, cols] = (dk + add).astype(BF16)


def weight_kernel(*refs):
    gs, wf_ref, o_ref = refs[:Y], refs[Y], refs[Y + 1]
    for h in range(H):
        rows = slice(h * M, (h + 1) * M)
        a, b, c, d = (ref[rows, :] for ref in gs)
        o_ref[:, h * HEAD_SIZE : (h + 1) * HEAD_SIZE] = dot(
            (a + b) + (c + d), wf_ref[rows, :], 0, 0, HIGHEST
        )


def to_all(x, axes, n):
    return lax.all_to_all(jnp.broadcast_to(x[None], (n,) + x.shape), axes, 0, 0, tiled=True)


def gather_rows(x, means):
    here = lax.axis_index("y")
    x, means = lax.optimization_barrier((x, means))
    blocks = [
        lax.ppermute(x, "y", [(i, (i + step) % Y) for i in range(Y)]) for step in range(1, Y)
    ]
    out = jnp.zeros((Y,) + x.shape, x.dtype)
    out = lax.dynamic_update_index_in_dim(out, x, here, 0)
    for step, block in enumerate(blocks, 1):
        out = lax.dynamic_update_index_in_dim(out, block, (here - step) % Y, 0)
    return out.reshape(Y * x.shape[0], x.shape[1]), means


RIGHT = [(i, (i + 1) % X) for i in range(X)]
LEFT = [(i, (i - 1) % X) for i in range(X)]
OTHER = [(0, 1), (1, 0)]
FAR = [(i * C + c, (i + 1 - 2 * c) % X * C + c) for i in range(X) for c in range(C)]


def places():
    px, pc = lax.axis_index("x"), lax.axis_index("core")
    out = []
    for step in (0, -1, 1, 2):
        for core in (pc, 1 - pc):
            out.append(((px + step) % X) * C + core)
    return jnp.stack(out).astype(jnp.int32)


def local(queries, keys, values, out_weight, out_grad):
    full = lambda *shape: spec(shape)
    smem = pl.BlockSpec(memory_space=pltpu.SMEM)
    half = spec((T // 2, W), lambda s: (s, 0))
    slab = spec((T // 4, W), lambda i: (i, 0))
    means = call(
        means_kernel, "means", (2,), [half, half], spec((1, 8, HEAD_SIZE), lambda s: (s, 0, 0)),
        sds((2, 8, HEAD_SIZE)), 2,
    )(queries, keys)
    weight, means = gather_rows(out_weight, means)
    weight = lax.all_gather(weight, "z", axis=0, tiled=True)
    out_grad, means = lax.optimization_barrier((out_grad, means))
    tiles = to_all(means.reshape(16, HEAD_SIZE), SEQ, S)
    right = lax.ppermute(out_grad, "x", RIGHT)
    left = lax.ppermute(out_grad, "x", LEFT)
    beside = lax.ppermute(out_grad, "core", OTHER)
    right, left, tiles = lax.optimization_barrier((right, left, tiles))
    far = jnp.where(lax.axis_index("core") == 0, right, left)
    right, left, far = lax.optimization_barrier((right, left, far))
    far = lax.ppermute(far, HEAD, FAR)
    right2, left2 = lax.ppermute(right, "core", OTHER), lax.ppermute(left, "core", OTHER)
    tiles = tiles.reshape(S, 2, 2, H, HEAD_SIZE).transpose(3, 2, 1, 0, 4)
    tiles = tiles.reshape(H, 2 * M, HEAD_SIZE)

    f, fb, e, sent, stats, a, tops = call(
        scores_kernel, "scores", (H,), [COLS, COLS, COLS, TILE],
        [ROWS, ROWS, ROWS, spec((8, 16, HEAD_SIZE), lambda h: (h, 0, 0)), LAND, SQUARE, full(8, HEAD_SIZE)],
        [sds((H * M, T)), sds((H * M, T), BF16), sds((H * M, T)), sds((S, 16, HEAD_SIZE)),
         sds((H * M, HEAD_SIZE)), sds((H, M, M)), sds((8, HEAD_SIZE))], 60,
    )(queries, keys, values, tiles)

    blocks = [out_grad, beside, right, right2, left, left2]
    where = places()

    got = lax.all_to_all(sent, SEQ, 0, 0, tiled=True)
    wide = spec((T, 256), lambda i: (0, i))
    g = call(
        outer_kernel, "outer", (2,), [smem, full(H * M, T)] + [wide] * 6,
        spec((Z, 2, H * M, 128), lambda i: (0, i, 0, 0)), sds((Z, Y, H * M, 128)), 20,
    )(where, fb, *blocks)
    g, far, tops = lax.optimization_barrier((g, far, tops))
    far2 = lax.ppermute(far, "core", OTHER)
    tops = jnp.maximum(tops, lax.ppermute(tops, "core", OTHER))
    ahead = [lax.ppermute(tops, "x", [(i, (i + n) % X) for i in range(X)]) for n in range(1, X)]
    tops = jnp.maximum(jnp.maximum(tops, ahead[0]), jnp.maximum(ahead[1], ahead[2]))
    g = pl.pallas_call(
        outer_far_kernel,
        grid_spec=pltpu.PrefetchScalarGridSpec(
            num_scalar_prefetch=1,
            grid=(2,),
            in_specs=[
                pl.BlockSpec((H * M, T), lambda i, j: (0, 0)),
                pl.BlockSpec((T, W), lambda i, j: (0, 0)),
                pl.BlockSpec((T, W), lambda i, j: (0, 0)),
                pl.BlockSpec(memory_space=pl.ANY),
            ],
            out_specs=pl.BlockSpec((1, Y, H * M, 128), lambda i, j: (j[6 + i], 0, 0, 0)),
        ),
        out_shape=sds((Z, Y, H * M, 128)),
        input_output_aliases={4: 0},
        name="outer_far",
        compiler_params=pltpu.CompilerParams(vmem_limit_bytes=int(63.9 * 2**20)),
        cost_estimate=pl.CostEstimate(flops=10**9, bytes_accessed=1 << 20, transcendentals=0),
    )(where, fb, far, far2, g)
    g, got, tops = lax.optimization_barrier((g, got, tops))
    merged = call(
        merge_kernel, "merge", (1,), [full(S, 16, HEAD_SIZE)], full(S, 16, HEAD_SIZE),
        sds((S, 16, HEAD_SIZE)), 1,
    )(got)
    land = lax.all_to_all(merged, SEQ, 0, 0, tiled=True)
    g = lax.psum_scatter(g, "z", scatter_dimension=0, tiled=True).reshape(Y, H * M, 128)

    tokens = 512
    panel = spec((H * M, tokens), lambda i: (0, i))
    block = spec((tokens, W), lambda i: (i, 0))
    do, sent = call(
        cotangent_kernel, "cotangent", (T // tokens,),
        [smem, full(Z * Y * 128, W), panel] + [block] * 8,
        [block, full(S, 8, HEAD_SIZE)], [sds((T, W), BF16), sds((S, 8, HEAD_SIZE))], 10,
    )(where, weight, fb, *blocks, far, far2)

    land, sent, tops = lax.optimization_barrier((land, sent, tops))
    inverse, xs, t2, t3 = call(
        newton_kernel, "newton", (1,), [full(H, M, M), full(8, HEAD_SIZE)],
        [full(NEWTON + 1, H, M, M)] + [full(NEWTON, H, M, M)] * 3,
        [sds((NEWTON + 1, H, M, M))] + [sds((NEWTON, H, M, M))] * 3, 6,
    )(a, tops)

    got = lax.all_to_all(sent, SEQ, 0, 0, tiled=True)
    sent = call(
        spread_kernel, "spread", (1,), [full(S, 8, HEAD_SIZE)], full(S, 8, HEAD_SIZE), sds((S, 8, HEAD_SIZE)), 1
    )(got)
    dw = lax.all_to_all(sent, SEQ, 0, 0, tiled=True)

    parts = spec((8, 16, HEAD_SIZE), lambda h: (h, 0, 0))
    last = spec((1, 1, M, M), lambda h: (NEWTON, h, 0, 0))
    dq, dktf, wf = call(
        query_panel_kernel, "query_panel", (H,), [COLS, COLS, TILE, ROWS, parts, last],
        [COLS, full(S, 8, HEAD_SIZE), LAND], [sds((T, W)), sds((S, 8, HEAD_SIZE)), sds((H * M, HEAD_SIZE))], 5,
    )(queries, do, tiles, f, land, inverse)
    dsb, bb, dbv, sent = call(
        key_panel_kernel, "key_panel", (H,),
        [COLS, COLS, ROWS, LAND, parts, spec((8, 8, HEAD_SIZE), lambda h: (h, 0, 0)), last,
         full(S, 8, HEAD_SIZE)],
        [ROWS, ROWS, LAND, full(S, 16, HEAD_SIZE)],
        [sds((H * M, T), BF16), sds((H * M, T), BF16), sds((H * M, HEAD_SIZE), BF16),
         sds((S, 16, HEAD_SIZE))], 4,
    )(keys, values, e, stats, land, dw, inverse, dktf)
    dv = call(
        value_rows_kernel, "value_rows", (H,), [ROWS, LAND], COLS, sds((T, W), BF16), 2
    )(bb, dbv)

    g, dsb = lax.optimization_barrier((g, dsb))
    here = lax.axis_index("y")
    gs = [lax.dynamic_index_in_dim(g, (here + n) % Y, keepdims=False) for n in range(Y)]
    gs[1:] = [
        lax.ppermute(gs[n], "y", [(i, (i + n) % Y) for i in range(Y)]) for n in range(1, Y)
    ]
    summed = lax.all_to_all(sent, SEQ, 0, 0, tiled=True)
    own = lax.axis_index(SEQ).astype(jnp.int32).reshape(1)
    da = call(
        adjoint_kernel, "adjoint", (1,),
        [smem, full(S, 8, HEAD_SIZE), full(S, 16, HEAD_SIZE), full(8, HEAD_SIZE), full(H, M, M),
         full(NEWTON + 1, H, M, M)] + [full(NEWTON, H, M, M)] * 3 + [full(H, 2 * M, HEAD_SIZE)],
        full(16, HEAD_SIZE), sds((16, HEAD_SIZE)), 9,
    )(own, dw, land, tops, a, inverse, xs, t2, t3, tiles)
    query_grad, key_grad = call(
        final_kernel, "final", (4,), [slab, spec((H * M, T // 4), lambda i: (0, i)),
         full(H, 2 * M, HEAD_SIZE), full(S, 16, HEAD_SIZE), full(16, HEAD_SIZE)],
        [slab, slab], [sds((T, W), BF16)] * 2, 2, [pltpu.VMEM((16, HEAD_SIZE), F32)],
    )(dq, dsb, tiles, summed, da)
    weight_grad = call(
        weight_kernel, "weight", (1,), [full(H * M, 128)] * Y + [full(H * M, HEAD_SIZE)], full(128, W), sds((128, W)), 2,
    )(*gs, wf)
    return query_grad, key_grad, dv, weight_grad


def solution(mesh):
    grid = Mesh(mesh.devices.reshape(Z, Y, X, C), SEQ + HEAD)
    place = P(SEQ, HEAD)
    return jax.shard_map(
        local, mesh=grid, in_specs=(place,) * 5, out_specs=(place,) * 4, check_vma=False
    )
```

```python
import jax
import jax.numpy as jnp
from jax import lax
from jax.experimental import pallas as pl
from jax.experimental.pallas import tpu as pltpu
from jax.sharding import Mesh
from jax.sharding import PartitionSpec as P

HEAD_SIZE = 128
M = 64
NEWTON = 6
SCALE = HEAD_SIZE**-0.5
HIGHEST = lax.Precision.HIGHEST
F32 = jnp.float32
BF16 = jnp.bfloat16

Z, Y, X, C = 8, 4, 4, 2
SEQ = ("z", "y")
HEAD = ("x", "core")
S = Z * Y
H = 4
T = 1024
W = H * HEAD_SIZE


def dot(a, b, ca=1, cb=0, precision=None):
    return lax.dot_general(
        a, b, (((ca,), (cb,)), ((), ())), preferred_element_type=F32, precision=precision
    )


def parts_of(x):
    hi = x.astype(BF16)
    rest = x - hi.astype(F32)
    mid = rest.astype(BF16)
    lo = (rest - mid.astype(F32)).astype(BF16)
    return hi, mid, lo


def wide_dot(x, y, ca=1, cb=0):
    hi, mid, lo = parts_of(x)
    return dot(hi, y, ca, cb) + (dot(mid, y, ca, cb) + dot(lo, y, ca, cb))


def close_dot(x, y, ca=1, cb=0):
    xh, yh = x.astype(BF16), y.astype(BF16)
    xl = (x - xh.astype(F32)).astype(BF16)
    yl = (y - yh.astype(F32)).astype(BF16)
    return dot(xh, yh, ca, cb) + (dot(xh, yl, ca, cb) + dot(xl, yh, ca, cb))


def call(kernel, name, grid, in_specs, out_specs, out_shape, cost, scratch=(), vmem=63.9):
    return pl.pallas_call(
        kernel,
        grid=grid,
        in_specs=in_specs,
        out_specs=out_specs,
        out_shape=out_shape,
        scratch_shapes=scratch,
        name=name,
        compiler_params=pltpu.CompilerParams(vmem_limit_bytes=int(vmem * 2**20)),
        cost_estimate=pl.CostEstimate(
            flops=int(cost * 1e9), bytes_accessed=1 << 20, transcendentals=0
        ),
    )


def spec(shape, index=None):
    if index is None:
        index = lambda h, n=len(shape): (0,) * n
    return pl.BlockSpec(shape, index)


def sds(shape, dtype=F32):
    return jax.ShapeDtypeStruct(shape, dtype)


COLS = spec((T, HEAD_SIZE), lambda h: (0, h))
ROWS = spec((M, T), lambda h: (h, 0))
LAND = spec((M, HEAD_SIZE), lambda h: (h, 0))
TILE = spec((1, 2 * M, HEAD_SIZE), lambda h: (h, 0, 0))
SQUARE = spec((1, M, M), lambda h: (h, 0, 0))


def means_kernel(q_ref, k_ref, o_ref):
    for i, ref in enumerate((q_ref, k_ref)):
        mean = jnp.sum(ref[...].astype(F32), axis=0, keepdims=True) / ref.shape[0]
        for h in range(H):
            o_ref[0, H * i + h : H * i + h + 1, :] = mean[:, h * HEAD_SIZE : (h + 1) * HEAD_SIZE]


def scores_kernel(q_ref, k_ref, v_ref, t_ref, f_ref, fb_ref, e_ref, sent_ref, st_ref, a_ref, mx_ref):
    qt, kt = t_ref[0, :M], t_ref[0, M:]
    s1 = dot(kt.astype(BF16), q_ref[...], 1, 1) * SCALE
    p = jnp.exp(s1 - jnp.max(s1, axis=0, keepdims=True))
    f = p / jnp.sum(p, axis=0, keepdims=True)
    f_ref[...] = f
    fb_ref[...] = f.astype(BF16)
    s2 = dot(qt.astype(BF16), k_ref[...], 1, 1) * SCALE
    top = jnp.max(s2, axis=1, keepdims=True)
    e = jnp.exp(s2 - top)
    e_ref[...] = e
    total = jnp.sum(e, axis=1, keepdims=True)
    sent_ref[:, :8] = wide_dot(e, v_ref[...]).reshape(8, 8, HEAD_SIZE)
    lane = lax.broadcasted_iota(jnp.int32, (M, HEAD_SIZE), 1)
    stats = jnp.where(lane < M, top, total)
    st_ref[...] = stats
    sent_ref[:, 8:] = stats.reshape(8, 8, HEAD_SIZE)
    sa = dot(qt, kt, 1, 1, HIGHEST) * SCALE
    pa = jnp.exp(sa - jnp.max(sa, axis=1, keepdims=True))
    a = pa / jnp.sum(pa, axis=1, keepdims=True)
    a_ref[0] = a
    col = jnp.max(jnp.sum(a, axis=0, keepdims=True), axis=1, keepdims=True)
    row = jnp.max(jnp.sum(a, axis=1, keepdims=True), axis=0, keepdims=True)
    sub = lax.broadcasted_iota(jnp.int32, (8, HEAD_SIZE), 0)
    both = jnp.where(sub < 4, col, row)

    @pl.when(pl.program_id(0) == 0)
    def _():
        mx_ref[...] = both

    @pl.when(pl.program_id(0) > 0)
    def _():
        mx_ref[...] = jnp.maximum(mx_ref[...], both)


def newton_kernel(a_ref, mx_ref, z_ref, x_ref, t2_ref, t3_ref):
    eye = (
        lax.broadcasted_iota(jnp.int32, (M, M), 0) == lax.broadcasted_iota(jnp.int32, (M, M), 1)
    ).astype(F32)
    mx = mx_ref[...]
    denom = mx[0:1, 0:1] * mx[4:5, 0:1]
    zs = []
    for h in range(H):
        z = a_ref[h].T / denom
        z_ref[0, h] = z
        zs.append(z)
    for n in range(NEWTON):
        xs = [dot(a_ref[h], zs[h], precision=HIGHEST) for h in range(H)]
        t2 = [15.0 * eye - dot(x, 7.0 * eye - x, precision=HIGHEST) for x in xs]
        t3 = [13.0 * eye - dot(x, t, precision=HIGHEST) for x, t in zip(xs, t2)]
        zs = [0.25 * dot(z, t, precision=HIGHEST) for z, t in zip(zs, t3)]
        for h in range(H):
            x_ref[n, h] = xs[h]
            t2_ref[n, h] = t2[h]
            t3_ref[n, h] = t3[h]
            z_ref[n + 1, h] = zs[h]


def merge_kernel(r_ref, o_ref):
    v, st = r_ref[:, :8, :], r_ref[:, 8:, :]
    top, total = st[:, :, 0:1], st[:, :, M : M + 1]
    mx = jnp.max(top, axis=0, keepdims=True)
    scale = jnp.exp(top - mx)
    whole = jnp.sum(scale * total, axis=0)
    lane = lax.broadcasted_iota(jnp.int32, (8, HEAD_SIZE), 1)
    o_ref[:, :8] = jnp.broadcast_to((jnp.sum(scale * v, axis=0) / whole)[None], (S, 8, HEAD_SIZE))
    o_ref[:, 8:] = jnp.broadcast_to(jnp.where(lane < M, mx[0], whole)[None], (S, 8, HEAD_SIZE))


def outer_kernel(j_ref, fb_ref, *refs):
    ogs, out = refs[:-1], refs[-1]
    for b, og in enumerate(ogs):
        res = dot(fb_ref[...], og[...])
        for y in range(2):
            out[j_ref[b], y] = res[:, y * 128 : (y + 1) * 128]


def outer_far_kernel(j_ref, fb_ref, far_ref, far2_ref, g_ref, out_ref):
    for i, og in enumerate((far_ref, far2_ref)):

        @pl.when(pl.program_id(0) == i)
        def _(og=og):
            res = dot(fb_ref[...], og[...])
            for y in range(Y):
                out_ref[0, y] = res[:, y * 128 : (y + 1) * 128]


def cotangent_kernel(j_ref, w_ref, fb_ref, *refs):
    ogs, do_ref, sent_ref = refs[:8], refs[8], refs[9]
    i = pl.program_id(0)
    acc = None
    for b in range(8):
        at = pl.multiple_of(j_ref[b] * W, W)
        part = dot(ogs[b][...], w_ref[pl.ds(at, W), :])
        acc = part if acc is None else acc + part
    do = acc.astype(BF16)
    do_ref[...] = do

    @pl.when(i == 0)
    def _():
        sent_ref[...] = jnp.zeros((S, 8, HEAD_SIZE), F32)

    for h in range(H):
        part = dot(fb_ref[h * M : (h + 1) * M, :], do[:, h * HEAD_SIZE : (h + 1) * HEAD_SIZE])
        sent_ref[8 * h : 8 * h + 8] += part.reshape(8, 8, HEAD_SIZE)


def spread_kernel(r_ref, o_ref):
    o_ref[...] = jnp.broadcast_to(jnp.sum(r_ref[...], axis=0)[None], (S, 8, HEAD_SIZE))


def put_rows(ref, x):
    for s in range(2):
        ref[:, pl.ds(2 * pl.program_id(0) + s, 1), :] = x[s * S : (s + 1) * S][:, None, :]


def query_panel_kernel(q_ref, do_ref, t_ref, f_ref, got_ref, z_ref, dq_ref, dt_ref, wf_ref):
    ktb = t_ref[0, M:].astype(BF16)
    bv = got_ref[:, :8].reshape(M, HEAD_SIZE)
    wf = dot(z_ref[0, 0], bv, precision=HIGHEST)
    wf_ref[...] = wf
    f = f_ref[...]
    df = wide_dot(wf, do_ref[...], 1, 1)
    dsf = (f * (df - jnp.sum(df * f, axis=0, keepdims=True))).astype(BF16)
    put_rows(dt_ref, dot(dsf, q_ref[...]) * SCALE)
    dq_ref[...] = dot(dsf, ktb, 0, 0) * SCALE


def key_panel_kernel(
    k_ref, v_ref, e_ref, st_ref, got_ref, dw_ref, z_ref, dt_ref, dsb_ref, bb_ref, dbv_ref, sent_ref
):
    dw = dw_ref[...].reshape(M, HEAD_SIZE)
    bv = got_ref[:, :8].reshape(M, HEAD_SIZE)
    whole = got_ref[:, 8:].reshape(M, HEAD_SIZE)
    dbv = dot(z_ref[0, 0], dw, 0, 0, HIGHEST).astype(BF16)
    dbv_ref[...] = dbv
    db = dot(dbv, v_ref[...], 1, 1)
    beta = jnp.sum(dbv.astype(F32) * bv, axis=1, keepdims=True)
    rescale = jnp.exp(st_ref[:, 0:1] - whole[:, 0:1]) / whole[:, M : M + 1]
    bf = e_ref[...] * rescale
    dsb = (bf * (db - beta)).astype(BF16)
    dsb_ref[...] = dsb
    bb_ref[...] = bf.astype(BF16)
    put_rows(sent_ref, dot(dsb, k_ref[...]) * SCALE)

    @pl.when(pl.program_id(0) == 0)
    def _():
        sent_ref[:, 8:] = dt_ref[...]


def adjoint_kernel(
    own_ref, bb_ref, dbv_ref, dw_ref, got_ref, mx_ref, a_ref, z_ref, x_ref, t2_ref, t3_ref, t_ref,
    o_ref, dv_ref,
):
    eye = (
        lax.broadcasted_iota(jnp.int32, (M, M), 0) == lax.broadcasted_iota(jnp.int32, (M, M), 1)
    ).astype(F32)
    hi = close_dot
    heads = range(H)
    dz = []
    for h in heads:
        dw = dw_ref[8 * h : 8 * h + 8].reshape(M, HEAD_SIZE)
        bv = got_ref[8 * h : 8 * h + 8, :8].reshape(M, HEAD_SIZE)
        dz.append(hi(dw, bv, 1, 1))
    da = [jnp.zeros((M, M), F32) for h in heads]
    for n in reversed(range(NEWTON)):
        if n < H:
            rows, cols = slice(n * M, (n + 1) * M), slice(n * HEAD_SIZE, (n + 1) * HEAD_SIZE)
            dv_ref[:, cols] = dot(bb_ref[rows, :], dbv_ref[rows, :], 0, 0).astype(BF16)
        x = [x_ref[n, h] for h in heads]
        g = [0.25 * d for d in dz]
        dp2 = [-hi(z_ref[n, h], g[h], 0, 0) for h in heads]
        dz = [hi(g[h], t3_ref[n, h], 1, 1) for h in heads]
        dp1 = [-hi(x[h], dp2[h], 0, 0) for h in heads]
        dx = [hi(dp2[h], t2_ref[n, h], 1, 1) for h in heads]
        dt1 = [hi(x[h], dp1[h], 0, 0) for h in heads]
        dx = [dx[h] + hi(dp1[h], 7.0 * eye - x[h], 1, 1) - dt1[h] for h in heads]
        dz = [dz[h] + hi(a_ref[h], dx[h], 0, 0) for h in heads]
        da = [da[h] + hi(dx[h], z_ref[n, h], 1, 1) for h in heads]
    mx = mx_ref[...]
    denom = mx[0:1, 0:1] * mx[4:5, 0:1]
    row = lax.broadcasted_iota(jnp.int32, (M, HEAD_SIZE), 0)
    for h in heads:
        d = da[h] + dz[h].T / denom
        a = a_ref[h]
        dsa = a * (d - jnp.sum(d * a, axis=1, keepdims=True))
        dqt = hi(dsa, t_ref[h, M:]) * SCALE
        dkt = hi(dsa, t_ref[h, :M], 0, 0) * SCALE
        for i, x in enumerate((dqt, dkt)):
            for s in range(2):
                mine = jnp.where(row == own_ref[0] + s * S, x, 0.0)
                r = 8 * i + 2 * h + s
                o_ref[r : r + 1, :] = jnp.sum(mine, axis=0, keepdims=True)


def final_kernel(dq_ref, dsb_ref, t_ref, got_ref, add_ref, q_out, k_out, tot_ref):
    i = pl.program_id(0)

    @pl.when(i == 0)
    def _():
        tot_ref[...] = (jnp.sum(got_ref[...], axis=0) + add_ref[...]) / (T // 2)

    s = i // 2
    for h in range(H):
        cols = slice(h * HEAD_SIZE, (h + 1) * HEAD_SIZE)
        add = tot_ref[pl.ds(2 * h + s, 1), :]
        q_out[:, cols] = (dq_ref[:, cols] + add).astype(BF16)
        dk = dot(dsb_ref[h * M : (h + 1) * M, :], t_ref[h, :M].astype(BF16), 0, 0) * SCALE
        add = tot_ref[pl.ds(8 + 2 * h + s, 1), :]
        k_out[:, cols] = (dk + add).astype(BF16)


def weight_kernel(*refs):
    gs, wf_ref, o_ref = refs[:Y], refs[Y], refs[Y + 1]
    for h in range(H):
        rows = slice(h * M, (h + 1) * M)
        a, b, c, d = (ref[rows, :] for ref in gs)
        o_ref[:, h * HEAD_SIZE : (h + 1) * HEAD_SIZE] = dot(
            (a + b) + (c + d), wf_ref[rows, :], 0, 0, HIGHEST
        )


def to_all(x, axes, n):
    return lax.all_to_all(jnp.broadcast_to(x[None], (n,) + x.shape), axes, 0, 0, tiled=True)


def gather_rows(x, means):
    here = lax.axis_index("y")
    x, means = lax.optimization_barrier((x, means))
    blocks = [
        lax.ppermute(x, "y", [(i, (i + step) % Y) for i in range(Y)]) for step in range(1, Y)
    ]
    out = jnp.zeros((Y,) + x.shape, x.dtype)
    out = lax.dynamic_update_index_in_dim(out, x, here, 0)
    for step, block in enumerate(blocks, 1):
        out = lax.dynamic_update_index_in_dim(out, block, (here - step) % Y, 0)
    return out.reshape(Y * x.shape[0], x.shape[1]), means


RIGHT = [(i, (i + 1) % X) for i in range(X)]
LEFT = [(i, (i - 1) % X) for i in range(X)]
OTHER = [(0, 1), (1, 0)]
FAR = [(i * C + c, (i + 1 - 2 * c) % X * C + c) for i in range(X) for c in range(C)]


def places():
    px, pc = lax.axis_index("x"), lax.axis_index("core")
    out = []
    for step in (0, -1, 1, 2):
        for core in (pc, 1 - pc):
            out.append(((px + step) % X) * C + core)
    return jnp.stack(out).astype(jnp.int32)


def local(queries, keys, values, out_weight, out_grad):
    full = lambda *shape: spec(shape)
    smem = pl.BlockSpec(memory_space=pltpu.SMEM)
    half = spec((T // 2, W), lambda s: (s, 0))
    slab = spec((T // 4, W), lambda i: (i, 0))
    means = call(
        means_kernel, "means", (2,), [half, half], spec((1, 8, HEAD_SIZE), lambda s: (s, 0, 0)),
        sds((2, 8, HEAD_SIZE)), 2,
    )(queries, keys)
    weight, means = gather_rows(out_weight, means)
    weight = lax.all_gather(weight, "z", axis=0, tiled=True)
    out_grad, means = lax.optimization_barrier((out_grad, means))
    tiles = to_all(means.reshape(16, HEAD_SIZE), SEQ, S)
    right = lax.ppermute(out_grad, "x", RIGHT)
    left = lax.ppermute(out_grad, "x", LEFT)
    right, left, out_grad, tiles = lax.optimization_barrier((right, left, out_grad, tiles))
    beside = lax.ppermute(out_grad, "core", OTHER)
    far = jnp.where(lax.axis_index("core") == 0, right, left)
    right, left, far = lax.optimization_barrier((right, left, far))
    far = lax.ppermute(far, HEAD, FAR)
    right2, left2 = lax.ppermute(right, "core", OTHER), lax.ppermute(left, "core", OTHER)
    tiles = tiles.reshape(S, 2, 2, H, HEAD_SIZE).transpose(3, 2, 1, 0, 4)
    tiles = tiles.reshape(H, 2 * M, HEAD_SIZE)

    f, fb, e, sent, stats, a, tops = call(
        scores_kernel, "scores", (H,), [COLS, COLS, COLS, TILE],
        [ROWS, ROWS, ROWS, spec((8, 16, HEAD_SIZE), lambda h: (h, 0, 0)), LAND, SQUARE, full(8, HEAD_SIZE)],
        [sds((H * M, T)), sds((H * M, T), BF16), sds((H * M, T)), sds((S, 16, HEAD_SIZE)),
         sds((H * M, HEAD_SIZE)), sds((H, M, M)), sds((8, HEAD_SIZE))], 60,
    )(queries, keys, values, tiles)

    blocks = [out_grad, beside, right, right2, left, left2]
    where = places()

    got = lax.all_to_all(sent, SEQ, 0, 0, tiled=True)
    wide = spec((T, 256), lambda i: (0, i))
    g = call(
        outer_kernel, "outer", (2,), [smem, full(H * M, T)] + [wide] * 6,
        spec((Z, 2, H * M, 128), lambda i: (0, i, 0, 0)), sds((Z, Y, H * M, 128)), 20,
    )(where, fb, *blocks)
    g, far, tops = lax.optimization_barrier((g, far, tops))
    far2 = lax.ppermute(far, "core", OTHER)
    tops = jnp.maximum(tops, lax.ppermute(tops, "core", OTHER))
    ahead = [lax.ppermute(tops, "x", [(i, (i + n) % X) for i in range(X)]) for n in range(1, X)]
    tops = jnp.maximum(jnp.maximum(tops, ahead[0]), jnp.maximum(ahead[1], ahead[2]))
    g = pl.pallas_call(
        outer_far_kernel,
        grid_spec=pltpu.PrefetchScalarGridSpec(
            num_scalar_prefetch=1,
            grid=(2,),
            in_specs=[
                pl.BlockSpec((H * M, T), lambda i, j: (0, 0)),
                pl.BlockSpec((T, W), lambda i, j: (0, 0)),
                pl.BlockSpec((T, W), lambda i, j: (0, 0)),
                pl.BlockSpec(memory_space=pl.ANY),
            ],
            out_specs=pl.BlockSpec((1, Y, H * M, 128), lambda i, j: (j[6 + i], 0, 0, 0)),
        ),
        out_shape=sds((Z, Y, H * M, 128)),
        input_output_aliases={4: 0},
        name="outer_far",
        compiler_params=pltpu.CompilerParams(vmem_limit_bytes=int(63.9 * 2**20)),
        cost_estimate=pl.CostEstimate(flops=10**9, bytes_accessed=1 << 20, transcendentals=0),
    )(where, fb, far, far2, g)
    g, got, tops = lax.optimization_barrier((g, got, tops))
    merged = call(
        merge_kernel, "merge", (1,), [full(S, 16, HEAD_SIZE)], full(S, 16, HEAD_SIZE),
        sds((S, 16, HEAD_SIZE)), 1,
    )(got)
    land = lax.all_to_all(merged, SEQ, 0, 0, tiled=True)
    g = lax.psum_scatter(g, "z", scatter_dimension=0, tiled=True).reshape(Y, H * M, 128)

    tokens = 512
    panel = spec((H * M, tokens), lambda i: (0, i))
    block = spec((tokens, W), lambda i: (i, 0))
    do, sent = call(
        cotangent_kernel, "cotangent", (T // tokens,),
        [smem, full(Z * Y * 128, W), panel] + [block] * 8,
        [block, full(S, 8, HEAD_SIZE)], [sds((T, W), BF16), sds((S, 8, HEAD_SIZE))], 10,
    )(where, weight, fb, *blocks, far, far2)

    land, sent, tops = lax.optimization_barrier((land, sent, tops))
    inverse, xs, t2, t3 = call(
        newton_kernel, "newton", (1,), [full(H, M, M), full(8, HEAD_SIZE)],
        [full(NEWTON + 1, H, M, M)] + [full(NEWTON, H, M, M)] * 3,
        [sds((NEWTON + 1, H, M, M))] + [sds((NEWTON, H, M, M))] * 3, 6,
    )(a, tops)

    got = lax.all_to_all(sent, SEQ, 0, 0, tiled=True)
    sent = call(
        spread_kernel, "spread", (1,), [full(S, 8, HEAD_SIZE)], full(S, 8, HEAD_SIZE), sds((S, 8, HEAD_SIZE)), 1
    )(got)
    dw = lax.all_to_all(sent, SEQ, 0, 0, tiled=True)

    parts = spec((8, 16, HEAD_SIZE), lambda h: (h, 0, 0))
    last = spec((1, 1, M, M), lambda h: (NEWTON, h, 0, 0))
    dq, dktf, wf = call(
        query_panel_kernel, "query_panel", (H,), [COLS, COLS, TILE, ROWS, parts, last],
        [COLS, full(S, 8, HEAD_SIZE), LAND], [sds((T, W)), sds((S, 8, HEAD_SIZE)), sds((H * M, HEAD_SIZE))], 5,
    )(queries, do, tiles, f, land, inverse)
    dsb, bb, dbv, sent = call(
        key_panel_kernel, "key_panel", (H,),
        [COLS, COLS, ROWS, LAND, parts, spec((8, 8, HEAD_SIZE), lambda h: (h, 0, 0)), last,
         full(S, 8, HEAD_SIZE)],
        [ROWS, ROWS, LAND, full(S, 16, HEAD_SIZE)],
        [sds((H * M, T), BF16), sds((H * M, T), BF16), sds((H * M, HEAD_SIZE), BF16),
         sds((S, 16, HEAD_SIZE))], 4,
    )(keys, values, e, stats, land, dw, inverse, dktf)
    g, dsb = lax.optimization_barrier((g, dsb))
    here = lax.axis_index("y")
    gs = [lax.dynamic_index_in_dim(g, (here + n) % Y, keepdims=False) for n in range(Y)]
    gs[1:] = [
        lax.ppermute(gs[n], "y", [(i, (i + n) % Y) for i in range(Y)]) for n in range(1, Y)
    ]
    summed = lax.all_to_all(sent, SEQ, 0, 0, tiled=True)
    own = lax.axis_index(SEQ).astype(jnp.int32).reshape(1)
    da, dv = call(
        adjoint_kernel, "adjoint", (1,),
        [smem, full(H * M, T), full(H * M, HEAD_SIZE), full(S, 8, HEAD_SIZE), full(S, 16, HEAD_SIZE), full(8, HEAD_SIZE), full(H, M, M),
         full(NEWTON + 1, H, M, M)] + [full(NEWTON, H, M, M)] * 3 + [full(H, 2 * M, HEAD_SIZE)],
        [full(16, HEAD_SIZE), full(T, W)], [sds((16, HEAD_SIZE)), sds((T, W), BF16)], 11,
    )(own, bb, dbv, dw, land, tops, a, inverse, xs, t2, t3, tiles)
    query_grad, key_grad = call(
        final_kernel, "final", (4,), [slab, spec((H * M, T // 4), lambda i: (0, i)),
         full(H, 2 * M, HEAD_SIZE), full(S, 16, HEAD_SIZE), full(16, HEAD_SIZE)],
        [slab, slab], [sds((T, W), BF16)] * 2, 2, [pltpu.VMEM((16, HEAD_SIZE), F32)],
    )(dq, dsb, tiles, summed, da)
    weight_grad = call(
        weight_kernel, "weight", (1,), [full(H * M, 128)] * Y + [full(H * M, HEAD_SIZE)], full(128, W), sds((128, W)), 2,
    )(*gs, wf)
    return query_grad, key_grad, dv, weight_grad


def solution(mesh):
    grid = Mesh(mesh.devices.reshape(Z, Y, X, C), SEQ + HEAD)
    place = P(SEQ, HEAD)
    return jax.shard_map(
        local, mesh=grid, in_specs=(place,) * 5, out_specs=(place,) * 4, check_vma=False
    )
```

```python
import jax
import jax.numpy as jnp
from jax import lax
from jax.experimental import pallas as pl
from jax.experimental.pallas import tpu as pltpu
from jax.sharding import Mesh
from jax.sharding import PartitionSpec as P

HEAD_SIZE = 128
M = 64
NEWTON = 6
SCALE = HEAD_SIZE**-0.5
HIGHEST = lax.Precision.HIGHEST
F32 = jnp.float32
BF16 = jnp.bfloat16

Z, Y, X, C = 8, 4, 4, 2
SEQ = ("z", "y")
HEAD = ("x", "core")
S = Z * Y
H = 4
T = 1024
PAIR = 2
W = H * HEAD_SIZE


def dot(a, b, ca=1, cb=0, precision=None):
    return lax.dot_general(
        a, b, (((ca,), (cb,)), ((), ())), preferred_element_type=F32, precision=precision
    )


def parts_of(x):
    hi = x.astype(BF16)
    rest = x - hi.astype(F32)
    mid = rest.astype(BF16)
    lo = (rest - mid.astype(F32)).astype(BF16)
    return hi, mid, lo


def wide_dot(x, y, ca=1, cb=0):
    hi, mid, lo = parts_of(x)
    return dot(hi, y, ca, cb) + (dot(mid, y, ca, cb) + dot(lo, y, ca, cb))


def close_dot(x, y, ca=1, cb=0):
    xh, yh = x.astype(BF16), y.astype(BF16)
    xl = (x - xh.astype(F32)).astype(BF16)
    yl = (y - yh.astype(F32)).astype(BF16)
    return dot(xh, yh, ca, cb) + (dot(xh, yl, ca, cb) + dot(xl, yh, ca, cb))


def call(kernel, name, grid, in_specs, out_specs, out_shape, cost, scratch=(), vmem=63.9):
    return pl.pallas_call(
        kernel,
        grid=grid,
        in_specs=in_specs,
        out_specs=out_specs,
        out_shape=out_shape,
        scratch_shapes=scratch,
        name=name,
        compiler_params=pltpu.CompilerParams(vmem_limit_bytes=int(vmem * 2**20)),
        cost_estimate=pl.CostEstimate(
            flops=int(cost * 1e9), bytes_accessed=1 << 20, transcendentals=0
        ),
    )


def spec(shape, index=None):
    if index is None:
        index = lambda h, n=len(shape): (0,) * n
    return pl.BlockSpec(shape, index)


def sds(shape, dtype=F32):
    return jax.ShapeDtypeStruct(shape, dtype)


COLS = spec((T, HEAD_SIZE), lambda h: (0, h))
ROWS = spec((M, T), lambda h: (h, 0))
LAND = spec((M, HEAD_SIZE), lambda h: (h, 0))
TILE = spec((1, 2 * M, HEAD_SIZE), lambda h: (h, 0, 0))
SQUARE = spec((1, M, M), lambda h: (h, 0, 0))


def means_kernel(q_ref, k_ref, o_ref):
    for i, ref in enumerate((q_ref, k_ref)):
        mean = jnp.sum(ref[...].astype(F32), axis=0, keepdims=True) / ref.shape[0]
        for h in range(H):
            o_ref[0, H * i + h : H * i + h + 1, :] = mean[:, h * HEAD_SIZE : (h + 1) * HEAD_SIZE]


def scores_kernel(q_ref, k_ref, v_ref, t_ref, f_ref, fb_ref, e_ref, sent_ref, st_ref, a_ref, mx_ref):
    qt, kt = t_ref[0, :M], t_ref[0, M:]
    s1 = dot(kt.astype(BF16), q_ref[...], 1, 1) * SCALE
    p = jnp.exp(s1 - jnp.max(s1, axis=0, keepdims=True))
    f = p / jnp.sum(p, axis=0, keepdims=True)
    f_ref[...] = f
    fb_ref[...] = f.astype(BF16)
    s2 = dot(qt.astype(BF16), k_ref[...], 1, 1) * SCALE
    top = jnp.max(s2, axis=1, keepdims=True)
    e = jnp.exp(s2 - top)
    e_ref[...] = e
    total = jnp.sum(e, axis=1, keepdims=True)
    sent_ref[:, :8] = wide_dot(e, v_ref[...]).reshape(8, 8, HEAD_SIZE)
    lane = lax.broadcasted_iota(jnp.int32, (M, HEAD_SIZE), 1)
    stats = jnp.where(lane < M, top, total)
    st_ref[...] = stats
    sent_ref[:, 8:] = stats.reshape(8, 8, HEAD_SIZE)
    sa = dot(qt, kt, 1, 1, HIGHEST) * SCALE
    pa = jnp.exp(sa - jnp.max(sa, axis=1, keepdims=True))
    a = pa / jnp.sum(pa, axis=1, keepdims=True)
    a_ref[0] = a
    col = jnp.max(jnp.sum(a, axis=0, keepdims=True), axis=1, keepdims=True)
    row = jnp.max(jnp.sum(a, axis=1, keepdims=True), axis=0, keepdims=True)
    sub = lax.broadcasted_iota(jnp.int32, (8, HEAD_SIZE), 0)
    both = jnp.where(sub < 4, col, row)

    @pl.when(pl.program_id(0) == 0)
    def _():
        mx_ref[...] = both

    @pl.when(pl.program_id(0) > 0)
    def _():
        mx_ref[...] = jnp.maximum(mx_ref[...], both)


def newton_kernel(a_ref, mx_ref, z_ref, x_ref, t2_ref, t3_ref):
    eye = (
        lax.broadcasted_iota(jnp.int32, (M, M), 0) == lax.broadcasted_iota(jnp.int32, (M, M), 1)
    ).astype(F32)
    mx = mx_ref[...]
    denom = mx[0:1, 0:1] * mx[4:5, 0:1]
    zs = []
    for h in range(H):
        z = a_ref[h].T / denom
        z_ref[0, h] = z
        zs.append(z)
    for n in range(NEWTON):
        xs = [dot(a_ref[h], zs[h], precision=HIGHEST) for h in range(H)]
        t2 = [15.0 * eye - dot(x, 7.0 * eye - x, precision=HIGHEST) for x in xs]
        t3 = [13.0 * eye - dot(x, t, precision=HIGHEST) for x, t in zip(xs, t2)]
        zs = [0.25 * dot(z, t, precision=HIGHEST) for z, t in zip(zs, t3)]
        for h in range(H):
            x_ref[n, h] = xs[h]
            t2_ref[n, h] = t2[h]
            t3_ref[n, h] = t3[h]
            z_ref[n + 1, h] = zs[h]


def merge_kernel(r_ref, o_ref):
    v, st = r_ref[:, :8, :], r_ref[:, 8:, :]
    top, total = st[:, :, 0:1], st[:, :, M : M + 1]
    mx = jnp.max(top, axis=0, keepdims=True)
    scale = jnp.exp(top - mx)
    whole = jnp.sum(scale * total, axis=0)
    lane = lax.broadcasted_iota(jnp.int32, (8, HEAD_SIZE), 1)
    o_ref[:, :8] = jnp.broadcast_to((jnp.sum(scale * v, axis=0) / whole)[None], (S, 8, HEAD_SIZE))
    o_ref[:, 8:] = jnp.broadcast_to(jnp.where(lane < M, mx[0], whole)[None], (S, 8, HEAD_SIZE))


def outer_kernel(j_ref, fb_ref, *refs):
    ogs, out = refs[:-1], refs[-1]
    for b, og in enumerate(ogs):
        res = dot(fb_ref[...], og[...])
        for y in range(2):
            out[j_ref[b], y] = res[:, y * 128 : (y + 1) * 128]


def outer_far_kernel(j_ref, fb_ref, far_ref, far2_ref, g_ref, out_ref):
    for i, og in enumerate((far_ref, far2_ref)):

        @pl.when(pl.program_id(0) == i)
        def _(og=og):
            res = dot(fb_ref[...], og[...])
            for y in range(Y):
                out_ref[0, y] = res[:, y * 128 : (y + 1) * 128]


def cotangent_kernel(j_ref, w_ref, fb_ref, *refs):
    ogs, do_ref, sent_ref = refs[:8], refs[8], refs[9]
    i = pl.program_id(0)
    acc = None
    for b in range(8):
        at = pl.multiple_of(j_ref[b] * W, W)
        part = dot(ogs[b][...], w_ref[pl.ds(at, W), :])
        acc = part if acc is None else acc + part
    do = acc.astype(BF16)
    do_ref[...] = do

    @pl.when(i == 0)
    def _():
        sent_ref[...] = jnp.zeros((S, 8, HEAD_SIZE), F32)

    for h in range(H):
        part = dot(fb_ref[h * M : (h + 1) * M, :], do[:, h * HEAD_SIZE : (h + 1) * HEAD_SIZE])
        sent_ref[8 * h : 8 * h + 8] += part.reshape(8, 8, HEAD_SIZE)


def spread_kernel(r_ref, o_ref):
    o_ref[...] = jnp.broadcast_to(jnp.sum(r_ref[...], axis=0)[None], (S, 8, HEAD_SIZE))


def put_rows(ref, x, h):
    for s in range(2):
        ref[:, pl.ds(2 * h + s, 1), :] = x[s * S : (s + 1) * S][:, None, :]


def query_panel_kernel(q_ref, do_ref, t_ref, f_ref, got_ref, z_ref, dq_ref, dt_ref, wf_ref):
    ktb = t_ref[0, M:].astype(BF16)
    bv = got_ref[:, :8].reshape(M, HEAD_SIZE)
    wf = dot(z_ref[0, 0], bv, precision=HIGHEST)
    wf_ref[...] = wf
    f = f_ref[...]
    df = wide_dot(wf, do_ref[...], 1, 1)
    dsf = (f * (df - jnp.sum(df * f, axis=0, keepdims=True))).astype(BF16)
    put_rows(dt_ref, dot(dsf, q_ref[...]) * SCALE, pl.program_id(0))
    dq_ref[...] = dot(dsf, ktb, 0, 0) * SCALE


def key_panel_kernel(
    k_ref, v_ref, e_ref, st_ref, got_ref, dw_ref, z_ref, dt_ref, dsb_ref, bb_ref, dbv_ref, sent_ref
):
    for i in range(PAIR):
        at, cols = slice(i * M, (i + 1) * M), slice(i * HEAD_SIZE, (i + 1) * HEAD_SIZE)
        dw = dw_ref[8 * i : 8 * i + 8].reshape(M, HEAD_SIZE)
        bv = got_ref[8 * i : 8 * i + 8, :8].reshape(M, HEAD_SIZE)
        whole = got_ref[8 * i : 8 * i + 8, 8:].reshape(M, HEAD_SIZE)
        dbv = dot(z_ref[0, i], dw, 0, 0, HIGHEST).astype(BF16)
        dbv_ref[at] = dbv
        db = dot(dbv, v_ref[:, cols], 1, 1)
        beta = jnp.sum(dbv.astype(F32) * bv, axis=1, keepdims=True)
        rescale = jnp.exp(st_ref[at, 0:1] - whole[:, 0:1]) / whole[:, M : M + 1]
        bf = e_ref[at] * rescale
        dsb = (bf * (db - beta)).astype(BF16)
        dsb_ref[at] = dsb
        bb_ref[at] = bf.astype(BF16)
        put_rows(sent_ref, dot(dsb, k_ref[:, cols]) * SCALE, PAIR * pl.program_id(0) + i)

    @pl.when(pl.program_id(0) == 0)
    def _():
        sent_ref[:, 8:] = dt_ref[...]


def adjoint_kernel(
    own_ref, bb_ref, dbv_ref, dw_ref, got_ref, mx_ref, a_ref, z_ref, x_ref, t2_ref, t3_ref, t_ref,
    o_ref, dv_ref,
):
    eye = (
        lax.broadcasted_iota(jnp.int32, (M, M), 0) == lax.broadcasted_iota(jnp.int32, (M, M), 1)
    ).astype(F32)
    hi = close_dot
    heads = range(H)
    dz = []
    for h in heads:
        dw = dw_ref[8 * h : 8 * h + 8].reshape(M, HEAD_SIZE)
        bv = got_ref[8 * h : 8 * h + 8, :8].reshape(M, HEAD_SIZE)
        dz.append(hi(dw, bv, 1, 1))
    da = [jnp.zeros((M, M), F32) for h in heads]
    for n in reversed(range(NEWTON)):
        if n < H:
            rows, cols = slice(n * M, (n + 1) * M), slice(n * HEAD_SIZE, (n + 1) * HEAD_SIZE)
            dv_ref[:, cols] = dot(bb_ref[rows, :], dbv_ref[rows, :], 0, 0).astype(BF16)
        x = [x_ref[n, h] for h in heads]
        g = [0.25 * d for d in dz]
        dp2 = [-hi(z_ref[n, h], g[h], 0, 0) for h in heads]
        dz = [hi(g[h], t3_ref[n, h], 1, 1) for h in heads]
        dp1 = [-hi(x[h], dp2[h], 0, 0) for h in heads]
        dx = [hi(dp2[h], t2_ref[n, h], 1, 1) for h in heads]
        dt1 = [hi(x[h], dp1[h], 0, 0) for h in heads]
        dx = [dx[h] + hi(dp1[h], 7.0 * eye - x[h], 1, 1) - dt1[h] for h in heads]
        dz = [dz[h] + hi(a_ref[h], dx[h], 0, 0) for h in heads]
        da = [da[h] + hi(dx[h], z_ref[n, h], 1, 1) for h in heads]
    mx = mx_ref[...]
    denom = mx[0:1, 0:1] * mx[4:5, 0:1]
    row = lax.broadcasted_iota(jnp.int32, (M, HEAD_SIZE), 0)
    for h in heads:
        d = da[h] + dz[h].T / denom
        a = a_ref[h]
        dsa = a * (d - jnp.sum(d * a, axis=1, keepdims=True))
        dqt = hi(dsa, t_ref[h, M:]) * SCALE
        dkt = hi(dsa, t_ref[h, :M], 0, 0) * SCALE
        for i, x in enumerate((dqt, dkt)):
            for s in range(2):
                mine = jnp.where(row == own_ref[0] + s * S, x, 0.0)
                r = 8 * i + 2 * h + s
                o_ref[r : r + 1, :] = jnp.sum(mine, axis=0, keepdims=True)


def final_kernel(dq_ref, dsb_ref, t_ref, got_ref, add_ref, q_out, k_out, tot_ref):
    i = pl.program_id(0)

    @pl.when(i == 0)
    def _():
        tot_ref[...] = (jnp.sum(got_ref[...], axis=0) + add_ref[...]) / (T // 2)

    s = i // 2
    for h in range(H):
        cols = slice(h * HEAD_SIZE, (h + 1) * HEAD_SIZE)
        add = tot_ref[pl.ds(2 * h + s, 1), :]
        q_out[:, cols] = (dq_ref[:, cols] + add).astype(BF16)
        dk = dot(dsb_ref[h * M : (h + 1) * M, :], t_ref[h, :M].astype(BF16), 0, 0) * SCALE
        add = tot_ref[pl.ds(8 + 2 * h + s, 1), :]
        k_out[:, cols] = (dk + add).astype(BF16)


def weight_kernel(*refs):
    here_ref, g_ref, gs, wf_ref, o_ref = refs[0], refs[1], refs[2 : Y + 1], refs[Y + 1], refs[Y + 2]
    for h in range(H):
        rows = slice(h * M, (h + 1) * M)
        b, c, d = (ref[rows, :] for ref in gs)
        o_ref[:, h * HEAD_SIZE : (h + 1) * HEAD_SIZE] = close_dot(
            (g_ref[here_ref[0], rows, :] + b) + (c + d), wf_ref[rows, :], 0, 0
        )


def to_all(x, axes, n):
    return lax.all_to_all(jnp.broadcast_to(x[None], (n,) + x.shape), axes, 0, 0, tiled=True)


def gather_rows(x, means):
    here = lax.axis_index("y")
    x, means = lax.optimization_barrier((x, means))
    blocks = [
        lax.ppermute(x, "y", [(i, (i + step) % Y) for i in range(Y)]) for step in range(1, Y)
    ]
    out = jnp.zeros((Y,) + x.shape, x.dtype)
    out = lax.dynamic_update_index_in_dim(out, x, here, 0)
    for step, block in enumerate(blocks, 1):
        out = lax.dynamic_update_index_in_dim(out, block, (here - step) % Y, 0)
    return out.reshape(Y * x.shape[0], x.shape[1]), means


RIGHT = [(i, (i + 1) % X) for i in range(X)]
LEFT = [(i, (i - 1) % X) for i in range(X)]
OTHER = [(0, 1), (1, 0)]
FAR = [(i * C + c, (i + 1 - 2 * c) % X * C + c) for i in range(X) for c in range(C)]


def places():
    px, pc = lax.axis_index("x"), lax.axis_index("core")
    out = []
    for step in (0, -1, 1, 2):
        for core in (pc, 1 - pc):
            out.append(((px + step) % X) * C + core)
    return jnp.stack(out).astype(jnp.int32)


def local(queries, keys, values, out_weight, out_grad):
    full = lambda *shape: spec(shape)
    smem = pl.BlockSpec(memory_space=pltpu.SMEM)
    half = spec((T // 2, W), lambda s: (s, 0))
    slab = spec((T // 4, W), lambda i: (i, 0))
    means = call(
        means_kernel, "means", (2,), [half, half], spec((1, 8, HEAD_SIZE), lambda s: (s, 0, 0)),
        sds((2, 8, HEAD_SIZE)), 2,
    )(queries, keys)
    weight, means = gather_rows(out_weight, means)
    weight = lax.all_gather(weight, "z", axis=0, tiled=True)
    out_grad, means = lax.optimization_barrier((out_grad, means))
    tiles = to_all(means.reshape(16, HEAD_SIZE), SEQ, S)
    right = lax.ppermute(out_grad, "x", RIGHT)
    left = lax.ppermute(out_grad, "x", LEFT)
    right, left, out_grad, tiles = lax.optimization_barrier((right, left, out_grad, tiles))
    beside = lax.ppermute(out_grad, "core", OTHER)
    far = jnp.where(lax.axis_index("core") == 0, right, left)
    right, left, far = lax.optimization_barrier((right, left, far))
    far = lax.ppermute(far, HEAD, FAR)
    right2, left2 = lax.ppermute(right, "core", OTHER), lax.ppermute(left, "core", OTHER)
    tiles = tiles.reshape(S, 2, 2, H, HEAD_SIZE).transpose(3, 2, 1, 0, 4)
    tiles = tiles.reshape(H, 2 * M, HEAD_SIZE)

    f, fb, e, sent, stats, a, tops = call(
        scores_kernel, "scores", (H,), [COLS, COLS, COLS, TILE],
        [ROWS, ROWS, ROWS, spec((8, 16, HEAD_SIZE), lambda h: (h, 0, 0)), LAND, SQUARE, full(8, HEAD_SIZE)],
        [sds((H * M, T)), sds((H * M, T), BF16), sds((H * M, T)), sds((S, 16, HEAD_SIZE)),
         sds((H * M, HEAD_SIZE)), sds((H, M, M)), sds((8, HEAD_SIZE))], 60,
    )(queries, keys, values, tiles)

    blocks = [out_grad, beside, right, right2, left, left2]
    where = places()

    got = lax.all_to_all(sent, SEQ, 0, 0, tiled=True)
    wide = spec((T, 256), lambda i: (0, i))
    g = call(
        outer_kernel, "outer", (2,), [smem, full(H * M, T)] + [wide] * 6,
        spec((Z, 2, H * M, 128), lambda i: (0, i, 0, 0)), sds((Z, Y, H * M, 128)), 20,
    )(where, fb, *blocks)
    g, far, tops = lax.optimization_barrier((g, far, tops))
    far2 = lax.ppermute(far, "core", OTHER)
    tops = jnp.maximum(tops, lax.ppermute(tops, "core", OTHER))
    ahead = [lax.ppermute(tops, "x", [(i, (i + n) % X) for i in range(X)]) for n in range(1, X)]
    tops = jnp.maximum(jnp.maximum(tops, ahead[0]), jnp.maximum(ahead[1], ahead[2]))
    g = pl.pallas_call(
        outer_far_kernel,
        grid_spec=pltpu.PrefetchScalarGridSpec(
            num_scalar_prefetch=1,
            grid=(2,),
            in_specs=[
                pl.BlockSpec((H * M, T), lambda i, j: (0, 0)),
                pl.BlockSpec((T, W), lambda i, j: (0, 0)),
                pl.BlockSpec((T, W), lambda i, j: (0, 0)),
                pl.BlockSpec(memory_space=pl.ANY),
            ],
            out_specs=pl.BlockSpec((1, Y, H * M, 128), lambda i, j: (j[6 + i], 0, 0, 0)),
        ),
        out_shape=sds((Z, Y, H * M, 128)),
        input_output_aliases={4: 0},
        name="outer_far",
        compiler_params=pltpu.CompilerParams(vmem_limit_bytes=int(63.9 * 2**20)),
        cost_estimate=pl.CostEstimate(flops=10**9, bytes_accessed=1 << 20, transcendentals=0),
    )(where, fb, far, far2, g)
    g, got, tops = lax.optimization_barrier((g, got, tops))
    merged = call(
        merge_kernel, "merge", (1,), [full(S, 16, HEAD_SIZE)], full(S, 16, HEAD_SIZE),
        sds((S, 16, HEAD_SIZE)), 1,
    )(got)
    land = lax.all_to_all(merged, SEQ, 0, 0, tiled=True)
    g = lax.psum_scatter(g, "z", scatter_dimension=0, tiled=True).reshape(Y, H * M, 128)

    tokens = 512
    panel = spec((H * M, tokens), lambda i: (0, i))
    block = spec((tokens, W), lambda i: (i, 0))
    do, sent = call(
        cotangent_kernel, "cotangent", (T // tokens,),
        [smem, full(Z * Y * 128, W), panel] + [block] * 8,
        [block, full(S, 8, HEAD_SIZE)], [sds((T, W), BF16), sds((S, 8, HEAD_SIZE))], 10,
    )(where, weight, fb, *blocks, far, far2)

    land, sent, tops = lax.optimization_barrier((land, sent, tops))
    inverse, xs, t2, t3 = call(
        newton_kernel, "newton", (1,), [full(H, M, M), full(8, HEAD_SIZE)],
        [full(NEWTON + 1, H, M, M)] + [full(NEWTON, H, M, M)] * 3,
        [sds((NEWTON + 1, H, M, M))] + [sds((NEWTON, H, M, M))] * 3, 6,
    )(a, tops)

    got = lax.all_to_all(sent, SEQ, 0, 0, tiled=True)
    sent = call(
        spread_kernel, "spread", (1,), [full(S, 8, HEAD_SIZE)], full(S, 8, HEAD_SIZE), sds((S, 8, HEAD_SIZE)), 1
    )(got)
    dw = lax.all_to_all(sent, SEQ, 0, 0, tiled=True)

    parts = spec((8, 16, HEAD_SIZE), lambda h: (h, 0, 0))
    last = spec((1, 1, M, M), lambda h: (NEWTON, h, 0, 0))
    dq, dktf, wf = call(
        query_panel_kernel, "query_panel", (H,), [COLS, COLS, TILE, ROWS, parts, last],
        [COLS, full(S, 8, HEAD_SIZE), LAND], [sds((T, W)), sds((S, 8, HEAD_SIZE)), sds((H * M, HEAD_SIZE))], 5,
    )(queries, do, tiles, f, land, inverse)
    wide = spec((T, PAIR * HEAD_SIZE), lambda h: (0, h))
    rows = spec((PAIR * M, T), lambda h: (h, 0))
    marks = spec((PAIR * M, HEAD_SIZE), lambda h: (h, 0))
    dsb, bb, dbv, sent = call(
        key_panel_kernel, "key_panel", (H // PAIR,),
        [wide, wide, rows, marks, spec((8 * PAIR, 16, HEAD_SIZE), lambda h: (h, 0, 0)),
         spec((8 * PAIR, 8, HEAD_SIZE), lambda h: (h, 0, 0)),
         spec((1, PAIR, M, M), lambda h: (NEWTON, h, 0, 0)), full(S, 8, HEAD_SIZE)],
        [rows, rows, marks, full(S, 16, HEAD_SIZE)],
        [sds((H * M, T), BF16), sds((H * M, T), BF16), sds((H * M, HEAD_SIZE), BF16),
         sds((S, 16, HEAD_SIZE))], 4,
    )(keys, values, e, stats, land, dw, inverse, dktf)
    g, dsb = lax.optimization_barrier((g, dsb))
    here = lax.axis_index("y")
    gs = [lax.dynamic_index_in_dim(g, (here + n) % Y, keepdims=False) for n in range(1, Y)]
    gs = [
        lax.ppermute(x, "y", [(i, (i + n) % Y) for i in range(Y)]) for n, x in enumerate(gs, 1)
    ]
    summed = lax.all_to_all(sent, SEQ, 0, 0, tiled=True)
    own = lax.axis_index(SEQ).astype(jnp.int32).reshape(1)
    da, dv = call(
        adjoint_kernel, "adjoint", (1,),
        [smem, full(H * M, T), full(H * M, HEAD_SIZE), full(S, 8, HEAD_SIZE), full(S, 16, HEAD_SIZE), full(8, HEAD_SIZE), full(H, M, M),
         full(NEWTON + 1, H, M, M)] + [full(NEWTON, H, M, M)] * 3 + [full(H, 2 * M, HEAD_SIZE)],
        [full(16, HEAD_SIZE), full(T, W)], [sds((16, HEAD_SIZE)), sds((T, W), BF16)], 11,
    )(own, bb, dbv, dw, land, tops, a, inverse, xs, t2, t3, tiles)
    query_grad, key_grad = call(
        final_kernel, "final", (4,), [slab, spec((H * M, T // 4), lambda i: (0, i)),
         full(H, 2 * M, HEAD_SIZE), full(S, 16, HEAD_SIZE), full(16, HEAD_SIZE)],
        [slab, slab], [sds((T, W), BF16)] * 2, 2, [pltpu.VMEM((16, HEAD_SIZE), F32)],
    )(dq, dsb, tiles, summed, da)
    weight_grad = call(
        weight_kernel, "weight", (1,),
        [smem, full(Y, H * M, 128)] + [full(H * M, 128)] * (Y - 1) + [full(H * M, HEAD_SIZE)],
        full(128, W), sds((128, W)), 2,
    )(here.astype(jnp.int32).reshape(1), g, *gs, wf)
    return query_grad, key_grad, dv, weight_grad


def solution(mesh):
    grid = Mesh(mesh.devices.reshape(Z, Y, X, C), SEQ + HEAD)
    place = P(SEQ, HEAD)
    return jax.shard_map(
        local, mesh=grid, in_specs=(place,) * 5, out_specs=(place,) * 4, check_vma=False
    )
```
